32 devices in a mesh: tables: 8 (over z, x), heads: 4 (over y, core).
Axes of the slice: x: 2, y: 2, z: 4, core: 2. Of those that a mesh axis runs over, the one named last changes fastest.
Arguments:
- ctx_feat: bfloat16 [8, 2048, 100], P('tables', 'heads'), may hold values from -6 to 6
- qry_feat: bfloat16 [8, 704, 100], P('tables', 'heads'), may hold values from -6 to 6
- counts: int32 [8], P('tables'), may hold values from 64 to 2048, as said below
- ctx_bins: int32 [8, 2048], P('tables', 'heads'), may hold values from 0 to 63
- qry_bins: int32 [8, 704], P('tables', 'heads'), may hold values from 0 to 63
- query_mask: int32 [8, 704], P('tables', 'heads'), may hold values from 0 to 1
- w_embed: float32 [100, 768], replicated, may hold values from -0.625 to 0.625
- w_bins: float32 [64, 768], replicated, may hold values from -6 to 6
- norm_gains: float32 [3, 768], replicated, may hold values from 0.5 to 1.5
- w_qkv: float32 [3, 768, 768], P(None, None, 'heads'), may hold values from -0.21875 to 0.21875
- w_out: float32 [768, 768], P('heads')
- w_up: float32 [768, 3072], P(None, 'heads')
- w_down: float32 [3072, 768], P('heads')
- w_head: float32 [768, 64], replicated, may hold values from -0.21875 to 0.21875
- m_embed: float32 [100, 768], replicated, may hold values from -4.7683716e-06 to 4.7683716e-06
- m_bins: float32 [64, 768], replicated, may hold values from -1.9073486e-06 to 1.9073486e-06
- m_gains: float32 [3, 768], replicated, may hold values from -2.2888184e-05 to 2.2888184e-05
- m_qkv: float32 [3, 768, 768], P(None, None, 'heads'), may hold values from -4.7683716e-06 to 4.7683716e-06
- m_out: float32 [768, 768], P('heads'), may hold values from -2.3841858e-07 to 2.3841858e-07
- m_up: float32 [768, 3072], P(None, 'heads'), may hold values from -9.536743e-07 to 9.536743e-07
- m_down: float32 [3072, 768], P('heads'), may hold values from -4.7683716e-06 to 4.7683716e-06
- m_head: float32 [768, 64], replicated, may hold values from -4.7683716e-06 to 4.7683716e-06
- v_embed: float32 [100, 768], replicated, may hold values from 2.756607e-12 to 1.1026428e-11
- v_bins: float32 [64, 768], replicated, may hold values from 4.4105713e-13 to 1.7642285e-12
- v_gains: float32 [3, 768], replicated, may hold values from 6.891518e-11 to 2.7566072e-10
- v_qkv: float32 [3, 768, 768], P(None, None, 'heads'), may hold values from 2.756607e-12 to 1.1026428e-11
- v_out: float32 [768, 768], P('heads'), may hold values from 6.8915177e-15 to 2.756607e-14
- v_up: float32 [768, 3072], P(None, 'heads'), may hold values from 1.1026428e-13 to 4.4105713e-13
- v_down: float32 [3072, 768], P('heads'), may hold values from 2.756607e-12 to 1.1026428e-11
- v_head: float32 [768, 64], replicated, may hold values from 2.756607e-12 to 1.1026428e-11
Outputs:
- embed_new: float32 [100, 768], replicated
- bins_new: float32 [64, 768], replicated
- gains_new: float32 [3, 768], replicated
- qkv_new: float32 [3, 768, 768], P(None, None, 'heads')
- out_new: float32 [768, 768], P('heads')
- up_new: float32 [768, 3072], P(None, 'heads')
- down_new: float32 [3072, 768], P('heads')
- head_new: float32 [768, 64], replicated
- embed_first: float32 [100, 768], replicated
- bins_first: float32 [64, 768], replicated
- gains_first: float32 [3, 768], replicated
- qkv_first: float32 [3, 768, 768], P(None, None, 'heads')
- out_first: float32 [768, 768], P('heads')
- up_first: float32 [768, 3072], P(None, 'heads')
- down_first: float32 [3072, 768], P('heads')
- head_first: float32 [768, 64], replicated
- embed_second: float32 [100, 768], replicated
- bins_second: float32 [64, 768], replicated
- gains_second: float32 [3, 768], replicated
- qkv_second: float32 [3, 768, 768], P(None, None, 'heads')
- out_second: float32 [768, 768], P('heads')
- up_second: float32 [768, 3072], P(None, 'heads')
- down_second: float32 [3072, 768], P('heads')
- head_second: float32 [768, 64], replicated
- loss_sum: float32 [], replicated
- query_count: float32 [], replicated
- grad_norm: float32 [], replicated
The draws below stay inside these ranges and needn't reach their ends.
Inputs may be any that keep to these rules, and one draw needn't show every extreme that they name: `counts`: one table, drawn from the seed, has all 2048 slots live.
All inputs are finite; a program needn't handle non-finite values.
Results may differ from the reference program's by a relative error of at most 0.013.
The reference program's roundings to bfloat16 on the way count: a program that leaves them out, or rounds other values in their place, can miss the bound.
Values may be sent and summed in bfloat16 or wider, within the bound.
A program may use at most 256 MiB of HBM per device.

```python
import math
import jax
import jax.numpy as jnp
from jax import lax

D = 768
HEADS = 12
HD = 64
FF = 3072
FEAT = 100
BINS = 64
CTX = 2048
QRY = 704
STEP = 10
TABLES = 8
NPARAM = 7255296


def ramp_matrix(key, row_count, col_count, ramp_dim, upper_factor, spread):
    noise = jnp.clip(jax.random.normal(key, (row_count, col_count), jnp.float32), -6.0, 6.0)
    length = row_count if ramp_dim == 0 else col_count
    place = jnp.arange(length, dtype=jnp.float32) / max(length - 1, 1)
    factor = 1.0 + (upper_factor - 1.0) * place
    factor = factor[:, None] if ramp_dim == 0 else factor[None, :]
    return noise * factor * spread


def draw_w_out(key, part):
    return ramp_matrix(key, D, D, 0, 3.0, max(1, D // CTX) ** (-0.5))


def draw_w_up(key, part):
    return ramp_matrix(key, D, FF, 1, 2.0, D ** (-0.5))


def draw_w_down(key, part):
    return ramp_matrix(key, FF, D, 0, 2.0, FF ** (-0.5))


def draw_counts(key, part):
    low_end = max(1, min(64, CTX // 4))
    key_one, key_two = jax.random.split(jax.random.fold_in(key, 11))
    tables_at = jnp.arange(TABLES)
    highest = low_end + (CTX - low_end) * (tables_at + 1) // TABLES
    counted = jax.random.randint(key_one, (TABLES,), low_end, highest + 1)
    chosen = jax.random.randint(key_two, (), 0, TABLES)
    return jnp.where(tables_at == chosen, CTX, counted).astype(jnp.int32)


def draw_query_mask(key, part):
    table_no = jnp.arange(TABLES)[:, None]
    query_no = jnp.arange(QRY)[None, :]
    per_mille = 75 * (TABLES - 1 + 2 * table_no) * (QRY - 1 + 3 * query_no) // ((TABLES - 1) * (QRY - 1))
    rolled = jax.random.randint(jax.random.fold_in(key, 23), (TABLES, QRY), 0, 1000)
    return (rolled < per_mille).astype(jnp.int32)


def set_ends(values, rng, least, top_value):
    extent = values.shape
    spot = [jax.random.randint(jax.random.fold_in(rng, axis), (), 0, extent[axis]) for axis in range(len(extent))]
    values = values.at[tuple(spot)].set(least)
    longest = extent.index(max(extent))
    spot[longest] = (spot[longest] + 1) % extent[longest]
    return values.at[tuple(spot)].set(top_value)


def block_scale(rng, dims, cuts, smallest, top_value):
    factor_of = 1.0
    for position, shards_of in cuts:
        heights = jax.random.uniform(jax.random.fold_in(jax.random.fold_in(rng, 6), position), (shards_of,), jnp.float32, smallest / len(cuts), top_value / len(cuts))
        factor_of = factor_of * jnp.repeat(jnp.exp(heights), dims[position] // shards_of).reshape((-1,) + (1,) * (len(dims) - 1 - position))
    return factor_of


def scatter_about(key, dims, deviation, reach, pieces=(), kind=jnp.bfloat16):
    loudness = block_scale(key, dims, pieces, -0.22, 0.18) if pieces else 1.0
    result = jax.random.normal(key, dims, jnp.float32) * deviation * loudness
    return jnp.minimum(jnp.maximum(result, -reach), reach).astype(kind)


def setup_inputs(seed: int = 0) -> dict:
    seeds = jax.random.split(jax.random.key(seed), 31)
    return {
        "ctx_feat": scatter_about(seeds[0], (TABLES, CTX, FEAT), 1.0, 6.0, ((0, 8), (1, 4))),
        "qry_feat": scatter_about(seeds[1], (TABLES, QRY, FEAT), 1.0, 6.0, ((0, 8), (1, 4))),
        "counts": draw_counts(jax.random.fold_in(seeds[30], 71), 0),
        "ctx_bins": set_ends(jax.random.randint(seeds[3], (TABLES, CTX), 0, BINS), jax.random.fold_in(seeds[3], 1), 0, BINS - 1).astype(jnp.int32),
        "qry_bins": set_ends(jax.random.randint(seeds[4], (TABLES, QRY), 0, BINS), jax.random.fold_in(seeds[4], 1), 0, BINS - 1).astype(jnp.int32),
        "query_mask": draw_query_mask(jax.random.fold_in(seeds[30], 71), 0),
        "w_embed": scatter_about(seeds[6], (FEAT, D), FEAT ** -0.5, 0.625, (), jnp.float32),
        "w_bins": scatter_about(seeds[7], (BINS, D), 1.0, 6.0, (), jnp.float32),
        "norm_gains": jnp.clip(1.0 + 0.1 * jax.random.normal(seeds[8], (3, D), jnp.float32), 0.5, 1.5),
        "w_qkv": scatter_about(seeds[9], (3, D, D), D ** -0.5, 0.21875, ((2, 4),), jnp.float32),
        "w_out": draw_w_out(jax.random.fold_in(seeds[30], 71), 0),
        "w_up": draw_w_up(jax.random.fold_in(seeds[30], 71), 0),
        "w_down": draw_w_down(jax.random.fold_in(seeds[30], 71), 0),
        "w_head": scatter_about(seeds[13], (D, BINS), D ** -0.5, 0.21875, (), jnp.float32),
        "m_embed": scatter_about(seeds[14], (FEAT, D), (0.0022 * NPARAM ** -0.5), 4.76837158203125e-06, (), jnp.float32),
        "m_bins": scatter_about(seeds[15], (BINS, D), (0.00088 * NPARAM ** -0.5), 1.9073486328125e-06, (), jnp.float32),
        "m_gains": scatter_about(seeds[16], (3, D), (0.011 * NPARAM ** -0.5), 2.288818359375e-05, (), jnp.float32),
        "m_qkv": scatter_about(seeds[17], (3, D, D), (0.0022 * NPARAM ** -0.5), 4.76837158203125e-06, ((2, 4),), jnp.float32),
        "m_out": scatter_about(seeds[18], (D, D), (0.00011 * NPARAM ** -0.5), 2.384185791015625e-07, ((0, 4),), jnp.float32),
        "m_up": scatter_about(seeds[19], (D, FF), (0.00044 * NPARAM ** -0.5), 9.5367431640625e-07, ((1, 4),), jnp.float32),
        "m_down": scatter_about(seeds[20], (FF, D), (0.0022 * NPARAM ** -0.5), 4.76837158203125e-06, ((0, 4),), jnp.float32),
        "m_head": scatter_about(seeds[21], (D, BINS), (0.0022 * NPARAM ** -0.5), 4.76837158203125e-06, (), jnp.float32),
        "v_embed": jnp.clip(jnp.exp(jax.random.uniform(seeds[22], (FEAT, D), jnp.float32, math.log(2.7566070086304517e-12), math.log(1.1026428034521807e-11))), 2.7566070086304517e-12, 1.1026428034521807e-11),
        "v_bins": jnp.clip(jnp.exp(jax.random.uniform(seeds[23], (BINS, D), jnp.float32, math.log(4.4105713005448965e-13), math.log(1.7642285202179586e-12))), 4.4105713005448965e-13, 1.7642285202179586e-12),
        "v_gains": jnp.clip(jnp.exp(jax.random.uniform(seeds[24], (3, D), jnp.float32, math.log(6.891517911888911e-11), math.log(2.7566071647555646e-10))), 6.891517911888911e-11, 2.7566071647555646e-10),
        "v_qkv": jnp.clip(jnp.exp(math.log(1.1026428034521807e-11) - 1.3862944 * jax.random.uniform(seeds[25], (3, D, D), jnp.float32) ** block_scale(seeds[25], (3, D, D), ((2, 4),), -0.2, 0.2)), 2.7566070086304517e-12, 1.1026428034521807e-11),
        "v_out": jnp.clip(jnp.exp(math.log(2.7566070628405603e-14) - 1.3862944 * jax.random.uniform(seeds[26], (D, D), jnp.float32) ** block_scale(seeds[26], (D, D), ((0, 4),), -0.2, 0.2)), 6.891517657101401e-15, 2.7566070628405603e-14),
        "v_up": jnp.clip(jnp.exp(math.log(4.4105713005448965e-13) - 1.3862944 * jax.random.uniform(seeds[27], (D, FF), jnp.float32) ** block_scale(seeds[27], (D, FF), ((1, 4),), -0.2, 0.2)), 1.1026428251362241e-13, 4.4105713005448965e-13),
        "v_down": jnp.clip(jnp.exp(math.log(1.1026428034521807e-11) - 1.3862944 * jax.random.uniform(seeds[28], (FF, D), jnp.float32) ** block_scale(seeds[28], (FF, D), ((0, 4),), -0.2, 0.2)), 2.7566070086304517e-12, 1.1026428034521807e-11),
        "v_head": jnp.clip(jnp.exp(jax.random.uniform(seeds[29], (D, BINS), jnp.float32, math.log(2.7566070086304517e-12), math.log(1.1026428034521807e-11))), 2.7566070086304517e-12, 1.1026428034521807e-11),
    }


@jax.custom_vjp
def low(v):
    return lax.optimization_barrier(v.astype(jnp.bfloat16)).astype(jnp.float32)

@jax.custom_vjp
def low_back(v):
    return v

def low_keep(v):
    return (low(v), None)

def low_pass(kept, grad):
    return (grad,)

def back_keep(v):
    return (v, None)

def back_low(kept, grad):
    return (low(grad),)
low.defvjp(low_keep, low_pass)
low_back.defvjp(back_keep, back_low)
NORM_EPS = 1e-05
ADAM_EPS = 1e-08
RATE = 0.05
RATE_WIDE = 1.0
BETA_ONE = 0.9
BETA_TWO = 0.95
DECAY = 0.1
CLIP_NORM = 0.02
MASKED = -1e+30
HIGH = lax.Precision.HIGHEST

def both_ways(value):
    return low(low_back(value))

def product(left, right):
    return jnp.dot(left, right, precision=HIGH)

def normalize(hidden, gain_row):
    center = hidden - lax.optimization_barrier(jnp.mean(hidden, axis=-1, keepdims=True))
    spread = lax.optimization_barrier(jnp.mean(center * center, axis=-1, keepdims=True))
    return center * lax.rsqrt(spread + NORM_EPS) * gain_row

def adam_update(weight, moment_one, moment_two, gradient, rate, decay_rate):
    moment_one = BETA_ONE * moment_one + (1.0 - BETA_ONE) * gradient
    moment_two = BETA_TWO * moment_two + (1.0 - BETA_TWO) * gradient * gradient
    first_hat = moment_one / (1.0 - BETA_ONE ** STEP)
    second_hat = moment_two / (1.0 - BETA_TWO ** STEP)
    weight = weight - rate * (first_hat / (jnp.sqrt(second_hat) + ADAM_EPS) + decay_rate * weight)
    return (weight, moment_one, moment_two)

def block_count(total_rows):
    blocks = max(1, total_rows // 1024)
    while total_rows % blocks:
        blocks -= 1
    return blocks

def table_loss(params, ctx_feat, qry_feat, context_len, ctx_bins, qry_bins, query_mask, divisor):
    w_embed, w_bins, norm_gains, w_qkv, w_out, w_up, w_down, w_head = params
    total_rows = CTX + QRY
    features = jnp.concatenate([ctx_feat, qry_feat], axis=0).astype(jnp.float32)
    bin_hits = (ctx_bins[:, None] == jnp.arange(BINS)[None, :]).astype(jnp.float32)
    bin_hits = jnp.concatenate([bin_hits, jnp.zeros((QRY, BINS), jnp.float32)], axis=0)
    stream_zero = low_back(product(features, low(w_embed)) + product(bin_hits, low(w_bins)))
    normed_one = low(normalize(stream_zero, norm_gains[0]))
    projected = jnp.einsum('rd,tdc->trc', normed_one, low(w_qkv), precision=HIGH)
    queries = both_ways(projected[0]).reshape(total_rows, HEADS, HD)
    key_heads = both_ways(projected[1][:CTX]).reshape(CTX, HEADS, HD)
    value_heads = both_ways(projected[2][:CTX]).reshape(CTX, HEADS, HD)
    live_keys = jnp.arange(CTX) < context_len
    blocks = block_count(total_rows)

    def attend(query_blk):
        raw_scores = jnp.einsum('bhe,khe->hbk', query_blk, key_heads, precision=HIGH) * HD ** (-0.5)
        masked = jnp.where(live_keys[None, None, :], low_back(raw_scores), MASKED)
        weights = low(jax.nn.softmax(masked, axis=-1))
        return jnp.einsum('hbk,khe->bhe', weights, value_heads, precision=HIGH)
    mixture = lax.map(jax.checkpoint(attend), queries.reshape(blocks, total_rows // blocks, HEADS, HD))
    mixture = both_ways(mixture.reshape(total_rows, D))
    stream_one = stream_zero + low_back(product(mixture, low(w_out)))
    normed_two = low(normalize(stream_one, norm_gains[1]))
    hidden_up = low_back(product(normed_two, low(w_up)))
    active = low(jax.nn.gelu(hidden_up))
    stream_two = stream_one + low_back(product(active, low(w_down)))
    normed_final = low(normalize(stream_two[CTX:], norm_gains[2]))
    logits = low_back(product(normed_final, low(w_head)))
    target_hits = (qry_bins[:, None] == jnp.arange(BINS)[None, :]).astype(jnp.float32)
    losses = query_mask.astype(jnp.float32) * (jax.nn.logsumexp(logits, axis=-1) - lax.optimization_barrier(jnp.sum(target_hits * logits, axis=-1)))
    loss_table = jnp.sum(losses)
    return (loss_table / divisor, loss_table)

def reference(ctx_feat, qry_feat, counts, ctx_bins, qry_bins, query_mask, w_embed, w_bins, norm_gains, w_qkv, w_out, w_up, w_down, w_head, m_embed, m_bins, m_gains, m_qkv, m_out, m_up, m_down, m_head, v_embed, v_bins, v_gains, v_qkv, v_out, v_up, v_down, v_head):
    params = (w_embed, w_bins, norm_gains, w_qkv, w_out, w_up, w_down, w_head)
    query_count = jnp.sum(query_mask.astype(jnp.float32))
    divisor = jnp.maximum(query_count, 1.0)

    def one_table(running, table_data):
        running_sum, loss_sum = running
        scaled_loss, pullback, loss_table = jax.vjp(lambda weights: table_loss(weights, *table_data, divisor), params, has_aux=True)
        gradients = pullback(jnp.ones_like(scaled_loss))[0]
        return ((jax.tree.map(jnp.add, running_sum, gradients), loss_sum + loss_table), None)
    initial = (jax.tree.map(jnp.zeros_like, params), jnp.zeros((), jnp.float32))
    (gradients, loss_sum), _ = lax.scan(one_table, initial, (ctx_feat, qry_feat, counts, ctx_bins, qry_bins, query_mask))
    grad_norm = jnp.sqrt(sum((jnp.sum(entry * entry) for entry in gradients)))
    factor = jnp.minimum(1.0, CLIP_NORM / (grad_norm + 1e-06))
    grad_embed, grad_bins, grad_gains, grad_qkv, grad_out, grad_up, grad_down, grad_head = gradients
    embed_new, embed_first, embed_second = adam_update(w_embed, m_embed, v_embed, grad_embed * factor, RATE, DECAY)
    bins_new, bins_first, bins_second = adam_update(w_bins, m_bins, v_bins, grad_bins * factor, RATE_WIDE, DECAY)
    gains_new, gains_first, gains_second = adam_update(norm_gains, m_gains, v_gains, grad_gains * factor, RATE_WIDE, 0.0)
    qkv_new, qkv_first, qkv_second = adam_update(w_qkv, m_qkv, v_qkv, grad_qkv * factor, RATE, DECAY)
    out_new, out_first, out_second = adam_update(w_out, m_out, v_out, grad_out * factor, RATE_WIDE, DECAY)
    up_new, up_first, up_second = adam_update(w_up, m_up, v_up, grad_up * factor, RATE, DECAY)
    down_new, down_first, down_second = adam_update(w_down, m_down, v_down, grad_down * factor, RATE, DECAY)
    head_new, head_first, head_second = adam_update(w_head, m_head, v_head, grad_head * factor, RATE, DECAY)
    return (embed_new, bins_new, gains_new, qkv_new, out_new, up_new, down_new, head_new, embed_first, bins_first, gains_first, qkv_first, out_first, up_first, down_first, head_first, embed_second, bins_second, gains_second, qkv_second, out_second, up_second, down_second, head_second, loss_sum, query_count, grad_norm)
```

```python
import jax
import jax.numpy as jnp
from jax import lax
from jax.sharding import PartitionSpec as P

HD = 64
BINS = 64
STEP = 10


NORM_EPS = 1e-05
ADAM_EPS = 1e-08
RATE = 0.05
RATE_WIDE = 1.0
BETA_ONE = 0.9
BETA_TWO = 0.95
DECAY = 0.1
CLIP_NORM = 0.02
MASKED = -1e30
FLOAT = jnp.float32
HALF = jnp.bfloat16


def product(left, right):
    return jnp.dot(left, right, preferred_element_type=FLOAT)


def normalize(hidden, gain_row):
    center = hidden - jnp.mean(hidden, axis=-1, keepdims=True)
    spread = jnp.mean(center * center, axis=-1, keepdims=True)
    return center * lax.rsqrt(spread + NORM_EPS) * gain_row


def norm_back(hidden, gain_row, upstream):
    _, pullback = jax.vjp(normalize, hidden, gain_row)
    return pullback(upstream)


def adam_update(weight, moment_one, moment_two, gradient, rate, decay_rate):
    moment_one = BETA_ONE * moment_one + (1.0 - BETA_ONE) * gradient
    moment_two = BETA_TWO * moment_two + (1.0 - BETA_TWO) * gradient * gradient
    first_hat = moment_one / (1.0 - BETA_ONE**STEP)
    second_hat = moment_two / (1.0 - BETA_TWO**STEP)
    weight = weight - rate * (first_hat / (jnp.sqrt(second_hat) + ADAM_EPS) + decay_rate * weight)
    return (weight, moment_one, moment_two)


def softmax_rows(query_heads, key_heads, live_keys):
    raw_scores = jnp.einsum(
        "bhe,khe->hbk", query_heads, key_heads, preferred_element_type=FLOAT
    ) * HD ** (-0.5)
    masked = jnp.where(live_keys[None, None, :], raw_scores, MASKED)
    top_score = jnp.max(masked, axis=-1, keepdims=True)
    unnormed = jnp.exp(masked - top_score)
    return unnormed / jnp.sum(unnormed, axis=-1, keepdims=True)


def gather(rows, axis=0):
    return lax.all_gather(rows, "heads", axis=axis, tiled=True)


def shards(
    ctx_feat,
    qry_feat,
    counts,
    ctx_bins,
    qry_bins,
    query_mask,
    w_embed,
    w_bins,
    norm_gains,
    w_qkv,
    w_out,
    w_up,
    w_down,
    w_head,
    m_embed,
    m_bins,
    m_gains,
    m_qkv,
    m_out,
    m_up,
    m_down,
    m_head,
    v_embed,
    v_bins,
    v_gains,
    v_qkv,
    v_out,
    v_up,
    v_down,
    v_head,
):
    model_width = w_embed.shape[1]
    heads_here = w_qkv.shape[2] // HD
    me = lax.axis_index("heads")
    qry_local = qry_feat.shape[1]
    ctx_rows = gather(ctx_feat[0])
    qry_rows = gather(qry_feat[0])
    all_bins = gather(jnp.concatenate([ctx_bins[0], qry_bins[0], query_mask[0]]).reshape(1, -1))
    ctx_local = ctx_feat.shape[1]
    all_ctx_bins = all_bins[:, :ctx_local].reshape(-1)
    all_qry_bins = all_bins[:, ctx_local : ctx_local + qry_local].reshape(-1)
    mask_rows = all_bins[:, ctx_local + qry_local :].reshape(-1).astype(FLOAT)
    total_ctx = ctx_rows.shape[0]
    total_qry = qry_rows.shape[0]
    bin_hits = (all_ctx_bins[:, None] == jnp.arange(BINS)[None, :]).astype(HALF)
    query_count = lax.psum(jnp.sum(mask_rows), "tables")
    divisor = jnp.maximum(query_count, 1.0)
    embed_half = w_embed.astype(HALF)
    bins_half = w_bins.astype(HALF)
    qkv_half = w_qkv.astype(HALF)
    out_half = w_out.astype(HALF)
    up_half = w_up.astype(HALF)
    down_half = w_down.astype(HALF)
    head_half = w_head.astype(HALF)
    out_full = gather(out_half)
    zero_ctx = product(ctx_rows, embed_half) + product(bin_hits, bins_half)
    zero_qry = product(qry_rows, embed_half)
    normed_ctx = normalize(zero_ctx, norm_gains[0]).astype(HALF)
    normed_qry = normalize(zero_qry, norm_gains[0]).astype(HALF)
    queries = product(normed_qry, qkv_half[0]).astype(HALF).reshape(total_qry, heads_here, HD)
    key_heads = product(normed_ctx, qkv_half[1]).astype(HALF).reshape(total_ctx, heads_here, HD)
    value_heads = product(normed_ctx, qkv_half[2]).astype(HALF).reshape(total_ctx, heads_here, HD)
    live_keys = jnp.arange(total_ctx) < counts[0]
    weights = softmax_rows(queries, key_heads, live_keys)
    mixture = jnp.einsum(
        "hbk,khe->bhe", weights.astype(HALF), value_heads, preferred_element_type=FLOAT
    )
    mixture = mixture.reshape(total_qry, -1).astype(HALF)
    stream_one = zero_qry + product(gather(mixture, 1), out_full)
    normed_two = normalize(stream_one, norm_gains[1]).astype(HALF)
    hidden_up = product(normed_two, up_half)
    active = jax.nn.gelu(hidden_up).astype(HALF)
    mlp = lax.psum(product(active, down_half).astype(HALF), "heads")
    stream_two = stream_one + mlp.astype(FLOAT)
    normed_final = normalize(stream_two, norm_gains[2]).astype(HALF)
    logits = product(normed_final, head_half)
    log_bins = jax.nn.logsumexp(logits, axis=-1)
    target_hits = (all_qry_bins[:, None] == jnp.arange(BINS)[None, :]).astype(FLOAT)
    loss_local = jnp.sum(mask_rows * (log_bins - jnp.sum(target_hits * logits, axis=-1)))
    back_logits = (
        mask_rows[:, None] * (jnp.exp(logits - log_bins[:, None]) - target_hits) / divisor
    ).astype(HALF)
    grad_head = jnp.einsum("rd,rb->db", normed_final, back_logits, preferred_element_type=FLOAT)
    back_final = jnp.einsum("rb,db->rd", back_logits, head_half, preferred_element_type=FLOAT)
    back_two, grad_final = norm_back(stream_two, norm_gains[2], back_final)
    back_mlp = back_two.astype(HALF)
    grad_down = jnp.einsum("rf,rd->fd", active, back_mlp, preferred_element_type=FLOAT)
    back_active = jnp.einsum("rd,fd->rf", back_mlp, down_half, preferred_element_type=FLOAT)
    _, gelu_pull = jax.vjp(jax.nn.gelu, hidden_up)
    back_up = gelu_pull(back_active)[0].astype(HALF)
    grad_up = jnp.einsum("rd,rf->df", normed_two, back_up, preferred_element_type=FLOAT)
    back_norm_two = jnp.einsum("rf,df->rd", back_up, up_half, preferred_element_type=FLOAT)
    back_norm_two = lax.psum(back_norm_two.astype(HALF), "heads").astype(FLOAT)
    back_mid, grad_mid = norm_back(stream_one, norm_gains[1], back_norm_two)
    back_one = back_two + back_mid
    back_attn = back_one.astype(HALF)
    grad_out = jnp.einsum("rc,rd->cd", mixture, back_attn, preferred_element_type=FLOAT)
    back_mix = jnp.einsum("rd,cd->rc", back_attn, out_half, preferred_element_type=FLOAT)
    back_mix = back_mix.astype(HALF).reshape(total_qry, heads_here, HD)
    back_value = jnp.einsum(
        "hbk,bhe->khe", weights.astype(HALF), back_mix, preferred_element_type=FLOAT
    )
    back_weights = jnp.einsum("bhe,khe->hbk", back_mix, value_heads, preferred_element_type=FLOAT)
    back_scores = weights * (
        back_weights - jnp.sum(weights * back_weights, axis=-1, keepdims=True)
    )
    back_scores = back_scores.astype(HALF) * HD ** (-0.5)
    back_query = jnp.einsum("hbk,khe->bhe", back_scores, key_heads, preferred_element_type=FLOAT)
    back_key = jnp.einsum("hbk,bhe->khe", back_scores, queries, preferred_element_type=FLOAT)
    back_query = back_query.reshape(total_qry, -1).astype(HALF)
    back_key = back_key.reshape(total_ctx, -1).astype(HALF)
    back_value = back_value.reshape(total_ctx, -1).astype(HALF)
    grad_qkv = jnp.stack(
        [
            jnp.einsum("rd,rc->dc", normed_qry, back_query, preferred_element_type=FLOAT),
            jnp.einsum("rd,rc->dc", normed_ctx, back_key, preferred_element_type=FLOAT),
            jnp.einsum("rd,rc->dc", normed_ctx, back_value, preferred_element_type=FLOAT),
        ]
    )
    part_qry = jnp.einsum("rc,dc->rd", back_query, qkv_half[0], preferred_element_type=FLOAT)
    part_ctx = jnp.einsum(
        "rc,dc->rd", back_key, qkv_half[1], preferred_element_type=FLOAT
    ) + jnp.einsum("rc,dc->rd", back_value, qkv_half[2], preferred_element_type=FLOAT)
    first_qry, gain_qry = norm_back(zero_qry, norm_gains[0], part_qry)
    first_ctx, gain_ctx = norm_back(zero_ctx, norm_gains[0], part_ctx)
    mine = (jnp.arange(total_qry) // qry_local == me)[:, None]
    back_qry = (first_qry + jnp.where(mine, back_one, 0.0)).astype(HALF)
    back_ctx = first_ctx.astype(HALF)
    grad_embed = jnp.einsum(
        "rx,rd->xd", qry_rows, back_qry, preferred_element_type=FLOAT
    ) + jnp.einsum("rx,rd->xd", ctx_rows, back_ctx, preferred_element_type=FLOAT)
    grad_bins = jnp.einsum("rb,rd->bd", bin_hits, back_ctx, preferred_element_type=FLOAT)
    grad_qkv, grad_out, grad_up, grad_down = [
        total.astype(FLOAT)
        for total in lax.psum(
            tuple(part.astype(HALF) for part in (grad_qkv, grad_out, grad_up, grad_down)), "tables"
        )
    ]
    grad_embed, grad_bins, grad_first = lax.psum(
        (grad_embed, grad_bins, gain_qry + gain_ctx), ("tables", "heads")
    )
    grad_head, grad_mid, grad_final, loss_sum = lax.psum(
        (grad_head, grad_mid, grad_final, loss_local), "tables"
    )
    grad_gains = jnp.stack([grad_first, grad_mid, grad_final])
    split_squares = (
        jnp.sum(grad_qkv * grad_qkv)
        + jnp.sum(grad_out * grad_out)
        + jnp.sum(grad_up * grad_up)
        + jnp.sum(grad_down * grad_down)
    )
    whole_squares = (
        jnp.sum(grad_embed * grad_embed)
        + jnp.sum(grad_bins * grad_bins)
        + jnp.sum(grad_gains * grad_gains)
        + jnp.sum(grad_head * grad_head)
    )
    grad_norm = jnp.sqrt(lax.psum(split_squares, "heads") + whole_squares)
    factor = jnp.minimum(1.0, CLIP_NORM / (grad_norm + 1e-06))
    embed_new, embed_first, embed_second = adam_update(
        w_embed, m_embed, v_embed, grad_embed * factor, RATE, DECAY
    )
    bins_new, bins_first, bins_second = adam_update(
        w_bins, m_bins, v_bins, grad_bins * factor, RATE_WIDE, DECAY
    )
    gains_new, gains_first, gains_second = adam_update(
        norm_gains, m_gains, v_gains, grad_gains * factor, RATE_WIDE, 0.0
    )
    qkv_new, qkv_first, qkv_second = adam_update(
        w_qkv, m_qkv, v_qkv, grad_qkv * factor, RATE, DECAY
    )
    out_new, out_first, out_second = adam_update(
        w_out, m_out, v_out, grad_out * factor, RATE_WIDE, DECAY
    )
    up_new, up_first, up_second = adam_update(w_up, m_up, v_up, grad_up * factor, RATE, DECAY)
    down_new, down_first, down_second = adam_update(
        w_down, m_down, v_down, grad_down * factor, RATE, DECAY
    )
    head_new, head_first, head_second = adam_update(
        w_head, m_head, v_head, grad_head * factor, RATE, DECAY
    )
    return (
        embed_new,
        bins_new,
        gains_new,
        qkv_new,
        out_new,
        up_new,
        down_new,
        head_new,
        embed_first,
        bins_first,
        gains_first,
        qkv_first,
        out_first,
        up_first,
        down_first,
        head_first,
        embed_second,
        bins_second,
        gains_second,
        qkv_second,
        out_second,
        up_second,
        down_second,
        head_second,
        loss_sum,
        query_count,
        grad_norm,
    )


def solution(mesh):
    in_specs = (
        P("tables", "heads", None),
        P("tables", "heads", None),
        P("tables"),
        P("tables", "heads"),
        P("tables", "heads"),
        P("tables", "heads"),
        P(),
        P(),
        P(),
        P(None, None, "heads"),
        P("heads", None),
        P(None, "heads"),
        P("heads", None),
        P(),
        P(),
        P(),
        P(),
        P(None, None, "heads"),
        P("heads", None),
        P(None, "heads"),
        P("heads", None),
        P(),
        P(),
        P(),
        P(),
        P(None, None, "heads"),
        P("heads", None),
        P(None, "heads"),
        P("heads", None),
        P(),
    )
    out_specs = (
        P(),
        P(),
        P(),
        P(None, None, "heads"),
        P("heads", None),
        P(None, "heads"),
        P("heads", None),
        P(),
        P(),
        P(),
        P(),
        P(None, None, "heads"),
        P("heads", None),
        P(None, "heads"),
        P("heads", None),
        P(),
        P(),
        P(),
        P(),
        P(None, None, "heads"),
        P("heads", None),
        P(None, "heads"),
        P("heads", None),
        P(),
        P(),
        P(),
        P(),
    )
    return jax.shard_map(shards, mesh=mesh, in_specs=in_specs, out_specs=out_specs, check_vma=False)
```

```python
import jax
import jax.numpy as jnp
from jax import lax
from jax.experimental import pallas as pl
from jax.experimental.pallas import tpu as pltpu
from jax.sharding import PartitionSpec as P

HD = 64
BINS = 64
STEP = 10


NORM_EPS = 1e-05
ADAM_EPS = 1e-08
RATE = 0.05
RATE_WIDE = 1.0
BETA_ONE = 0.9
BETA_TWO = 0.95
DECAY = 0.1
CLIP_NORM = 0.02
MASKED = -1e30
FLOAT = jnp.float32
HALF = jnp.bfloat16
MESH = pl.DeviceIdType.MESH


def product(left, right):
    return jnp.dot(left, right, preferred_element_type=FLOAT)


def normalize(hidden, gain_row):
    center = hidden - jnp.mean(hidden, axis=-1, keepdims=True)
    spread = jnp.mean(center * center, axis=-1, keepdims=True)
    return center * lax.rsqrt(spread + NORM_EPS) * gain_row


def norm_back(hidden, gain_row, upstream):
    _, pullback = jax.vjp(normalize, hidden, gain_row)
    return pullback(upstream)


def adam_update(weight, moment_one, moment_two, gradient, rate, decay_rate):
    moment_one = BETA_ONE * moment_one + (1.0 - BETA_ONE) * gradient
    moment_two = BETA_TWO * moment_two + (1.0 - BETA_TWO) * gradient * gradient
    first_hat = moment_one / (1.0 - BETA_ONE**STEP)
    second_hat = moment_two / (1.0 - BETA_TWO**STEP)
    weight = weight - rate * (first_hat / (jnp.sqrt(second_hat) + ADAM_EPS) + decay_rate * weight)
    return (weight, moment_one, moment_two)


def softmax_rows(query_heads, key_heads, live_keys):
    raw_scores = jnp.einsum(
        "bhe,khe->hbk", query_heads, key_heads, preferred_element_type=FLOAT
    ) * HD ** (-0.5)
    masked = jnp.where(live_keys[None, None, :], raw_scores, MASKED)
    top_score = jnp.max(masked, axis=-1, keepdims=True)
    unnormed = jnp.exp(masked - top_score)
    return unnormed / jnp.sum(unnormed, axis=-1, keepdims=True)


def gather(rows, axis=0):
    return lax.all_gather(rows, "heads", axis=axis, tiled=True)


def place_bit(place, bit):
    return lax.rem(lax.div(place, bit), 2)


def bits_of(size):
    return [1 << power for power in range(size.bit_length() - 1)]


class Pool:
    def __init__(self, send_sems, recv_sems, landing):
        self.send_sems, self.recv_sems, self.landing = send_sems, recv_sems, landing
        self.copies = self.rows = 0

    def semaphores(self):
        self.copies += 1
        return self.send_sems.at[self.copies - 1], self.recv_sems.at[self.copies - 1]

    def land(self, rows):
        self.rows += rows
        return self.landing.at[pl.ds(self.rows - rows, rows), :]


def stages_of(rows, axes, least):
    steps = []
    for axis, bit in axes:
        if rows // 2 >= least and rows % 32 == 0:
            rows //= 2
            steps.append((axis, bit, "halve", rows))
        else:
            steps.append((axis, bit, "whole", rows))
    back = [(axis, bit, "back", left) for axis, bit, kind, left in reversed(steps) if kind == "halve"]
    return steps + back


def landing_rows(steps):
    return sum(left for _, _, kind, left in steps if kind != "back")


class Sum:
    def __init__(self, pool, buffer, result, start, steps, places):
        self.pool, self.buffer, self.result, self.low = pool, buffer, result, start
        self.steps, self.places = steps, places
        self.at, self.copy, self.landed = 0, None, None

    def rows(self, low, count):
        return pl.ds(pl.multiple_of(low, 16), count)

    def finish(self):
        if self.copy is None:
            return
        _, _, kind, count = self.steps[self.at - 1]
        self.copy.wait()
        self.copy = None
        if kind != "back":
            mine = self.rows(self.low, count)
            total = self.buffer[mine, :].astype(FLOAT) + self.landed[...].astype(FLOAT)
            last = self.at == len(self.steps) or self.steps[self.at][2] == "back"
            target = self.result if last else self.buffer
            target[mine, :] = total.astype(self.buffer.dtype)

    def start(self):
        if self.at >= len(self.steps):
            return
        axis, bit, kind, count = self.steps[self.at]
        self.at += 1
        side = place_bit(self.places[axis], bit)
        other = dict(self.places)
        other[axis] = self.places[axis] + bit - 2 * bit * side
        if kind == "halve":
            source = self.buffer.at[self.rows(self.low + count * (1 - side), count), :]
            self.low = self.low + count * side
            self.landed = self.pool.land(count)
            target = self.landed
        elif kind == "whole":
            source = self.buffer.at[self.rows(self.low, count), :]
            self.landed = self.pool.land(count)
            target = self.landed
        else:
            source = target = self.result.at[self.rows(self.low, count), :]
            self.low = self.low - count * side
        send_sem, recv_sem = self.pool.semaphores()
        self.copy = pltpu.make_async_remote_copy(
            src_ref=source,
            dst_ref=target,
            send_sem=send_sem,
            recv_sem=recv_sem,
            device_id=(other["tables"], other["heads"]),
            device_id_type=MESH,
        )
        self.copy.start()

    def advance(self):
        self.finish()
        self.start()

    def done(self):
        return self.at >= len(self.steps) and self.copy is None


def places_here():
    return {"tables": lax.axis_index("tables"), "heads": lax.axis_index("heads")}


def greet(places, axes):
    barrier = pltpu.get_barrier_semaphore()
    for axis, bit in axes:
        other = dict(places)
        other[axis] = places[axis] + bit - 2 * bit * place_bit(places[axis], bit)
        pl.semaphore_signal(
            barrier, inc=1, device_id=(other["tables"], other["heads"]), device_id_type=MESH
        )
    pl.semaphore_wait(barrier, len(axes))


SMALL = {"head": (0, 64), "bins": (64, 64), "embed": (128, 112), "gains": (240, 16)}
SMALL_ROWS = 256


def reduce_plan(sizes, main_rows):
    over_tables = [("tables", bit) for bit in bits_of(sizes["tables"])]
    over_heads = [("heads", bit) for bit in bits_of(sizes["heads"])]
    chunk = 384 if main_rows % 384 == 0 else main_rows
    main = [stages_of(chunk, over_tables, 16) for _ in range(main_rows // chunk)]
    small = stages_of(SMALL_ROWS, over_heads + over_tables, 64)
    return over_tables, over_heads, chunk, main, small


def sum_squares(rows_ref, count):
    def piece(step, total):
        part = rows_ref[pl.ds(pl.multiple_of(step * 64, 64), 64), :].astype(FLOAT)
        return total + jnp.sum((part * part).reshape(8, 8, part.shape[1]), axis=0)

    return lax.fori_loop(0, count // 64, piece, jnp.zeros((8, rows_ref.shape[1]), FLOAT))


def one_value(total):
    value = jnp.sum(jnp.sum(total, axis=0, keepdims=True), axis=1, keepdims=True)
    return jnp.broadcast_to(value, (8, 128))


def reduce_kernel(sizes, in_refs, out_refs, scratch):
    down, up, out, qkv, small, loss = in_refs
    main_ref, small_ref, stats_ref = out_refs
    main_work, small_work, loss_work, square_work, landing, loss_buf, square_buf, loss_land, square_land, sends, recvs = scratch
    places = places_here()
    over_tables, over_heads, chunk, main_steps, small_steps = reduce_plan(sizes, main_ref.shape[0])
    greet(places, over_tables + over_heads)
    low = 0
    for part in (down, up, out, qkv):
        main_work[pl.ds(low, part.shape[0]), :] = part[...]
        low += part.shape[0]
    small_work[...] = small[...]
    loss_work[...] = loss[...]
    pool = Pool(sends, recvs, landing)
    mains = [
        Sum(pool, main_work, main_ref, chunk * place, steps, places) for place, steps in enumerate(main_steps)
    ]
    smalls = Sum(pool, small_work, small_ref, 0, small_steps, places)
    losses = Sum(
        Pool(sends.at[pl.ds(64, 16)], recvs.at[pl.ds(64, 16)], loss_land),
        loss_work,
        loss_buf,
        0,
        stages_of(16, over_heads + over_tables, 16),
        places,
    )
    waiting = len(over_heads)
    slots = len(mains) - 1 + len(main_steps[0]) + 1
    for slot in range(slots):
        for place, part in enumerate(mains):
            if 0 <= slot - place <= len(part.steps):
                part.advance()
        if smalls.at < len(small_steps) - waiting:
            smalls.advance()
        losses.advance()
    while smalls.at < len(small_steps) - waiting:
        smalls.advance()
    while not losses.done():
        losses.advance()
    square_work[...] = jnp.broadcast_to(
        one_value(sum_squares(main_ref, main_ref.shape[0]))[:1], square_work.shape
    )
    squares = Sum(
        Pool(sends.at[pl.ds(80, 8)], recvs.at[pl.ds(80, 8)], square_land),
        square_work,
        square_buf,
        0,
        stages_of(16, list(reversed(over_heads)), 16),
        places,
    )
    while not (squares.done() and smalls.done()):
        smalls.advance()
        squares.advance()
    whole = one_value(sum_squares(small_ref, SMALL_ROWS))
    row = lax.broadcasted_iota(jnp.int32, (8, 128), 0)
    stats_ref[...] = jnp.where(row == 0, square_buf[:8] + whole, loss_buf[:8])


def reduce_gradients(sizes, down, up, out, qkv, small, loss):
    main_rows = down.shape[0] + up.shape[0] + out.shape[0] + qkv.shape[0]
    width = down.shape[1]
    over_tables, over_heads, chunk, main_steps, small_steps = reduce_plan(sizes, main_rows)
    rows = sum(map(landing_rows, main_steps)) + landing_rows(small_steps)
    tiny = 16 * (len(over_tables) + len(over_heads))
    whole = pl.BlockSpec(memory_space=pltpu.VMEM)
    assert sum(map(len, main_steps)) + len(small_steps) <= 64 or sizes["tables"] > 8

    def kernel(*refs):
        reduce_kernel(sizes, refs[:6], refs[6:9], refs[9:])

    return pl.pallas_call(
        kernel,
        out_shape=(
            jax.ShapeDtypeStruct((main_rows, width), HALF),
            jax.ShapeDtypeStruct((SMALL_ROWS, width), HALF),
            jax.ShapeDtypeStruct((8, 128), FLOAT),
        ),
        in_specs=[whole] * 6,
        out_specs=(whole,) * 3,
        scratch_shapes=[
            pltpu.VMEM((main_rows, width), HALF),
            pltpu.VMEM((SMALL_ROWS, width), HALF),
            pltpu.VMEM((16, 128), FLOAT),
            pltpu.VMEM((16, 128), FLOAT),
            pltpu.VMEM((rows, width), HALF),
            pltpu.VMEM((16, 128), FLOAT),
            pltpu.VMEM((16, 128), FLOAT),
            pltpu.VMEM((tiny, 128), FLOAT),
            pltpu.VMEM((16 * len(over_heads), 128), FLOAT),
            pltpu.SemaphoreType.DMA((160,)),
            pltpu.SemaphoreType.DMA((160,)),
        ],
        compiler_params=pltpu.CompilerParams(
            collective_id=1, has_side_effects=True, vmem_limit_bytes=32 * 2**20
        ),
        name="reduce_gradients",
    )(down, up, out, qkv, small, loss)


def adam_kernel(refs):
    (stats, main_d, main_u, main_o, main_q, small) = refs[:6]
    w = refs[6:14]
    m = refs[14:22]
    v = refs[22:30]
    w_new = refs[30:38]
    m_new = refs[38:46]
    v_new = refs[46:54]
    norm_ref = refs[54]
    norm = jnp.sqrt(stats[0:1, 0:1])
    norm_ref[...] = jnp.broadcast_to(norm, norm_ref.shape)
    factor = jnp.minimum(1.0, CLIP_NORM / (norm + 1e-06))

    def update(which, gradient, rate, decay, at=...):
        gradient = gradient.astype(FLOAT) * factor
        results = adam_update(w[which][at], m[which][at], v[which][at], gradient, rate, decay)
        for target, value in zip((w_new, m_new, v_new), results):
            target[which][at] = value

    update(6, main_d[...], RATE, DECAY)
    update(5, main_u[...], RATE, DECAY)
    update(4, main_o[...], RATE_WIDE, DECAY)
    width = w[3].shape[2]
    turned = main_q[...].astype(FLOAT).T
    for part in range(3):
        update(3, turned[:, part * width : (part + 1) * width], RATE, DECAY, at=part)

    @pl.when(pl.program_id(0) == 0)
    def _():
        def rows(name, count):
            low, size = SMALL[name]
            return small[low : low + size, :].astype(FLOAT)[:count]

        update(0, rows("embed", w[0].shape[0]), RATE, DECAY)
        update(1, rows("bins", w[1].shape[0]), RATE_WIDE, DECAY)
        update(2, rows("gains", w[2].shape[0]), RATE_WIDE, 0.0)
        update(7, rows("head", w[7].shape[1]).T, RATE, DECAY)


def adam_all(stats, main, small, weights, firsts, seconds):
    width = main.shape[1]
    steps = width // 128
    hidden = weights[5].shape[1]
    inner = weights[4].shape[0]
    low_out, low_qkv = 2 * hidden, 2 * hidden + inner

    def fixed(array):
        return pl.BlockSpec(array.shape, lambda step: (0,) * array.ndim)

    def rows_of(array):
        return pl.BlockSpec((array.shape[0] // steps, array.shape[1]), lambda step: (step, 0))

    blocks = [
        fixed(weights[0]),
        fixed(weights[1]),
        fixed(weights[2]),
        pl.BlockSpec((3, width // steps, inner), lambda step: (0, step, 0)),
        rows_of(weights[4]),
        rows_of(weights[5]),
        rows_of(weights[6]),
        fixed(weights[7]),
    ]
    down = main[:hidden]
    up = main[hidden:low_out]
    out = main[low_out:low_qkv]
    qkv = main[low_qkv:]
    shapes = [jax.ShapeDtypeStruct(weight.shape, FLOAT) for weight in weights]
    return pl.pallas_call(
        lambda *refs: adam_kernel(refs),
        grid=(steps,),
        in_specs=[
            fixed(stats),
            rows_of(down),
            rows_of(up),
            rows_of(out),
            pl.BlockSpec((qkv.shape[0], width // steps), lambda step: (0, step)),
            fixed(small),
        ]
        + blocks * 3,
        out_specs=blocks * 3 + [fixed(stats)],
        out_shape=shapes * 3 + [jax.ShapeDtypeStruct(stats.shape, FLOAT)],
        compiler_params=pltpu.CompilerParams(vmem_limit_bytes=48 * 2**20),
        name="adam",
    )(stats, down, up, out, qkv, small, *weights, *firsts, *seconds)


def shards(
    ctx_feat,
    qry_feat,
    counts,
    ctx_bins,
    qry_bins,
    query_mask,
    w_embed,
    w_bins,
    norm_gains,
    w_qkv,
    w_out,
    w_up,
    w_down,
    w_head,
    m_embed,
    m_bins,
    m_gains,
    m_qkv,
    m_out,
    m_up,
    m_down,
    m_head,
    v_embed,
    v_bins,
    v_gains,
    v_qkv,
    v_out,
    v_up,
    v_down,
    v_head,
):
    model_width = w_embed.shape[1]
    heads_here = w_qkv.shape[2] // HD
    me = lax.axis_index("heads")
    qry_local = qry_feat.shape[1]
    ctx_rows = gather(ctx_feat[0])
    qry_rows = gather(qry_feat[0])
    all_bins = gather(jnp.concatenate([ctx_bins[0], qry_bins[0], query_mask[0]]).reshape(1, -1))
    ctx_local = ctx_feat.shape[1]
    all_ctx_bins = all_bins[:, :ctx_local].reshape(-1)
    all_qry_bins = all_bins[:, ctx_local : ctx_local + qry_local].reshape(-1)
    mask_rows = all_bins[:, ctx_local + qry_local :].reshape(-1).astype(FLOAT)
    total_ctx = ctx_rows.shape[0]
    total_qry = qry_rows.shape[0]
    bin_hits = (all_ctx_bins[:, None] == jnp.arange(BINS)[None, :]).astype(HALF)
    query_count = lax.psum(jnp.sum(mask_rows), "tables")
    divisor = jnp.maximum(query_count, 1.0)
    embed_half = w_embed.astype(HALF)
    bins_half = w_bins.astype(HALF)
    qkv_half = w_qkv.astype(HALF)
    out_half = w_out.astype(HALF)
    up_half = w_up.astype(HALF)
    down_half = w_down.astype(HALF)
    head_half = w_head.astype(HALF)
    out_full = gather(out_half)
    zero_ctx = product(ctx_rows, embed_half) + product(bin_hits, bins_half)
    zero_qry = product(qry_rows, embed_half)
    normed_ctx = normalize(zero_ctx, norm_gains[0]).astype(HALF)
    normed_qry = normalize(zero_qry, norm_gains[0]).astype(HALF)
    queries = product(normed_qry, qkv_half[0]).astype(HALF).reshape(total_qry, heads_here, HD)
    key_heads = product(normed_ctx, qkv_half[1]).astype(HALF).reshape(total_ctx, heads_here, HD)
    value_heads = product(normed_ctx, qkv_half[2]).astype(HALF).reshape(total_ctx, heads_here, HD)
    live_keys = jnp.arange(total_ctx) < counts[0]
    weights = softmax_rows(queries, key_heads, live_keys)
    mixture = jnp.einsum(
        "hbk,khe->bhe", weights.astype(HALF), value_heads, preferred_element_type=FLOAT
    )
    mixture = mixture.reshape(total_qry, -1).astype(HALF)
    stream_one = zero_qry + product(gather(mixture, 1), out_full)
    normed_two = normalize(stream_one, norm_gains[1]).astype(HALF)
    hidden_up = product(normed_two, up_half)
    active = jax.nn.gelu(hidden_up).astype(HALF)
    mlp = lax.psum(product(active, down_half).astype(HALF), "heads")
    stream_two = stream_one + mlp.astype(FLOAT)
    normed_final = normalize(stream_two, norm_gains[2]).astype(HALF)
    logits = product(normed_final, head_half)
    log_bins = jax.nn.logsumexp(logits, axis=-1)
    target_hits = (all_qry_bins[:, None] == jnp.arange(BINS)[None, :]).astype(FLOAT)
    loss_local = jnp.sum(mask_rows * (log_bins - jnp.sum(target_hits * logits, axis=-1)))
    back_logits = (
        mask_rows[:, None] * (jnp.exp(logits - log_bins[:, None]) - target_hits) / divisor
    ).astype(HALF)
    grad_head = jnp.einsum("rd,rb->db", normed_final, back_logits, preferred_element_type=FLOAT)
    back_final = jnp.einsum("rb,db->rd", back_logits, head_half, preferred_element_type=FLOAT)
    back_two, grad_final = norm_back(stream_two, norm_gains[2], back_final)
    back_mlp = back_two.astype(HALF)
    grad_down = jnp.einsum("rf,rd->fd", active, back_mlp, preferred_element_type=FLOAT)
    back_active = jnp.einsum("rd,fd->rf", back_mlp, down_half, preferred_element_type=FLOAT)
    _, gelu_pull = jax.vjp(jax.nn.gelu, hidden_up)
    back_up = gelu_pull(back_active)[0].astype(HALF)
    grad_up = jnp.einsum("rd,rf->df", normed_two, back_up, preferred_element_type=FLOAT)
    back_norm_two = jnp.einsum("rf,df->rd", back_up, up_half, preferred_element_type=FLOAT)
    back_norm_two = lax.psum(back_norm_two.astype(HALF), "heads").astype(FLOAT)
    back_mid, grad_mid = norm_back(stream_one, norm_gains[1], back_norm_two)
    back_one = back_two + back_mid
    back_attn = back_one.astype(HALF)
    grad_out = jnp.einsum("rc,rd->cd", mixture, back_attn, preferred_element_type=FLOAT)
    back_mix = jnp.einsum("rd,cd->rc", back_attn, out_half, preferred_element_type=FLOAT)
    back_mix = back_mix.astype(HALF).reshape(total_qry, heads_here, HD)
    back_value = jnp.einsum(
        "hbk,bhe->khe", weights.astype(HALF), back_mix, preferred_element_type=FLOAT
    )
    back_weights = jnp.einsum("bhe,khe->hbk", back_mix, value_heads, preferred_element_type=FLOAT)
    back_scores = weights * (
        back_weights - jnp.sum(weights * back_weights, axis=-1, keepdims=True)
    )
    back_scores = back_scores.astype(HALF) * HD ** (-0.5)
    back_query = jnp.einsum("hbk,khe->bhe", back_scores, key_heads, preferred_element_type=FLOAT)
    back_key = jnp.einsum("hbk,bhe->khe", back_scores, queries, preferred_element_type=FLOAT)
    back_query = back_query.reshape(total_qry, -1).astype(HALF)
    back_key = back_key.reshape(total_ctx, -1).astype(HALF)
    back_value = back_value.reshape(total_ctx, -1).astype(HALF)
    grad_qkv = jnp.concatenate(
        [
            jnp.einsum("rc,rd->cd", back_query, normed_qry, preferred_element_type=FLOAT),
            jnp.einsum("rc,rd->cd", back_key, normed_ctx, preferred_element_type=FLOAT),
            jnp.einsum("rc,rd->cd", back_value, normed_ctx, preferred_element_type=FLOAT),
        ]
    )
    part_qry = jnp.einsum("rc,dc->rd", back_query, qkv_half[0], preferred_element_type=FLOAT)
    part_ctx = jnp.einsum(
        "rc,dc->rd", back_key, qkv_half[1], preferred_element_type=FLOAT
    ) + jnp.einsum("rc,dc->rd", back_value, qkv_half[2], preferred_element_type=FLOAT)
    first_qry, gain_qry = norm_back(zero_qry, norm_gains[0], part_qry)
    first_ctx, gain_ctx = norm_back(zero_ctx, norm_gains[0], part_ctx)
    mine = (jnp.arange(total_qry) // qry_local == me)[:, None]
    back_qry = (first_qry + jnp.where(mine, back_one, 0.0)).astype(HALF)
    back_ctx = first_ctx.astype(HALF)
    grad_embed = jnp.einsum(
        "rx,rd->xd", qry_rows, back_qry, preferred_element_type=FLOAT
    ) + jnp.einsum("rx,rd->xd", ctx_rows, back_ctx, preferred_element_type=FLOAT)
    grad_bins = jnp.einsum("rb,rd->bd", bin_hits, back_ctx, preferred_element_type=FLOAT)
    groups = lax.axis_size("heads")
    sizes = {"tables": lax.axis_size("tables"), "heads": groups}
    grad_head = jnp.transpose(grad_head) / groups
    gains = jnp.stack([gain_qry + gain_ctx, grad_mid / groups, grad_final / groups])
    feature_pad = SMALL["embed"][1] - grad_embed.shape[0]
    gains_pad = SMALL["gains"][1] - gains.shape[0]
    small = jnp.concatenate(
        [
            grad_head,
            grad_bins,
            jnp.pad(grad_embed, ((0, feature_pad), (0, 0))),
            jnp.pad(gains, ((0, gains_pad), (0, 0))),
        ]
    ).astype(HALF)
    main, small, stats = reduce_gradients(
        sizes,
        grad_down.astype(HALF),
        grad_up.astype(HALF),
        grad_out.astype(HALF),
        grad_qkv.astype(HALF),
        small,
        jnp.full((16, 128), loss_local / groups, FLOAT),
    )
    results = adam_all(
        stats,
        main,
        small,
        (w_embed, w_bins, norm_gains, w_qkv, w_out, w_up, w_down, w_head),
        (m_embed, m_bins, m_gains, m_qkv, m_out, m_up, m_down, m_head),
        (v_embed, v_bins, v_gains, v_qkv, v_out, v_up, v_down, v_head),
    )
    return (*results[:24], stats[1, 0], query_count, results[24][0, 0])


def solution(mesh):
    in_specs = (
        P("tables", "heads", None),
        P("tables", "heads", None),
        P("tables"),
        P("tables", "heads"),
        P("tables", "heads"),
        P("tables", "heads"),
        P(),
        P(),
        P(),
        P(None, None, "heads"),
        P("heads", None),
        P(None, "heads"),
        P("heads", None),
        P(),
        P(),
        P(),
        P(),
        P(None, None, "heads"),
        P("heads", None),
        P(None, "heads"),
        P("heads", None),
        P(),
        P(),
        P(),
        P(),
        P(None, None, "heads"),
        P("heads", None),
        P(None, "heads"),
        P("heads", None),
        P(),
    )
    out_specs = (
        P(),
        P(),
        P(),
        P(None, None, "heads"),
        P("heads", None),
        P(None, "heads"),
        P("heads", None),
        P(),
        P(),
        P(),
        P(),
        P(None, None, "heads"),
        P("heads", None),
        P(None, "heads"),
        P("heads", None),
        P(),
        P(),
        P(),
        P(),
        P(None, None, "heads"),
        P("heads", None),
        P(None, "heads"),
        P("heads", None),
        P(),
        P(),
        P(),
        P(),
    )
    return jax.shard_map(shards, mesh=mesh, in_specs=in_specs, out_specs=out_specs, check_vma=False)
```

```python
import jax
import jax.numpy as jnp
from jax import lax
from jax.experimental import pallas as pl
from jax.experimental.pallas import tpu as pltpu
from jax.sharding import PartitionSpec as P

HD = 64
BINS = 64
STEP = 10


NORM_EPS = 1e-05
ADAM_EPS = 1e-08
RATE = 0.05
RATE_WIDE = 1.0
BETA_ONE = 0.9
BETA_TWO = 0.95
DECAY = 0.1
CLIP_NORM = 0.02
MASKED = -1e30
FLOAT = jnp.float32
HALF = jnp.bfloat16
MESH = pl.DeviceIdType.MESH


def adam_update(weight, moment_one, moment_two, gradient, rate, decay_rate):
    moment_one = BETA_ONE * moment_one + (1.0 - BETA_ONE) * gradient
    moment_two = BETA_TWO * moment_two + (1.0 - BETA_TWO) * gradient * gradient
    first_hat = moment_one / (1.0 - BETA_ONE**STEP)
    second_hat = moment_two / (1.0 - BETA_TWO**STEP)
    weight = weight - rate * (first_hat / (jnp.sqrt(second_hat) + ADAM_EPS) + decay_rate * weight)
    return (weight, moment_one, moment_two)


def place_bit(place, bit):
    return lax.rem(lax.div(place, bit), 2)


def flip(place, bit):
    return place + bit - 2 * bit * place_bit(place, bit)


def bits_of(size):
    return [1 << power for power in range(size.bit_length() - 1)]


def partner(places, axis, bit):
    other = dict(places)
    other[axis] = flip(places[axis], bit)
    return (other["tables"], other["heads"])


def greet(places, axes):
    barrier = pltpu.get_barrier_semaphore()
    for axis, bit in axes:
        pl.semaphore_signal(
            barrier, inc=1, device_id=partner(places, axis, bit), device_id_type=MESH
        )
    pl.semaphore_wait(barrier, len(axes))


class Copies:
    def __init__(self, sends, recvs):
        self.sends, self.recvs, self.used = sends, recvs, 0

    def start(self, source, target, device):
        self.used += 1
        copy = pltpu.make_async_remote_copy(
            src_ref=source,
            dst_ref=target,
            send_sem=self.sends.at[self.used - 1],
            recv_sem=self.recvs.at[self.used - 1],
            device_id=device,
            device_id_type=MESH,
        )
        copy.start()
        return copy


class Landing:
    def __init__(self, rows_ref):
        self.rows_ref, self.used = rows_ref, 0

    def take(self, rows):
        self.used += rows
        return self.rows_ref.at[pl.ds(self.used - rows, rows), :]


def stages_of(rows, axes, least):
    steps = []
    for axis, bit in axes:
        if rows // 2 >= least and rows % 32 == 0:
            rows //= 2
            steps.append((axis, bit, "halve", rows))
        else:
            steps.append((axis, bit, "whole", rows))
    back = [(axis, bit, "back", left) for axis, bit, kind, left in reversed(steps) if kind == "halve"]
    return steps + back


def landing_rows(steps):
    return sum(left for _, _, kind, left in steps if kind != "back")


class Sum:
    def __init__(self, copies, landing, buffer, result, start, steps, places):
        self.copies, self.landing, self.buffer, self.result = copies, landing, buffer, result
        self.low, self.steps, self.places = start, steps, places
        self.at, self.copy, self.landed = 0, None, None

    def rows(self, low, count):
        if isinstance(low, int):
            return pl.ds(low, count)
        return pl.ds(pl.multiple_of(low, 16), count)

    def finish(self):
        if self.copy is None:
            return
        _, _, kind, count = self.steps[self.at - 1]
        self.copy.wait()
        self.copy = None
        if kind != "back":
            mine = self.rows(self.low, count)
            total = self.buffer[mine, :].astype(FLOAT) + self.landed[...].astype(FLOAT)
            last = self.at == len(self.steps) or self.steps[self.at][2] == "back"
            target = self.result if last else self.buffer
            target[mine, :] = total.astype(self.buffer.dtype)

    def start(self):
        if self.at >= len(self.steps):
            return
        axis, bit, kind, count = self.steps[self.at]
        self.at += 1
        side = place_bit(self.places[axis], bit)
        if kind == "halve":
            source = self.buffer.at[self.rows(self.low + count * (1 - side), count), :]
            self.low = self.low + count * side
            target = self.landed = self.landing.take(count)
        elif kind == "whole":
            source = self.buffer.at[self.rows(self.low, count), :]
            target = self.landed = self.landing.take(count)
        else:
            source = target = self.result.at[self.rows(self.low, count), :]
            self.low = self.low - count * side
        self.copy = self.copies.start(source, target, partner(self.places, axis, bit))

    def advance(self):
        self.finish()
        self.start()

    def done(self):
        return self.at >= len(self.steps) and self.copy is None


class Gather:
    def __init__(self, copies, views, places, bits):
        self.copies, self.views, self.places = copies, views, places
        self.bits, self.at, self.held, self.sent = bits, 0, [places["heads"]], []

    def finish(self):
        for copy in self.sent:
            copy.wait()
        if self.sent:
            self.held = self.held + [flip(slot, self.bits[self.at - 1]) for slot in self.held]
        self.sent = []

    def start(self):
        if self.at < len(self.bits):
            other = partner(self.places, "heads", self.bits[self.at])
            self.sent = [
                self.copies.start(view(slot), view(slot), other)
                for slot in self.held
                for view in self.views
            ]
            self.at += 1

    def advance(self):
        self.finish()
        self.start()

    def done(self):
        return self.at >= len(self.bits) and not self.sent


def places_here():
    return {"tables": lax.axis_index("tables"), "heads": lax.axis_index("heads")}


SMALL = {"head": (0, 64), "bins": (64, 64), "embed": (128, 112), "gains": (240, 16)}
SMALL_ROWS = 256
CHUNK = 256


def dot(left, right, over=(1, 0)):
    return lax.dot_general(
        left, right, (((over[0],), (over[1],)), ((), ())), preferred_element_type=FLOAT
    )


def standard(rows):
    center = rows - jnp.mean(rows, axis=-1, keepdims=True)
    scale = lax.rsqrt(jnp.mean(center * center, axis=-1, keepdims=True) + NORM_EPS)
    return center * scale, scale


def standard_back(upstream, gain_row, unit, scale):
    inner = upstream * gain_row
    lean = jnp.mean(inner, axis=-1, keepdims=True)
    tilt = jnp.mean(inner * unit, axis=-1, keepdims=True)
    return (inner - lean - unit * tilt) * scale


def as_row(column):
    return jnp.broadcast_to(column, (column.shape[0], 128)).T[:1]


def as_column(row):
    return jnp.broadcast_to(row, (8, row.shape[1])).T[:, :1]


def column_sums(rows):
    return jnp.sum(rows, axis=0, keepdims=True)


def gelu_both(hidden):
    root = 0.7978845608028654
    square = hidden * hidden
    bent = jnp.tanh(root * hidden * (1.0 + 0.044715 * square))
    half = 0.5 * (1.0 + bent)
    slope = half + 0.5 * hidden * (1.0 - bent * bent) * root * (1.0 + 0.134145 * square)
    return hidden * half, slope


def sum_squares(rows_ref, count):
    def piece(step, total):
        part = rows_ref[pl.ds(pl.multiple_of(step * 64, 64), 64), :].astype(FLOAT)
        return total + jnp.sum((part * part).reshape(8, 8, part.shape[1]), axis=0)

    return lax.fori_loop(0, count // 64, piece, jnp.zeros((8, rows_ref.shape[1]), FLOAT))


def one_value(total):
    return jnp.sum(jnp.sum(total, axis=0, keepdims=True), axis=1, keepdims=True)


class Named:
    pass


def train_kernel(shape, r):
    groups, ctx, qry, width, inner, hidden = (
        shape.groups,
        shape.ctx,
        shape.qry,
        shape.width,
        shape.inner,
        shape.hidden,
    )
    heads = inner // HD
    total_ctx, total_qry = groups * ctx, groups * qry
    block = 2 * qry
    blocks = total_qry // block
    half = width // 2
    places = places_here()
    me = places["heads"]
    copies = Copies(r.sends, r.recvs)
    over_heads, over_tables = shape.over_heads, shape.over_tables
    far_first = [bit for _, bit in reversed(over_heads)]
    tiny = Landing(r.tiny_land)
    wide = Landing(r.wide_land)
    narrow = Landing(r.narrow_land)
    greet(places, over_heads + over_tables)

    r.feat[me, pl.ds(0, ctx), :] = r.ctx_feat[...]
    r.feat[me, pl.ds(ctx, qry), :] = r.qry_feat[...]
    r.ints[me] = jnp.zeros((8, ctx), jnp.int32)
    r.ints[me, 0:1, :] = r.ctx_bins[...]
    r.ints[me, 1:2, pl.ds(0, qry)] = r.qry_bins[...]
    r.ints[me, 2:3, pl.ds(0, qry)] = r.query_mask[...]
    rows_in = Gather(
        copies,
        [lambda slot: r.feat.at[slot], lambda slot: r.ints.at[slot]],
        places,
        far_first,
    )
    rows_in.start()
    mask_sum = jnp.sum(r.query_mask[...].astype(FLOAT), axis=1, keepdims=True)
    r.count_work[...] = jnp.broadcast_to(mask_sum, (16, 128))
    tiny_steps = stages_of(16, over_heads + over_tables, 16)
    counted = Sum(copies, tiny, r.count_work, r.count, 0, tiny_steps, places)
    counted.start()
    r.out_all[me] = r.w_out[...]
    outs_in = Gather(copies, [lambda slot: r.out_all.at[slot]], places, far_first)

    embed_half = r.w_embed[...].astype(HALF)
    bins_half = r.w_bins[...].astype(HALF)
    gain_one, gain_two, gain_last = (r.gains[row : row + 1, :] for row in range(3))
    bin_rows = lax.broadcasted_iota(jnp.int32, (BINS, 256), 0)

    def one_hot(slot, place):
        return jnp.where(
            bin_rows == r.ints[slot, 0:1, pl.ds(pl.multiple_of(place * 256, 256), 256)], 1.0, 0.0
        ).astype(HALF)

    def embed_shard(slot):
        def context(place, _):
            at = pl.multiple_of(slot * ctx + place * 256, 256)
            feat = r.feat[slot, pl.ds(pl.multiple_of(place * 256, 256), 256), :]
            zero = dot(feat, embed_half) + dot(one_hot(slot, place), bins_half, (0, 0))
            unit, scale = standard(zero)
            normed = (unit * gain_one).astype(HALF)
            r.normed_ctx[pl.ds(at, 256), :] = normed
            r.scale_ctx[pl.ds(slot * (ctx // 256) + place, 1), :] = as_row(scale)
            keys = dot(normed, r.w_qkv[1], (1, 1))
            values = dot(normed, r.w_qkv[2], (1, 1))
            r.keys[pl.ds(at, 256), :] = keys.astype(HALF)
            r.values[pl.ds(at, 256), :] = values.astype(HALF)
            r.keys_t[:, pl.ds(at, 256)] = keys.T.astype(HALF)
            r.values_t[:, pl.ds(at, 256)] = values.T.astype(HALF)
            return 0

        lax.fori_loop(0, ctx // 256, context, 0)
        at = pl.multiple_of(slot * qry, 16)
        zero = dot(r.feat[slot, pl.ds(ctx, qry), :], embed_half)
        r.stream[pl.ds(at, qry), :] = zero
        unit, scale = standard(zero)
        normed = (unit * gain_one).astype(HALF)
        r.normed_qry[pl.ds(at, qry), :] = normed
        r.scale_qry[pl.ds(slot, 1), :] = as_row(scale)
        queries = dot(normed, r.w_qkv[0], (1, 1))
        r.queries[pl.ds(at, qry), :] = queries.astype(HALF)
        r.queries_t[slot] = queries.T.astype(HALF)

    done = 0
    while done < groups:
        for slot in rows_in.held[done:]:
            embed_shard(slot)
            done += 1
            counted.advance()
            outs_in.advance()
        rows_in.advance()
    while not counted.done() and counted.at < len(counted.steps):
        counted.advance()

    lane = lax.broadcasted_iota(jnp.int32, (1, inner), 1)
    head_rows = [
        jnp.where((lane >= h * HD) & (lane < (h + 1) * HD), 1.0, 0.0).astype(FLOAT)
        for h in range(heads)
    ]
    slots_at = lax.broadcasted_iota(jnp.int32, (1, total_ctx), 1)
    dead = jnp.where(slots_at < r.counts[0], 0.0, MASKED)
    mixing = []
    for b in range(groups):
        rows = pl.ds(b * qry, qry)
        query_blk = r.queries[rows, :]
        mixed = jnp.zeros((qry, inner), FLOAT)
        for h in range(heads):
            raw = dot(query_blk * (head_rows[h] * HD**-0.5).astype(HALF), r.keys_t[...]) + dead
            raised = jnp.exp(raw - jnp.max(raw, axis=-1, keepdims=True))
            weights = (raised * (1.0 / jnp.sum(raised, axis=-1, keepdims=True))).astype(HALF)
            r.weights[h, rows, :] = weights
            mixed = mixed + dot(weights, r.values[...]) * head_rows[h]
        r.mixed[rows, :] = mixed
        r.mix_all[me, b] = mixed.astype(HALF)
        mixing.append(
            Gather(copies, [lambda slot, b=b: r.mix_all.at[slot, b]], places, far_first)
        )
        for gathering in mixing:
            gathering.advance()
        outs_in.advance()
    while not outs_in.done():
        outs_in.advance()
    while not counted.done():
        counted.advance()

    sum_steps = stages_of(2 * block, over_heads, block)
    down_sums, back_sums = [], []
    for b in range(blocks):
        for part in range(2 * b, 2 * b + 2):
            while not mixing[part].done():
                mixing[part].advance()
        rows = pl.ds(b * block, block)
        attended = []
        for part in range(2 * b, 2 * b + 2):
            total = dot(r.mix_all[0, part], r.out_all[0])
            for slot in range(1, groups):
                total = total + dot(r.mix_all[slot, part], r.out_all[slot])
            attended.append(total)
        stream = r.stream[rows, :] + jnp.concatenate(attended, axis=0)
        r.stream[rows, :] = stream
        unit, _ = standard(stream)
        normed = (unit * gain_two).astype(HALF)
        r.normed_two[rows, :] = normed
        active, slope = gelu_both(dot(normed, r.w_up[...]))
        active = active.astype(HALF)
        r.active[rows, :] = active
        r.slope[rows, :] = slope.astype(HALF)
        low = pl.ds(2 * b * block, block)
        high = pl.ds((2 * b + 1) * block, block)
        part = dot(active, r.w_down[...]).astype(HALF)
        r.down_work[low, :] = part[:, :half]
        r.down_work[high, :] = part[:, half:]
        summing = Sum(
            copies, narrow, r.down_work, r.down_sum, 2 * b * block, sum_steps, places
        )
        down_sums.append(summing)
        summing.start()
        for earlier in down_sums[:-1]:
            earlier.advance()

    head_half = r.w_head[...].astype(HALF)
    divisor = jnp.maximum(r.count[0:1, 0:1], 1.0)
    tall = lax.broadcasted_iota(jnp.int32, (BINS, 256), 0)
    loss = jnp.zeros((1, 1), FLOAT)
    grad_head = jnp.zeros((BINS, width), FLOAT)
    gain_sum_last = jnp.zeros((1, width), FLOAT)
    for b in range(blocks):
        for later in down_sums[b + 1 :]:
            later.advance()
        while not down_sums[b].done():
            down_sums[b].advance()
        rows = pl.ds(b * block, block)
        low = pl.ds(2 * b * block, block)
        high = pl.ds((2 * b + 1) * block, block)
        mlp = jnp.concatenate([r.down_sum[low, :], r.down_sum[high, :]], axis=1)
        unit, scale = standard(r.stream[rows, :] + mlp.astype(FLOAT))
        normed = (unit * gain_last).astype(HALF)
        logits = dot(normed, head_half, (1, 1))
        targets, masks = [], []
        for slot in range(2 * b, 2 * b + 2):
            target = jnp.where(tall == r.ints[slot, 1:2, 0:256], 1.0, 0.0)
            targets.append(target.T[:qry])
            mask = jnp.broadcast_to(r.ints[slot, 2:3, 0:256].astype(FLOAT), (8, 256))
            masks.append(mask.T[:qry, :1])
        target = jnp.concatenate(targets, axis=0)
        mask = jnp.concatenate(masks, axis=0)
        top = jnp.max(logits, axis=-1, keepdims=True)
        log_bins = top + jnp.log(jnp.sum(jnp.exp(logits - top), axis=-1, keepdims=True))
        missed = log_bins - jnp.sum(target * logits, axis=-1, keepdims=True)
        loss = loss + jnp.sum(mask * missed, axis=0, keepdims=True)
        back_logits = (mask * (jnp.exp(logits - log_bins) - target) / divisor).astype(HALF)
        grad_head = grad_head + dot(back_logits, normed, (0, 0))
        back_final = dot(back_logits, head_half)
        gain_sum_last = gain_sum_last + column_sums(back_final * unit)
        back_two = standard_back(back_final, gain_last, unit, scale)
        r.back[rows, :] = back_two
        back_mlp = back_two.astype(HALF)
        r.back_mlp[rows, :] = back_mlp
        back_active = dot(back_mlp, r.w_down[...], (1, 1))
        back_up = (r.slope[rows, :].astype(FLOAT) * back_active).astype(HALF)
        r.back_up[rows, :] = back_up
        part = dot(back_up, r.w_up[...], (1, 1)).astype(HALF)
        r.down_work[low, :] = part[:, :half]
        r.down_work[high, :] = part[:, half:]
        summing = Sum(
            copies, narrow, r.down_work, r.down_sum, 2 * b * block, sum_steps, places
        )
        back_sums.append(summing)
        summing.start()
        for earlier in back_sums[:-1]:
            earlier.advance()
    r.loss_work[...] = jnp.broadcast_to(loss / groups, (16, 128))
    losses = Sum(copies, tiny, r.loss_work, r.loss, 0, tiny_steps, places)
    losses.start()
    r.small[pl.ds(0, BINS), :] = grad_head / groups

    main_steps = stages_of(CHUNK, over_tables, 16)
    mains = []

    def pump():
        for part in mains:
            part.advance()
        losses.advance()

    def send_chunk(place):
        part = Sum(copies, wide, r.main_work, r.main, CHUNK * place, main_steps, places)
        part.start()
        mains.append(part)

    for place in range(hidden // CHUNK):
        at = pl.ds(place * CHUNK, CHUNK)
        r.main_work[at, :] = dot(r.active[:, at], r.back_mlp[...], (0, 0)).astype(HALF)
        send_chunk(len(mains))
        for summing in back_sums:
            summing.advance()
    for place in range(width // CHUNK):
        at = pl.ds(place * CHUNK, CHUNK)
        to = pl.ds(hidden + place * CHUNK, CHUNK)
        r.main_work[to, :] = dot(r.normed_two[:, at], r.back_up[...], (0, 0)).astype(HALF)
        send_chunk(len(mains))
        for summing in back_sums:
            summing.advance()

    gain_sum_two = jnp.zeros((1, width), FLOAT)
    r.keys_back[...] = jnp.zeros(r.keys_back.shape, FLOAT)
    r.values_back[...] = jnp.zeros(r.values_back.shape, FLOAT)
    for b in range(blocks):
        for later in back_sums[b + 1 :]:
            later.advance()
        while not back_sums[b].done():
            back_sums[b].advance()
        rows = pl.ds(b * block, block)
        low = pl.ds(2 * b * block, block)
        high = pl.ds((2 * b + 1) * block, block)
        upstream = jnp.concatenate([r.down_sum[low, :], r.down_sum[high, :]], axis=1).astype(FLOAT)
        unit, scale = standard(r.stream[rows, :])
        gain_sum_two = gain_sum_two + column_sums(upstream * unit)
        back_one = r.back[rows, :] + standard_back(upstream, gain_two, unit, scale)
        r.back[rows, :] = back_one
        back_attn = back_one.astype(HALF)
        r.slope[rows, :] = back_attn
        back_mix = dot(back_attn, r.w_out[...], (1, 1)).astype(HALF)
        r.back_mix[rows, :] = back_mix
        turned = back_mix.astype(FLOAT)
        for part in range(2):
            r.back_mix_t[2 * b + part] = turned[part * qry : (part + 1) * qry].T.astype(HALF)
        pump()
        for h in range(heads):

            def backward(part, _, h=h):
                here = 2 * b + part
                at = pl.ds(pl.multiple_of(here * qry, 16), qry)
                back_mix = r.back_mix[at, :]
                mine = back_mix * head_rows[h].astype(HALF)
                lean = jnp.sum(
                    mine.astype(FLOAT) * r.mixed[at, :], axis=-1, keepdims=True
                )
                weights = r.weights[h, at, :]
                back_weights = dot(mine, r.values_t[...])
                back_scores = (weights.astype(FLOAT) * (back_weights - lean)).astype(HALF)
                queries_back = dot(back_scores, r.keys[...]) * (head_rows[h] * HD**-0.5)
                if h == 0:
                    r.queries_back[at, :] = queries_back
                else:
                    r.queries_back[at, :] += queries_back
                lanes = pl.ds(h * HD, HD)
                r.values_back[lanes, :] += dot(r.back_mix_t[here, lanes, :], weights)
                r.keys_back[lanes, :] += dot(r.queries_t[here, lanes, :], back_scores)
                return 0

            lax.fori_loop(0, 2, backward, 0)
            pump()

    first = hidden + width
    pieces = [
        lambda: dot(r.mix_all[me].reshape(total_qry, inner), r.slope[...], (0, 0)),
        lambda: dot(r.queries_back[...].astype(HALF), r.normed_qry[...], (0, 0)),
        lambda: dot((r.keys_back[...] * HD**-0.5).astype(HALF), r.normed_ctx[...]),
        lambda: dot(r.values_back[...].astype(HALF), r.normed_ctx[...]),
    ]
    for place, piece in enumerate(pieces):
        r.main_work[pl.ds(first + place * inner, inner), :] = piece().astype(HALF)
        while (len(mains) + 1) * CHUNK <= first + (place + 1) * inner:
            send_chunk(len(mains))
        pump()

    over_gain = 1.0 / gain_one
    low_bins, low_embed, low_gains = (SMALL[name][0] for name in ("bins", "embed", "gains"))
    features = r.w_embed.shape[0]
    r.small[pl.ds(BINS, SMALL_ROWS - BINS), :] = jnp.zeros((SMALL_ROWS - BINS, width), FLOAT)
    bins_at = pl.ds(low_bins, BINS)
    embed_at = pl.ds(low_embed, features)

    def embed_back(upstream, normed, scale):
        unit = normed.astype(FLOAT) * over_gain
        return column_sums(upstream * unit), standard_back(upstream, gain_one, unit, scale)

    def context_back(place, gain_sum):
        slot, offset = lax.div(place, ctx // 256), lax.rem(place, ctx // 256)
        at = pl.ds(pl.multiple_of(place * 256, 256), 256)
        keys = (r.keys_back[:, at] * HD**-0.5).T.astype(HALF)
        values = r.values_back[:, at].T.astype(HALF)
        upstream = dot(keys, r.w_qkv[1]) + dot(values, r.w_qkv[2])
        gains, back_zero = embed_back(upstream, r.normed_ctx[at, :], as_column(r.scale_ctx[pl.ds(place, 1), :]))
        back_zero = back_zero.astype(HALF)
        feat = r.feat[slot, pl.ds(pl.multiple_of(offset * 256, 256), 256), :]
        r.small[embed_at, :] += dot(feat, back_zero, (0, 0))
        r.small[bins_at, :] += dot(one_hot(slot, offset), back_zero)
        return gain_sum + gains

    gain_sum_one = jnp.zeros((1, width), FLOAT)
    pieces = total_ctx // 256
    for part in range(2):
        gain_sum_one = lax.fori_loop(
            part * pieces // 2, (part + 1) * pieces // 2, context_back, gain_sum_one
        )
        pump()

    def query_back(slot, gain_sum):
        at = pl.ds(pl.multiple_of(slot * qry, 16), qry)
        upstream = dot(r.queries_back[at, :].astype(HALF), r.w_qkv[0])
        gains, back_zero = embed_back(upstream, r.normed_qry[at, :], as_column(r.scale_qry[pl.ds(slot, 1), :]))
        mine = jnp.where(slot == me, 1.0, 0.0)
        back_zero = (back_zero + mine * r.back[at, :]).astype(HALF)
        feat = r.feat[slot, pl.ds(ctx, qry), :]
        r.small[embed_at, :] += dot(feat, back_zero, (0, 0))
        return gain_sum + gains

    gain_sum_one = lax.fori_loop(0, groups, query_back, gain_sum_one)
    r.small[pl.ds(low_gains, 1), :] = gain_sum_one
    r.small[pl.ds(low_gains + 1, 1), :] = gain_sum_two / groups
    r.small[pl.ds(low_gains + 2, 1), :] = gain_sum_last / groups
    r.small_work[...] = r.small[...].astype(HALF)

    small_steps = stages_of(SMALL_ROWS, over_heads + over_tables, 64)
    smalls = Sum(copies, wide, r.small_work, r.small_out, 0, small_steps, places)
    smalls.start()
    waiting = len(over_heads)
    while not all(part.done() for part in mains) or smalls.at < len(small_steps) - waiting:
        pump()
        if smalls.at < len(small_steps) - waiting:
            smalls.advance()
    while not losses.done():
        losses.advance()
    squares = one_value(sum_squares(r.main, r.main.shape[0]))
    r.square_work[...] = jnp.broadcast_to(squares, (16, 128))
    square_steps = stages_of(16, list(reversed(over_heads)), 16)
    squared = Sum(copies, tiny, r.square_work, r.square, 0, square_steps, places)
    while not (squared.done() and smalls.done()):
        smalls.advance()
        squared.advance()
    squares = r.square[0:8, :] + one_value(sum_squares(r.small_out, SMALL_ROWS))
    row = lax.broadcasted_iota(jnp.int32, (8, 128), 0)
    r.stats[...] = jnp.where(row == 0, squares, jnp.where(row == 1, r.loss[0:8, :], r.count[0:8, :]))


def train(sizes, inputs):
    shape = Named()
    shape.groups = sizes["heads"]
    shape.ctx, features = inputs["ctx_feat"].shape
    shape.qry = inputs["qry_feat"].shape[0]
    shape.width = inputs["w_embed"].shape[1]
    shape.inner = inputs["w_out"].shape[0]
    shape.hidden = inputs["w_up"].shape[1]
    shape.over_tables = [("tables", bit) for bit in bits_of(sizes["tables"])]
    shape.over_heads = [("heads", bit) for bit in bits_of(sizes["heads"])]
    groups, ctx, qry, width, inner, hidden = (
        shape.groups,
        shape.ctx,
        shape.qry,
        shape.width,
        shape.inner,
        shape.hidden,
    )
    total_ctx, total_qry = groups * ctx, groups * qry
    heads = inner // HD
    main_rows = hidden + width + 4 * inner
    block = 2 * qry
    main_steps = stages_of(CHUNK, shape.over_tables, 16)
    small_steps = stages_of(SMALL_ROWS, shape.over_heads + shape.over_tables, 64)
    sum_steps = stages_of(2 * block, shape.over_heads, block)
    wide_rows = main_rows // CHUNK * landing_rows(main_steps) + landing_rows(small_steps)
    narrow_rows = 2 * (total_qry // block) * landing_rows(sum_steps)
    every = len(shape.over_tables) + len(shape.over_heads)
    tiny_rows = 16 * (2 * every + len(shape.over_heads))
    tiny = ((16, 128), FLOAT)
    scratch = {
        "feat": ((groups, ctx + qry, features), HALF),
        "ints": ((groups, 8, ctx), jnp.int32),
        "out_all": ((groups, inner, width), HALF),
        "count_work": tiny,
        "count": tiny,
        "loss_work": tiny,
        "loss": tiny,
        "square_work": tiny,
        "square": tiny,
        "normed_ctx": ((total_ctx, width), HALF),
        "scale_ctx": ((total_ctx // 256, 256), FLOAT),
        "normed_qry": ((total_qry, width), HALF),
        "scale_qry": ((groups, qry), FLOAT),
        "stream": ((total_qry, width), FLOAT),
        "queries": ((total_qry, inner), HALF),
        "queries_t": ((groups, inner, qry), HALF),
        "keys": ((total_ctx, inner), HALF),
        "values": ((total_ctx, inner), HALF),
        "keys_t": ((inner, total_ctx), HALF),
        "values_t": ((inner, total_ctx), HALF),
        "weights": ((heads, total_qry, total_ctx), HALF),
        "mixed": ((total_qry, inner), FLOAT),
        "mix_all": ((groups, groups, qry, inner), HALF),
        "normed_two": ((total_qry, width), HALF),
        "active": ((total_qry, hidden), HALF),
        "slope": ((total_qry, hidden), HALF),
        "down_work": ((2 * total_qry, width // 2), HALF),
        "down_sum": ((2 * total_qry, width // 2), HALF),
        "back": ((total_qry, width), FLOAT),
        "back_mlp": ((total_qry, width), HALF),
        "back_up": ((total_qry, hidden), HALF),
        "back_mix": ((total_qry, inner), HALF),
        "back_mix_t": ((groups, inner, qry), HALF),
        "queries_back": ((total_qry, inner), FLOAT),
        "keys_back": ((inner, total_ctx), FLOAT),
        "values_back": ((inner, total_ctx), FLOAT),
        "main_work": ((main_rows, width), HALF),
        "small": ((SMALL_ROWS, width), FLOAT),
        "small_work": ((SMALL_ROWS, width), HALF),
        "wide_land": ((wide_rows, width), HALF),
        "narrow_land": ((narrow_rows, width // 2), HALF),
        "tiny_land": ((tiny_rows, 128), FLOAT),
    }
    outputs = {
        "main": jax.ShapeDtypeStruct((main_rows, width), HALF),
        "small_out": jax.ShapeDtypeStruct((SMALL_ROWS, width), HALF),
        "stats": jax.ShapeDtypeStruct((8, 128), FLOAT),
    }
    names = list(inputs) + list(outputs) + list(scratch) + ["sends", "recvs"]

    def kernel(*refs):
        named = Named()
        named.__dict__.update(zip(names, refs))
        train_kernel(shape, named)

    whole = pl.BlockSpec(memory_space=pltpu.VMEM)
    semaphores = pltpu.SemaphoreType.DMA((160,))
    return pl.pallas_call(
        kernel,
        out_shape=tuple(outputs.values()),
        in_specs=[
            pl.BlockSpec(memory_space=pltpu.SMEM) if name == "counts" else whole for name in inputs
        ],
        out_specs=(whole,) * 3,
        scratch_shapes=[pltpu.VMEM(size, kind) for size, kind in scratch.values()]
        + [semaphores, semaphores],
        compiler_params=pltpu.CompilerParams(
            collective_id=1, has_side_effects=True, vmem_limit_bytes=60 * 2**20
        ),
        name="train",
    )(*inputs.values())


def adam_kernel(refs):
    (stats, main_d, main_u, main_o, main_q, main_k, main_v, small) = refs[:8]
    w = refs[8:16]
    m = refs[16:24]
    v = refs[24:32]
    w_new = refs[32:40]
    m_new = refs[40:48]
    v_new = refs[48:56]
    norm_ref = refs[56]
    norm = jnp.sqrt(stats[0:1, 0:1])
    norm_ref[...] = jnp.broadcast_to(norm, norm_ref.shape)
    factor = jnp.minimum(1.0, CLIP_NORM / (norm + 1e-06))

    def update(which, gradient, rate, decay, at=...):
        gradient = gradient.astype(FLOAT) * factor
        results = adam_update(w[which][at], m[which][at], v[which][at], gradient, rate, decay)
        for target, value in zip((w_new, m_new, v_new), results):
            target[which][at] = value

    update(6, main_d[...], RATE, DECAY)
    update(5, main_u[...], RATE, DECAY)
    update(4, main_o[...], RATE_WIDE, DECAY)
    for part, gradient in enumerate((main_q, main_k, main_v)):
        update(3, gradient[...], RATE, DECAY, at=part)

    @pl.when(pl.program_id(0) == 0)
    def _():
        def rows(name, count):
            low, size = SMALL[name]
            return small[low : low + size, :].astype(FLOAT)[:count]

        update(0, rows("embed", w[0].shape[0]), RATE, DECAY)
        update(1, rows("bins", w[1].shape[0]), RATE_WIDE, DECAY)
        update(2, rows("gains", w[2].shape[0]), RATE_WIDE, 0.0)
        update(7, rows("head", w[7].shape[0]), RATE, DECAY)


def adam_all(stats, main, small, weights, firsts, seconds):
    inner, width = weights[4].shape
    hidden = weights[5].shape[1]
    steps = 6

    def fixed(array):
        return pl.BlockSpec(array.shape, lambda step: (0,) * array.ndim)

    def rows_of(rows, low=0):
        size = rows // steps
        return pl.BlockSpec((size, width), lambda step: (low // size + step, 0))

    blocks = [
        fixed(weights[0]),
        fixed(weights[1]),
        fixed(weights[2]),
        pl.BlockSpec((3, inner // steps, width), lambda step: (0, step, 0)),
        rows_of(inner),
        pl.BlockSpec((width // steps, hidden), lambda step: (step, 0)),
        rows_of(hidden),
        fixed(weights[7]),
    ]
    first = hidden + width
    shapes = [jax.ShapeDtypeStruct(weight.shape, FLOAT) for weight in weights]
    return pl.pallas_call(
        lambda *refs: adam_kernel(refs),
        grid=(steps,),
        in_specs=[fixed(stats), rows_of(hidden), rows_of(width, hidden)]
        + [rows_of(inner, first + part * inner) for part in range(4)]
        + [fixed(small)]
        + blocks * 3,
        out_specs=blocks * 3 + [fixed(stats)],
        out_shape=shapes * 3 + [jax.ShapeDtypeStruct(stats.shape, FLOAT)],
        compiler_params=pltpu.CompilerParams(vmem_limit_bytes=48 * 2**20),
        name="adam",
    )(stats, *[main] * 6, small, *weights, *firsts, *seconds)


def shards(
    ctx_feat,
    qry_feat,
    counts,
    ctx_bins,
    qry_bins,
    query_mask,
    w_embed,
    w_bins,
    norm_gains,
    w_qkv,
    w_out,
    w_up,
    w_down,
    w_head,
    m_embed,
    m_bins,
    m_gains,
    m_qkv,
    m_out,
    m_up,
    m_down,
    m_head,
    v_embed,
    v_bins,
    v_gains,
    v_qkv,
    v_out,
    v_up,
    v_down,
    v_head,
):
    sizes = {"tables": lax.axis_size("tables"), "heads": lax.axis_size("heads")}
    main, small, stats = train(
        sizes,
        {
            "counts": counts,
            "ctx_feat": ctx_feat[0],
            "qry_feat": qry_feat[0],
            "ctx_bins": ctx_bins,
            "qry_bins": qry_bins,
            "query_mask": query_mask,
            "w_embed": w_embed,
            "w_bins": w_bins,
            "gains": norm_gains,
            "w_qkv": jnp.swapaxes(w_qkv, 1, 2).astype(HALF),
            "w_out": w_out.astype(HALF),
            "w_up": w_up.astype(HALF),
            "w_down": w_down.astype(HALF),
            "w_head": w_head.T,
        },
    )
    results = adam_all(
        stats,
        main,
        small,
        *(
            (embed, bins, gains, jnp.swapaxes(qkv, 1, 2), out, up, down, head.T)
            for embed, bins, gains, qkv, out, up, down, head in (
                (w_embed, w_bins, norm_gains, w_qkv, w_out, w_up, w_down, w_head),
                (m_embed, m_bins, m_gains, m_qkv, m_out, m_up, m_down, m_head),
                (v_embed, v_bins, v_gains, v_qkv, v_out, v_up, v_down, v_head),
            )
        ),
    )
    *updated, norm = results
    for low in range(0, 24, 8):
        updated[low + 3] = jnp.swapaxes(updated[low + 3], 1, 2)
        updated[low + 7] = updated[low + 7].T
    return (*updated, stats[1, 0], stats[2, 0], norm[0, 0])


def solution(mesh):
    in_specs = (
        P("tables", "heads", None),
        P("tables", "heads", None),
        P("tables"),
        P("tables", "heads"),
        P("tables", "heads"),
        P("tables", "heads"),
        P(),
        P(),
        P(),
        P(None, None, "heads"),
        P("heads", None),
        P(None, "heads"),
        P("heads", None),
        P(),
        P(),
        P(),
        P(),
        P(None, None, "heads"),
        P("heads", None),
        P(None, "heads"),
        P("heads", None),
        P(),
        P(),
        P(),
        P(),
        P(None, None, "heads"),
        P("heads", None),
        P(None, "heads"),
        P("heads", None),
        P(),
    )
    out_specs = (
        P(),
        P(),
        P(),
        P(None, None, "heads"),
        P("heads", None),
        P(None, "heads"),
        P("heads", None),
        P(),
        P(),
        P(),
        P(),
        P(None, None, "heads"),
        P("heads", None),
        P(None, "heads"),
        P("heads", None),
        P(),
        P(),
        P(),
        P(),
        P(None, None, "heads"),
        P("heads", None),
        P(None, "heads"),
        P("heads", None),
        P(),
        P(),
        P(),
        P(),
    )
    return jax.shard_map(shards, mesh=mesh, in_specs=in_specs, out_specs=out_specs, check_vma=False)
```

```python
import jax
import jax.numpy as jnp
from jax import lax
from jax.experimental import pallas as pl
from jax.experimental.pallas import tpu as pltpu
from jax.sharding import PartitionSpec as P

HD = 64
BINS = 64
STEP = 10


NORM_EPS = 1e-05
ADAM_EPS = 1e-08
RATE = 0.05
RATE_WIDE = 1.0
BETA_ONE = 0.9
BETA_TWO = 0.95
DECAY = 0.1
CLIP_NORM = 0.02
MASKED = -1e30
FLOAT = jnp.float32
HALF = jnp.bfloat16
MESH = pl.DeviceIdType.MESH


def adam_update(weight, moment_one, moment_two, gradient, rate, decay_rate):
    moment_one = BETA_ONE * moment_one + (1.0 - BETA_ONE) * gradient
    moment_two = BETA_TWO * moment_two + (1.0 - BETA_TWO) * gradient * gradient
    first_hat = moment_one / (1.0 - BETA_ONE**STEP)
    second_hat = moment_two / (1.0 - BETA_TWO**STEP)
    root = second_hat * lax.rsqrt(second_hat) + ADAM_EPS
    inverse = pl.reciprocal(root, approx=True)
    inverse = inverse * (2.0 - root * inverse)
    weight = weight - rate * (first_hat * inverse + decay_rate * weight)
    return (weight, moment_one, moment_two)


def place_bit(place, bit):
    return lax.rem(lax.div(place, bit), 2)


def flip(place, bit):
    return place + bit - 2 * bit * place_bit(place, bit)


def bits_of(size):
    return [1 << power for power in range(size.bit_length() - 1)]


def partner(places, axis, bit):
    other = dict(places)
    other[axis] = flip(places[axis], bit)
    return (other["tables"], other["heads"])


def greet(places, axes):
    barrier = pltpu.get_barrier_semaphore()
    for axis, bit in axes:
        pl.semaphore_signal(
            barrier, inc=1, device_id=partner(places, axis, bit), device_id_type=MESH
        )
    pl.semaphore_wait(barrier, len(axes))


class Copies:
    def __init__(self, sends, recvs):
        self.sends, self.recvs, self.used = sends, recvs, 0

    def start(self, source, target, device):
        self.used += 1
        copy = pltpu.make_async_remote_copy(
            src_ref=source,
            dst_ref=target,
            send_sem=self.sends.at[self.used - 1],
            recv_sem=self.recvs.at[self.used - 1],
            device_id=device,
            device_id_type=MESH,
        )
        copy.start()
        return copy


class Landing:
    def __init__(self, rows_ref):
        self.rows_ref, self.used = rows_ref, 0

    def take(self, rows):
        self.used += rows
        return self.rows_ref.at[pl.ds(self.used - rows, rows), :]


class Traffic:
    LATENCY = 2.0

    def __init__(self):
        self.now, self.free, self.flows = 0.0, {}, []

    def book(self, axis, bit, size):
        link, hops = ("core", 0.15) if (axis, bit) == ("heads", 1) else (axis + str(min(bit, 2)), 1)
        if axis == "tables" and bit > 2:
            hops = bit // 2
        self.free[link] = max(self.now, self.free.get(link, 0.0)) + hops * size * 2 / 1e5
        return self.free[link] + self.LATENCY * min(hops + 0.4, 1)

    def add(self, flow):
        self.flows.append(flow)
        flow.start()

    def waiting(self):
        return [flow for flow in self.flows if flow.sent]

    def step(self):
        flow = min(self.waiting(), key=lambda flow: flow.ready)
        self.now = max(self.now, flow.ready) + 0.3
        flow.advance()

    def spend(self, time):
        self.now += time
        while any(flow.ready <= self.now for flow in self.waiting()):
            self.step()

    def wait(self, *flows):
        while not all(flow.done() for flow in flows):
            self.step()


def stages_of(rows, axes, least):
    steps = []
    for axis, bit in axes:
        if rows // 2 >= least and rows % 32 == 0:
            rows //= 2
            steps.append((axis, bit, "halve", rows))
        else:
            steps.append((axis, bit, "whole", rows))
    back = [(axis, bit, "back", left) for axis, bit, kind, left in reversed(steps) if kind == "halve"]
    return steps + back


def landing_rows(steps):
    return sum(left for _, _, kind, left in steps if kind != "back")


class Sum:
    def __init__(self, copies, traffic, landing, buffer, result, start, steps, places, until=None):
        self.copies, self.traffic, self.landing = copies, traffic, landing
        self.buffer, self.result, self.low = buffer, result, start
        self.steps, self.places = steps, places
        self.until = len(steps) if until is None else until
        self.at, self.sent, self.landed, self.ready = 0, None, None, 0.0

    def rows(self, low, count):
        if isinstance(low, int):
            return pl.ds(low, count)
        return pl.ds(pl.multiple_of(low, 16), count)

    def finish(self):
        if self.sent is None:
            return
        _, _, kind, count = self.steps[self.at - 1]
        self.sent.wait()
        self.sent = None
        if kind != "back":
            mine = self.rows(self.low, count)
            total = self.buffer[mine, :].astype(FLOAT) + self.landed[...].astype(FLOAT)
            last = self.at == len(self.steps) or self.steps[self.at][2] == "back"
            target = self.result if last else self.buffer
            target[mine, :] = total.astype(self.buffer.dtype)

    def start(self):
        if self.at >= self.until:
            return
        axis, bit, kind, count = self.steps[self.at]
        self.at += 1
        side = place_bit(self.places[axis], bit)
        if kind == "halve":
            source = self.buffer.at[self.rows(self.low + count * (1 - side), count), :]
            self.low = self.low + count * side
            target = self.landed = self.landing.take(count)
        elif kind == "whole":
            source = self.buffer.at[self.rows(self.low, count), :]
            target = self.landed = self.landing.take(count)
        else:
            source = target = self.result.at[self.rows(self.low, count), :]
            self.low = self.low - count * side
        self.sent = self.copies.start(source, target, partner(self.places, axis, bit))
        self.ready = self.traffic.book(axis, bit, count * self.buffer.shape[-1] * 2)

    def advance(self):
        self.finish()
        self.start()

    def go_on(self):
        self.until = len(self.steps)
        self.start()

    def done(self):
        return self.at >= self.until and self.sent is None


class Gather:
    def __init__(self, copies, traffic, views, size, places, bits):
        self.copies, self.traffic, self.views, self.size = copies, traffic, views, size
        self.places, self.bits = places, bits
        self.at, self.held, self.sent, self.ready = 0, [places["heads"]], [], 0.0

    def advance(self):
        self.finish()
        self.start()

    def finish(self):
        for copy in self.sent:
            copy.wait()
        if self.sent:
            self.held = self.held + [flip(slot, self.bits[self.at - 1]) for slot in self.held]
        self.sent = []

    def start(self):
        if self.at < len(self.bits):
            bit = self.bits[self.at]
            other = partner(self.places, "heads", bit)
            self.sent = [
                self.copies.start(view(slot), view(slot), other)
                for slot in self.held
                for view in self.views
            ]
            self.ready = self.traffic.book("heads", bit, self.size * len(self.held))
            self.at += 1

    def done(self):
        return self.at >= len(self.bits) and not self.sent


def places_here():
    return {"tables": lax.axis_index("tables"), "heads": lax.axis_index("heads")}


SMALL = {"head": (0, 64), "bins": (64, 64), "embed": (128, 112), "gains": (240, 16)}
SMALL_ROWS = 256
CHUNK = 256


def dot(left, right, over=(1, 0)):
    return lax.dot_general(
        left, right, (((over[0],), (over[1],)), ((), ())), preferred_element_type=FLOAT
    )


def standard(rows):
    center = rows - jnp.mean(rows, axis=-1, keepdims=True)
    scale = lax.rsqrt(jnp.mean(center * center, axis=-1, keepdims=True) + NORM_EPS)
    return center * scale, scale


def standard_back(upstream, gain_row, unit, scale):
    inner = upstream * gain_row
    lean = jnp.mean(inner, axis=-1, keepdims=True)
    tilt = jnp.mean(inner * unit, axis=-1, keepdims=True)
    return (inner - lean - unit * tilt) * scale


def as_row(column):
    return jnp.broadcast_to(column, (column.shape[0], 128)).T[:1]


def as_column(row):
    return jnp.broadcast_to(row, (8, row.shape[1])).T[:, :1]


def column_sums(rows):
    return jnp.sum(rows, axis=0, keepdims=True)


def gelu_both(hidden):
    root = 0.7978845608028654
    square = hidden * hidden
    bent = jnp.tanh(root * hidden * (1.0 + 0.044715 * square))
    half = 0.5 * (1.0 + bent)
    slope = half + 0.5 * hidden * (1.0 - bent * bent) * root * (1.0 + 0.134145 * square)
    return hidden * half, slope


def sum_squares(rows_ref, count):
    def piece(step, total):
        part = rows_ref[pl.ds(pl.multiple_of(step * 64, 64), 64), :].astype(FLOAT)
        return total + jnp.sum((part * part).reshape(8, 8, part.shape[1]), axis=0)

    return lax.fori_loop(0, count // 64, piece, jnp.zeros((8, rows_ref.shape[1]), FLOAT))


def one_value(total):
    return jnp.sum(jnp.sum(total, axis=0, keepdims=True), axis=1, keepdims=True)


class Named:
    pass


def train_kernel(shape, r):
    groups, ctx, qry, width, inner, hidden = (
        shape.groups,
        shape.ctx,
        shape.qry,
        shape.width,
        shape.inner,
        shape.hidden,
    )
    heads = inner // HD
    total_ctx, total_qry = groups * ctx, groups * qry
    block = 2 * qry
    blocks = total_qry // block
    half = width // 2
    places = places_here()
    me = places["heads"]
    copies = Copies(r.sends, r.recvs)
    traffic = Traffic()
    over_heads, over_tables = shape.over_heads, shape.over_tables
    far_first = [bit for _, bit in reversed(over_heads)]
    tiny = Landing(r.tiny_land)
    wide = Landing(r.wide_land)
    narrow = Landing(r.narrow_land)
    def stage(number, source, target):
        copy = pltpu.make_async_copy(source, target, r.locals.at[number])
        copy.start()
        return copy

    low = 3 * inner
    loads = [
        stage(part, r.w_qkv_wide.at[part], r.back.at[pl.ds(part * inner, inner), :])
        for part in range(3)
    ]
    loads.append(stage(3, r.w_out_wide, r.small.at[pl.ds(0, inner), :]))

    def load_halves(number, source):
        rest = source.shape[0] - low
        return [
            stage(number, source.at[pl.ds(0, low), :], r.back.at[pl.ds(0, low), :]),
            stage(number + 1, source.at[pl.ds(low, rest), :], r.small.at[pl.ds(0, rest), :]),
        ]

    def take_halves(copies_in, target):
        rest = target.shape[0] - low
        for copy in copies_in:
            copy.wait()
        target[pl.ds(0, low), :] = r.back[pl.ds(0, low), :].astype(HALF)
        target[pl.ds(low, rest), :] = r.small[pl.ds(0, rest), :].astype(HALF)

    greet(places, over_heads + over_tables)

    r.feat[me, pl.ds(0, ctx), :] = r.ctx_feat[...].astype(FLOAT).T.astype(HALF)
    r.feat[me, pl.ds(ctx, qry), :] = r.qry_feat[...]
    r.ints[me] = jnp.zeros((8, ctx), jnp.int32)
    r.ints[me, 0:1, :] = r.ctx_bins[...]
    r.ints[me, 1:2, pl.ds(0, qry)] = r.qry_bins[...]
    r.ints[me, 2:3, pl.ds(0, qry)] = r.query_mask[...]
    rows_in = Gather(
        copies,
        traffic,
        [lambda slot: r.feat.at[slot], lambda slot: r.ints.at[slot]],
        (ctx + qry) * 256 + ctx * 32,
        places,
        far_first,
    )
    traffic.add(rows_in)
    mask_sum = jnp.sum(r.query_mask[...].astype(FLOAT), axis=1, keepdims=True)
    r.count_work[...] = jnp.broadcast_to(mask_sum, (16, 128))
    tiny_steps = stages_of(16, over_heads + over_tables, 16)
    counted = Sum(copies, traffic, tiny, r.count_work, r.count, 0, tiny_steps, places)
    traffic.add(counted)
    for copy in loads:
        copy.wait()
    for part in range(3):
        r.w_qkv[part] = r.back[pl.ds(part * inner, inner), :].astype(HALF)
    r.out_all[me] = r.small[pl.ds(0, inner), :].astype(HALF)
    loads = load_halves(4, r.w_up_wide)
    outs_in = Gather(
        copies, traffic, [lambda slot: r.out_all.at[slot]], inner * width * 2, places, far_first
    )

    embed_half = r.w_embed[...].astype(HALF)
    bins_half = r.w_bins[...].astype(HALF)
    gain_one, gain_two, gain_last = (r.gains[row : row + 1, :] for row in range(3))
    bin_rows = lax.broadcasted_iota(jnp.int32, (BINS, 256), 0)

    def one_hot(slot, place):
        return jnp.where(
            bin_rows == r.ints[slot, 0:1, pl.ds(pl.multiple_of(place * 256, 256), 256)], 1.0, 0.0
        ).astype(HALF)

    def embed_shard(slot):
        def context(place, _):
            at = pl.multiple_of(slot * ctx + place * 256, 256)
            feat = r.feat[slot, pl.ds(pl.multiple_of(place * 256, 256), 256), :]
            zero = dot(feat, embed_half) + dot(one_hot(slot, place), bins_half, (0, 0))
            unit, scale = standard(zero)
            normed = (unit * gain_one).astype(HALF)
            r.normed_ctx[pl.ds(at, 256), :] = normed
            r.scale_ctx[pl.ds(slot * (ctx // 256) + place, 1), :] = as_row(scale)
            keys = dot(normed, r.w_qkv[1], (1, 1))
            values = dot(normed, r.w_qkv[2], (1, 1))
            r.keys[pl.ds(at, 256), :] = keys.astype(HALF)
            r.values[pl.ds(at, 256), :] = values.astype(HALF)
            r.keys_t[:, pl.ds(at, 256)] = keys.T.astype(HALF)
            r.values_t[:, pl.ds(at, 256)] = values.T.astype(HALF)
            return 0

        lax.fori_loop(0, ctx // 256, context, 0)
        at = pl.multiple_of(slot * qry, 16)
        zero = dot(r.feat[slot, pl.ds(ctx, qry), :], embed_half)
        r.stream[pl.ds(at, qry), :] = zero
        unit, scale = standard(zero)
        normed = (unit * gain_one).astype(HALF)
        r.normed_qry[pl.ds(at, qry), :] = normed
        r.scale_qry[pl.ds(slot, 1), :] = as_row(scale)
        queries = dot(normed, r.w_qkv[0], (1, 1))
        r.queries[pl.ds(at, qry), :] = queries.astype(HALF)
        r.queries_t[slot] = queries.T.astype(HALF)

    done = 0
    while done < groups:
        for slot in rows_in.held[done:]:
            embed_shard(slot)
            done += 1
            traffic.spend(2.0)
            if done == 1:
                traffic.add(outs_in)
                take_halves(loads, r.w_up)
                loads = load_halves(6, r.w_down_wide)
            if done == 2:
                take_halves(loads, r.w_down)
        if done == len(rows_in.held) and done < groups:
            traffic.step()

    lane = lax.broadcasted_iota(jnp.int32, (1, inner), 1)
    head_rows = [
        jnp.where((lane >= h * HD) & (lane < (h + 1) * HD), 1.0, 0.0).astype(FLOAT)
        for h in range(heads)
    ]
    slots_at = lax.broadcasted_iota(jnp.int32, (1, total_ctx), 1)
    dead = jnp.where(slots_at < r.counts[0:1, 0:1], 0.0, MASKED)
    mixing = []
    for b in range(groups):
        rows = pl.ds(b * qry, qry)
        query_blk = r.queries[rows, :]
        mixed = jnp.zeros((qry, inner), FLOAT)
        for h in range(heads):
            raw = dot(query_blk * (head_rows[h] * HD**-0.5).astype(HALF), r.keys_t[...]) + dead
            raised = jnp.exp(raw - jnp.max(raw, axis=-1, keepdims=True))
            weights = (raised * (1.0 / jnp.sum(raised, axis=-1, keepdims=True))).astype(HALF)
            r.weights[h, rows, :] = weights
            mixed = mixed + dot(weights, r.values[...]) * head_rows[h]
        r.mixed[rows, :] = mixed
        r.mix_all[me, b] = mixed.astype(HALF)
        mixing.append(
            Gather(
                copies,
                traffic,
                [lambda slot, b=b: r.mix_all.at[slot, b]],
                qry * 512,
                places,
                far_first,
            )
        )
        traffic.add(mixing[-1])
        traffic.spend(2.0)

    sum_steps = stages_of(2 * block, over_heads, block)
    down_sums, back_sums = [], []
    for b in range(blocks):
        traffic.wait(outs_in, *mixing[2 * b : 2 * b + 2])
        rows = pl.ds(b * block, block)
        attended = []
        for part in range(2 * b, 2 * b + 2):
            total = dot(r.mix_all[0, part], r.out_all[0])
            for slot in range(1, groups):
                total = total + dot(r.mix_all[slot, part], r.out_all[slot])
            attended.append(total)
        stream = r.stream[rows, :] + jnp.concatenate(attended, axis=0)
        r.stream[rows, :] = stream
        unit, _ = standard(stream)
        normed = (unit * gain_two).astype(HALF)
        r.normed_two[rows, :] = normed
        active, slope = gelu_both(dot(normed, r.w_up[...]))
        active = active.astype(HALF)
        r.active[rows, :] = active
        r.slope[rows, :] = slope.astype(HALF)
        low = pl.ds(2 * b * block, block)
        high = pl.ds((2 * b + 1) * block, block)
        part = dot(active, r.w_down[...]).astype(HALF)
        r.down_work[low, :] = part[:, :half]
        r.down_work[high, :] = part[:, half:]
        down_sums.append(
            Sum(copies, traffic, narrow, r.down_work, r.down_sum, 2 * b * block, sum_steps, places)
        )
        traffic.add(down_sums[-1])
        traffic.spend(2.0)

    head_half = r.w_head[...].astype(HALF)
    traffic.wait(counted)
    divisor = jnp.maximum(r.count[0:1, 0:1], 1.0)
    tall = lax.broadcasted_iota(jnp.int32, (BINS, 256), 0)
    loss = jnp.zeros((1, 1), FLOAT)
    grad_head = jnp.zeros((BINS, width), FLOAT)
    gain_sum_last = jnp.zeros((1, width), FLOAT)
    for b in range(blocks):
        traffic.wait(counted, down_sums[b])
        rows = pl.ds(b * block, block)
        low = pl.ds(2 * b * block, block)
        high = pl.ds((2 * b + 1) * block, block)
        mlp = jnp.concatenate([r.down_sum[low, :], r.down_sum[high, :]], axis=1)
        unit, scale = standard(r.stream[rows, :] + mlp.astype(FLOAT))
        normed = (unit * gain_last).astype(HALF)
        logits = dot(normed, head_half, (1, 1))
        targets, masks = [], []
        for slot in range(2 * b, 2 * b + 2):
            target = jnp.where(tall == r.ints[slot, 1:2, 0:256], 1.0, 0.0)
            targets.append(target.T[:qry])
            mask = jnp.broadcast_to(r.ints[slot, 2:3, 0:256].astype(FLOAT), (8, 256))
            masks.append(mask.T[:qry, :1])
        target = jnp.concatenate(targets, axis=0)
        mask = jnp.concatenate(masks, axis=0)
        top = jnp.max(logits, axis=-1, keepdims=True)
        log_bins = top + jnp.log(jnp.sum(jnp.exp(logits - top), axis=-1, keepdims=True))
        missed = log_bins - jnp.sum(target * logits, axis=-1, keepdims=True)
        loss = loss + jnp.sum(mask * missed, axis=0, keepdims=True)
        back_logits = (mask * (jnp.exp(logits - log_bins) - target) / divisor).astype(HALF)
        grad_head = grad_head + dot(back_logits, normed, (0, 0))
        back_final = dot(back_logits, head_half)
        gain_sum_last = gain_sum_last + column_sums(back_final * unit)
        back_two = standard_back(back_final, gain_last, unit, scale)
        r.back[rows, :] = back_two
        back_mlp = back_two.astype(HALF)
        r.back_mlp[rows, :] = back_mlp
        back_active = dot(back_mlp, r.w_down[...], (1, 1))
        back_up = (r.slope[rows, :].astype(FLOAT) * back_active).astype(HALF)
        r.back_up[rows, :] = back_up
        part = dot(back_up, r.w_up[...], (1, 1)).astype(HALF)
        r.down_work[low, :] = part[:, :half]
        r.down_work[high, :] = part[:, half:]
        back_sums.append(
            Sum(copies, traffic, narrow, r.down_work, r.down_sum, 2 * b * block, sum_steps, places)
        )
        traffic.add(back_sums[-1])
        traffic.spend(3.0)
    r.loss_work[...] = jnp.broadcast_to(loss / groups, (16, 128))
    losses = Sum(copies, traffic, tiny, r.loss_work, r.loss, 0, tiny_steps, places)
    traffic.add(losses)
    r.small[pl.ds(0, BINS), :] = grad_head / groups

    main_steps = stages_of(CHUNK, over_tables, 16)
    mains = []

    def send_chunk(place):
        start = CHUNK * place
        part = Sum(copies, traffic, wide, r.main_work, r.main, start, main_steps, places)
        mains.append(part)
        traffic.add(part)
        traffic.spend(0.5)

    for place in range(hidden // CHUNK):
        at = pl.ds(place * CHUNK, CHUNK)
        r.main_work[at, :] = dot(r.active[:, at], r.back_mlp[...], (0, 0)).astype(HALF)
        send_chunk(len(mains))
    for place in range(width // CHUNK):
        at = pl.ds(place * CHUNK, CHUNK)
        to = pl.ds(hidden + place * CHUNK, CHUNK)
        r.main_work[to, :] = dot(r.normed_two[:, at], r.back_up[...], (0, 0)).astype(HALF)
        send_chunk(len(mains))

    gain_sum_two = jnp.zeros((1, width), FLOAT)
    r.keys_back[...] = jnp.zeros(r.keys_back.shape, FLOAT)
    r.values_back[...] = jnp.zeros(r.values_back.shape, FLOAT)
    for b in range(blocks):
        traffic.wait(back_sums[b])
        rows = pl.ds(b * block, block)
        low = pl.ds(2 * b * block, block)
        high = pl.ds((2 * b + 1) * block, block)
        upstream = jnp.concatenate([r.down_sum[low, :], r.down_sum[high, :]], axis=1).astype(FLOAT)
        unit, scale = standard(r.stream[rows, :])
        gain_sum_two = gain_sum_two + column_sums(upstream * unit)
        back_one = r.back[rows, :] + standard_back(upstream, gain_two, unit, scale)
        r.back[rows, :] = back_one
        back_attn = back_one.astype(HALF)
        r.slope[rows, :] = back_attn
        back_mix = dot(back_attn, r.out_all[me], (1, 1)).astype(HALF)
        r.back_mix[rows, :] = back_mix
        turned = back_mix.astype(FLOAT)
        for part in range(2):
            r.back_mix_t[2 * b + part] = turned[part * qry : (part + 1) * qry].T.astype(HALF)
        traffic.spend(1.5)
        for h in range(heads):

            def backward(part, _, h=h):
                here = 2 * b + part
                at = pl.ds(pl.multiple_of(here * qry, 16), qry)
                back_mix = r.back_mix[at, :]
                mine = back_mix * head_rows[h].astype(HALF)
                lean = jnp.sum(
                    mine.astype(FLOAT) * r.mixed[at, :], axis=-1, keepdims=True
                )
                weights = r.weights[h, at, :]
                back_weights = dot(mine, r.values_t[...])
                back_scores = (weights.astype(FLOAT) * (back_weights - lean)).astype(HALF)
                queries_back = dot(back_scores, r.keys[...]) * (head_rows[h] * HD**-0.5)
                if h == 0:
                    r.queries_back[at, :] = queries_back
                else:
                    r.queries_back[at, :] += queries_back
                lanes = pl.ds(h * HD, HD)
                r.values_back[lanes, :] += dot(r.back_mix_t[here, lanes, :], weights)
                r.keys_back[lanes, :] += dot(r.queries_t[here, lanes, :], back_scores)
                return 0

            lax.fori_loop(0, 2, backward, 0)
            traffic.spend(1.7)

    first = hidden + width
    pieces = [
        lambda: dot(r.mix_all[me].reshape(total_qry, inner), r.slope[...], (0, 0)),
        lambda: dot(r.queries_back[...].astype(HALF), r.normed_qry[...], (0, 0)),
        lambda: dot((r.keys_back[...] * HD**-0.5).astype(HALF), r.normed_ctx[...]),
        lambda: dot(r.values_back[...].astype(HALF), r.normed_ctx[...]),
    ]
    for place, piece in enumerate(pieces):
        r.main_work[pl.ds(first + place * inner, inner), :] = piece().astype(HALF)
        while (len(mains) + 1) * CHUNK <= first + (place + 1) * inner:
            send_chunk(len(mains))
        traffic.spend(0.7)

    over_gain = 1.0 / gain_one
    low_bins, low_embed, low_gains = (SMALL[name][0] for name in ("bins", "embed", "gains"))
    features = r.w_embed.shape[0]
    r.small[pl.ds(BINS, SMALL_ROWS - BINS), :] = jnp.zeros((SMALL_ROWS - BINS, width), FLOAT)
    bins_at = pl.ds(low_bins, BINS)
    embed_at = pl.ds(low_embed, features)

    def embed_back(upstream, normed, scale):
        unit = normed.astype(FLOAT) * over_gain
        return column_sums(upstream * unit), standard_back(upstream, gain_one, unit, scale)

    def context_back(place, gain_sum):
        slot, offset = lax.div(place, ctx // 256), lax.rem(place, ctx // 256)
        at = pl.ds(pl.multiple_of(place * 256, 256), 256)
        keys = (r.keys_back[:, at] * HD**-0.5).T.astype(HALF)
        values = r.values_back[:, at].T.astype(HALF)
        upstream = dot(keys, r.w_qkv[1]) + dot(values, r.w_qkv[2])
        gains, back_zero = embed_back(upstream, r.normed_ctx[at, :], as_column(r.scale_ctx[pl.ds(place, 1), :]))
        back_zero = back_zero.astype(HALF)
        feat = r.feat[slot, pl.ds(pl.multiple_of(offset * 256, 256), 256), :]
        r.small[embed_at, :] += dot(feat, back_zero, (0, 0))
        r.small[bins_at, :] += dot(one_hot(slot, offset), back_zero)
        return gain_sum + gains

    gain_sum_one = jnp.zeros((1, width), FLOAT)
    pieces = total_ctx // 256
    for part in range(2):
        gain_sum_one = lax.fori_loop(
            part * pieces // 2, (part + 1) * pieces // 2, context_back, gain_sum_one
        )
        traffic.spend(2.0)

    def query_back(slot, gain_sum):
        at = pl.ds(pl.multiple_of(slot * qry, 16), qry)
        upstream = dot(r.queries_back[at, :].astype(HALF), r.w_qkv[0])
        gains, back_zero = embed_back(upstream, r.normed_qry[at, :], as_column(r.scale_qry[pl.ds(slot, 1), :]))
        mine = jnp.where(slot == me, 1.0, 0.0)
        back_zero = (back_zero + mine * r.back[at, :]).astype(HALF)
        feat = r.feat[slot, pl.ds(ctx, qry), :]
        r.small[embed_at, :] += dot(feat, back_zero, (0, 0))
        return gain_sum + gains

    gain_sum_one = lax.fori_loop(0, groups, query_back, gain_sum_one)
    r.small[pl.ds(low_gains, 1), :] = gain_sum_one
    r.small[pl.ds(low_gains + 1, 1), :] = gain_sum_two / groups
    r.small[pl.ds(low_gains + 2, 1), :] = gain_sum_last / groups
    r.small_work[...] = r.small[...].astype(HALF)

    small_steps = stages_of(SMALL_ROWS, over_heads + over_tables, 64)
    pause = len(small_steps) - len(over_heads)
    smalls = Sum(
        copies, traffic, wide, r.small_work, r.small_out, 0, small_steps, places, until=pause
    )
    traffic.add(smalls)
    traffic.wait(smalls, losses, *mains)
    squares = one_value(sum_squares(r.main, r.main.shape[0]))
    r.square_work[...] = jnp.broadcast_to(squares, (16, 128))
    square_steps = stages_of(16, list(reversed(over_heads)), 16)
    squared = Sum(copies, traffic, tiny, r.square_work, r.square, 0, square_steps, places)
    smalls.go_on()
    traffic.add(squared)
    traffic.wait(squared, smalls)
    squares = r.square[0:8, :] + one_value(sum_squares(r.small_out, SMALL_ROWS))
    row = lax.broadcasted_iota(jnp.int32, (8, 128), 0)
    r.stats[...] = jnp.where(row == 0, squares, jnp.where(row == 1, r.loss[0:8, :], r.count[0:8, :]))


def train(sizes, inputs):
    shape = Named()
    shape.groups = sizes["heads"]
    features, shape.ctx = inputs["ctx_feat"].shape
    shape.qry = inputs["qry_feat"].shape[0]
    shape.width = inputs["w_embed"].shape[1]
    shape.inner = inputs["w_out_wide"].shape[0]
    shape.hidden = inputs["w_up_wide"].shape[1]
    shape.over_tables = [("tables", bit) for bit in bits_of(sizes["tables"])]
    shape.over_heads = [("heads", bit) for bit in bits_of(sizes["heads"])]
    groups, ctx, qry, width, inner, hidden = (
        shape.groups,
        shape.ctx,
        shape.qry,
        shape.width,
        shape.inner,
        shape.hidden,
    )
    total_ctx, total_qry = groups * ctx, groups * qry
    heads = inner // HD
    main_rows = hidden + width + 4 * inner
    block = 2 * qry
    main_steps = stages_of(CHUNK, shape.over_tables, 16)
    small_steps = stages_of(SMALL_ROWS, shape.over_heads + shape.over_tables, 64)
    sum_steps = stages_of(2 * block, shape.over_heads, block)
    wide_rows = main_rows // CHUNK * landing_rows(main_steps) + landing_rows(small_steps)
    narrow_rows = 2 * (total_qry // block) * landing_rows(sum_steps)
    every = len(shape.over_tables) + len(shape.over_heads)
    tiny_rows = 16 * (2 * every + len(shape.over_heads))
    tiny = ((16, 128), FLOAT)
    scratch = {
        "w_qkv": ((3, inner, width), HALF),
        "w_up": ((width, hidden), HALF),
        "w_down": ((hidden, width), HALF),
        "feat": ((groups, ctx + qry, features), HALF),
        "ints": ((groups, 8, ctx), jnp.int32),
        "out_all": ((groups, inner, width), HALF),
        "count_work": tiny,
        "count": tiny,
        "loss_work": tiny,
        "loss": tiny,
        "square_work": tiny,
        "square": tiny,
        "normed_ctx": ((total_ctx, width), HALF),
        "scale_ctx": ((total_ctx // 256, 256), FLOAT),
        "normed_qry": ((total_qry, width), HALF),
        "scale_qry": ((groups, qry), FLOAT),
        "stream": ((total_qry, width), FLOAT),
        "queries": ((total_qry, inner), HALF),
        "queries_t": ((groups, inner, qry), HALF),
        "keys": ((total_ctx, inner), HALF),
        "values": ((total_ctx, inner), HALF),
        "keys_t": ((inner, total_ctx), HALF),
        "values_t": ((inner, total_ctx), HALF),
        "weights": ((heads, total_qry, total_ctx), HALF),
        "mixed": ((total_qry, inner), FLOAT),
        "mix_all": ((groups, groups, qry, inner), HALF),
        "normed_two": ((total_qry, width), HALF),
        "active": ((total_qry, hidden), HALF),
        "slope": ((total_qry, hidden), HALF),
        "down_work": ((2 * total_qry, width // 2), HALF),
        "down_sum": ((2 * total_qry, width // 2), HALF),
        "back": ((total_qry, width), FLOAT),
        "back_mlp": ((total_qry, width), HALF),
        "back_up": ((total_qry, hidden), HALF),
        "back_mix": ((total_qry, inner), HALF),
        "back_mix_t": ((groups, inner, qry), HALF),
        "queries_back": ((total_qry, inner), FLOAT),
        "keys_back": ((inner, total_ctx), FLOAT),
        "values_back": ((inner, total_ctx), FLOAT),
        "main_work": ((main_rows, width), HALF),
        "small": ((SMALL_ROWS, width), FLOAT),
        "small_work": ((SMALL_ROWS, width), HALF),
        "wide_land": ((wide_rows, width), HALF),
        "narrow_land": ((narrow_rows, width // 2), HALF),
        "tiny_land": ((tiny_rows, 128), FLOAT),
    }
    outputs = {
        "main": jax.ShapeDtypeStruct((main_rows, width), HALF),
        "small_out": jax.ShapeDtypeStruct((SMALL_ROWS, width), HALF),
        "stats": jax.ShapeDtypeStruct((8, 128), FLOAT),
    }
    names = list(inputs) + list(outputs) + list(scratch) + ["sends", "recvs", "locals"]

    def kernel(*refs):
        named = Named()
        named.__dict__.update(zip(names, refs))
        train_kernel(shape, named)

    whole = pl.BlockSpec(memory_space=pltpu.VMEM)
    semaphores = pltpu.SemaphoreType.DMA((160,))
    return pl.pallas_call(
        kernel,
        out_shape=tuple(outputs.values()),
        in_specs=[
            pl.BlockSpec(memory_space=pl.ANY) if name.endswith("_wide") else whole
            for name in inputs
        ],
        out_specs=(whole,) * 3,
        scratch_shapes=[pltpu.VMEM(size, kind) for size, kind in scratch.values()]
        + [semaphores, semaphores, pltpu.SemaphoreType.DMA((8,))],
        compiler_params=pltpu.CompilerParams(
            collective_id=1, has_side_effects=True, vmem_limit_bytes=60 * 2**20
        ),
        name="train",
    )(*inputs.values())


def adam_kernel(refs):
    (stats, main_d, main_u, main_o, main_q, main_k, main_v, small) = refs[:8]
    w = refs[8:16]
    m = refs[16:24]
    v = refs[24:32]
    w_new = refs[32:40]
    m_new = refs[40:48]
    v_new = refs[48:56]
    loss, count, norm_out = refs[56:59]
    norm = jnp.sqrt(stats[0:1, 0:1])
    factor = jnp.minimum(1.0, CLIP_NORM / (norm + 1e-06))

    def update(which, gradient, rate, decay, at=...):
        gradient = gradient.astype(FLOAT) * factor
        results = adam_update(w[which][at], m[which][at], v[which][at], gradient, rate, decay)
        for target, value in zip((w_new, m_new, v_new), results):
            target[which][at] = value

    update(6, main_d[...], RATE, DECAY)
    update(5, main_u[...], RATE, DECAY)
    update(4, main_o[...], RATE_WIDE, DECAY)
    for part, gradient in enumerate((main_q, main_k, main_v)):
        update(3, gradient[...], RATE, DECAY, at=part)

    @pl.when(pl.program_id(0) == 0)
    def _():
        loss[...] = stats[1:2, 0:1]
        count[...] = stats[2:3, 0:1]
        norm_out[...] = norm

        def rows(name, count):
            low, size = SMALL[name]
            return small[low : low + size, :].astype(FLOAT)[:count]

        update(0, rows("embed", w[0].shape[0]), RATE, DECAY)
        update(1, rows("bins", w[1].shape[0]), RATE_WIDE, DECAY)
        update(2, rows("gains", w[2].shape[0]), RATE_WIDE, 0.0)
        update(7, rows("head", w[7].shape[0]), RATE, DECAY)


def adam_all(stats, main, small, weights, firsts, seconds):
    inner, width = weights[4].shape
    hidden = weights[5].shape[1]
    steps = 6

    def fixed(array):
        return pl.BlockSpec(array.shape, lambda step: (0,) * array.ndim)

    def rows_of(rows, low=0):
        size = rows // steps
        return pl.BlockSpec((size, width), lambda step: (low // size + step, 0))

    blocks = [
        fixed(weights[0]),
        fixed(weights[1]),
        fixed(weights[2]),
        pl.BlockSpec((3, inner // steps, width), lambda step: (0, step, 0)),
        rows_of(inner),
        pl.BlockSpec((width // steps, hidden), lambda step: (step, 0)),
        rows_of(hidden),
        fixed(weights[7]),
    ]
    first = hidden + width
    shapes = [jax.ShapeDtypeStruct(weight.shape, FLOAT) for weight in weights]
    return pl.pallas_call(
        lambda *refs: adam_kernel(refs),
        grid=(steps,),
        in_specs=[fixed(stats), rows_of(hidden), rows_of(width, hidden)]
        + [rows_of(inner, first + part * inner) for part in range(4)]
        + [fixed(small)]
        + blocks * 3,
        out_specs=blocks * 3 + [pl.BlockSpec((1, 1), lambda step: (0, 0))] * 3,
        out_shape=shapes * 3 + [jax.ShapeDtypeStruct((1, 1), FLOAT)] * 3,
        compiler_params=pltpu.CompilerParams(vmem_limit_bytes=58 * 2**20),
        name="adam",
    )(stats, *[main] * 6, small, *weights, *firsts, *seconds)


def shards(
    ctx_feat,
    qry_feat,
    counts,
    ctx_bins,
    qry_bins,
    query_mask,
    w_embed,
    w_bins,
    norm_gains,
    w_qkv,
    w_out,
    w_up,
    w_down,
    w_head,
    m_embed,
    m_bins,
    m_gains,
    m_qkv,
    m_out,
    m_up,
    m_down,
    m_head,
    v_embed,
    v_bins,
    v_gains,
    v_qkv,
    v_out,
    v_up,
    v_down,
    v_head,
):
    sizes = {"tables": lax.axis_size("tables"), "heads": lax.axis_size("heads")}
    main, small, stats = train(
        sizes,
        {
            "counts": counts.reshape(1, 1),
            "ctx_feat": ctx_feat[0].T,
            "qry_feat": qry_feat[0],
            "ctx_bins": ctx_bins,
            "qry_bins": qry_bins,
            "query_mask": query_mask,
            "w_embed": w_embed,
            "w_bins": w_bins,
            "gains": norm_gains,
            "w_qkv_wide": jnp.swapaxes(w_qkv, 1, 2),
            "w_out_wide": w_out,
            "w_up_wide": w_up,
            "w_down_wide": w_down,
            "w_head": w_head.T,
        },
    )
    results = adam_all(
        stats,
        main,
        small,
        *(
            (embed, bins, gains, jnp.swapaxes(qkv, 1, 2), out, up, down, head.T)
            for embed, bins, gains, qkv, out, up, down, head in (
                (w_embed, w_bins, norm_gains, w_qkv, w_out, w_up, w_down, w_head),
                (m_embed, m_bins, m_gains, m_qkv, m_out, m_up, m_down, m_head),
                (v_embed, v_bins, v_gains, v_qkv, v_out, v_up, v_down, v_head),
            )
        ),
    )
    *updated, loss, count, norm = results
    for low in range(0, 24, 8):
        updated[low + 3] = jnp.swapaxes(updated[low + 3], 1, 2)
        updated[low + 7] = updated[low + 7].T
    return (*updated, *(value.reshape(()) for value in (loss, count, norm)))


def solution(mesh):
    in_specs = (
        P("tables", "heads", None),
        P("tables", "heads", None),
        P("tables"),
        P("tables", "heads"),
        P("tables", "heads"),
        P("tables", "heads"),
        P(),
        P(),
        P(),
        P(None, None, "heads"),
        P("heads", None),
        P(None, "heads"),
        P("heads", None),
        P(),
        P(),
        P(),
        P(),
        P(None, None, "heads"),
        P("heads", None),
        P(None, "heads"),
        P("heads", None),
        P(),
        P(),
        P(),
        P(),
        P(None, None, "heads"),
        P("heads", None),
        P(None, "heads"),
        P("heads", None),
        P(),
    )
    out_specs = (
        P(),
        P(),
        P(),
        P(None, None, "heads"),
        P("heads", None),
        P(None, "heads"),
        P("heads", None),
        P(),
        P(),
        P(),
        P(),
        P(None, None, "heads"),
        P("heads", None),
        P(None, "heads"),
        P("heads", None),
        P(),
        P(),
        P(),
        P(),
        P(None, None, "heads"),
        P("heads", None),
        P(None, "heads"),
        P("heads", None),
        P(),
        P(),
        P(),
        P(),
    )
    return jax.shard_map(shards, mesh=mesh, in_specs=in_specs, out_specs=out_specs, check_vma=False)
```

```python
import functools

import jax
import jax.numpy as jnp
from jax import lax
from jax.experimental import pallas as pl
from jax.experimental.pallas import tpu as pltpu
from jax.sharding import PartitionSpec as P

HD = 64
BINS = 64
STEP = 10


NORM_EPS = 1e-05
ADAM_EPS = 1e-08
RATE = 0.05
RATE_WIDE = 1.0
BETA_ONE = 0.9
BETA_TWO = 0.95
DECAY = 0.1
CLIP_NORM = 0.02
MASKED = -1e30
FLOAT = jnp.float32
HALF = jnp.bfloat16
MESH = pl.DeviceIdType.MESH


def adam_update(weight, moment_one, moment_two, gradient, rate, decay_rate):
    moment_one = BETA_ONE * moment_one + (1.0 - BETA_ONE) * gradient
    moment_two = BETA_TWO * moment_two + (1.0 - BETA_TWO) * gradient * gradient
    first_hat = moment_one / (1.0 - BETA_ONE**STEP)
    second_hat = moment_two / (1.0 - BETA_TWO**STEP)
    root = second_hat * lax.rsqrt(second_hat) + ADAM_EPS
    inverse = pl.reciprocal(root, approx=True)
    inverse = inverse * (2.0 - root * inverse)
    weight = weight - rate * (first_hat * inverse + decay_rate * weight)
    return (weight, moment_one, moment_two)


def place_bit(place, bit):
    return lax.rem(lax.div(place, bit), 2)


def flip(place, bit):
    return place + bit - 2 * bit * place_bit(place, bit)


def bits_of(size):
    return [1 << power for power in range(size.bit_length() - 1)]


def partner(places, axis, bit):
    other = dict(places)
    other[axis] = flip(places[axis], bit)
    return (other["tables"], other["heads"])


def greet(places, axes):
    barrier = pltpu.get_barrier_semaphore()
    across = (flip(flip(places["tables"], 2), 4), places["heads"])
    others = [partner(places, axis, bit) for axis, bit in axes] + [across]
    for other in others:
        pl.semaphore_signal(barrier, inc=1, device_id=other, device_id_type=MESH)
    pl.semaphore_wait(barrier, len(others))


class Copies:
    def __init__(self, sends, recvs):
        self.sends, self.recvs, self.used = sends, recvs, 0

    def make(self, source, target, device):
        self.used += 1
        return pltpu.make_async_remote_copy(
            src_ref=source,
            dst_ref=target,
            send_sem=self.sends.at[self.used - 1],
            recv_sem=self.recvs.at[self.used - 1],
            device_id=device,
            device_id_type=MESH,
        )

    def start(self, source, target, device):
        copy = self.make(source, target, device)
        copy.start()
        return copy


class Landing:
    def __init__(self, rows_ref):
        self.rows_ref, self.used = rows_ref, 0

    def take(self, rows):
        self.used += rows
        return self.rows_ref.at[pl.ds(self.used - rows, rows), :]


class Traffic:
    LATENCY = 4.0

    def __init__(self):
        self.now, self.free, self.flows = 0.0, {}, []

    def book(self, axis, bit, size):
        link, hops = ("core", 0.15) if (axis, bit) == ("heads", 1) else (axis + str(min(bit, 2)), 1)
        if axis == "tables" and bit > 2:
            hops = bit // 2
        self.free[link] = max(self.now, self.free.get(link, 0.0)) + hops * size * 2 / 1e5
        return self.free[link] + self.LATENCY * min(hops + 0.4, 1)

    def book_link(self, link, size):
        self.free[link] = max(self.now, self.free.get(link, 0.0)) + size * 2 / 1e5
        return self.free[link] + self.LATENCY

    def add(self, flow):
        self.flows.append(flow)
        flow.start()

    def waiting(self):
        return [flow for flow in self.flows if flow.sent]

    def step(self):
        flow = min(self.waiting(), key=lambda flow: flow.ready)
        self.now = max(self.now, flow.ready) + 0.3
        flow.advance()

    def spend(self, time):
        self.now += time
        while any(flow.ready <= self.now for flow in self.waiting()):
            self.step()

    def wait(self, *flows):
        while not all(flow.done() for flow in flows):
            self.step()


def stages_of(rows, axes, least):
    steps = []
    for axis, bit in axes:
        if rows // 2 >= least and rows % 32 == 0:
            rows //= 2
            steps.append((axis, bit, "halve", rows))
        else:
            steps.append((axis, bit, "whole", rows))
    back = [(axis, bit, "back", left) for axis, bit, kind, left in reversed(steps) if kind == "halve"]
    return steps + back


def landing_rows(steps):
    return sum(left for _, _, kind, left in steps if kind != "back")


class Sum:
    def __init__(self, copies, traffic, landing, buffer, result, start, steps, places, until=None):
        self.copies, self.traffic, self.landing = copies, traffic, landing
        self.buffer, self.result, self.low = buffer, result, start
        self.steps, self.places = steps, places
        self.until = len(steps) if until is None else until
        self.at, self.sent, self.landed, self.ready = 0, None, None, 0.0
        self.last, self.found = None, None

    def rows(self, low, count):
        if isinstance(low, int):
            return pl.ds(low, count)
        return pl.ds(pl.multiple_of(low, 16), count)

    def finish(self):
        if self.sent is None:
            return
        _, _, kind, count = self.steps[self.at - 1]
        self.sent.wait()
        self.sent = None
        if kind != "back":
            mine = self.rows(self.low, count)
            total = self.buffer[mine, :].astype(FLOAT) + self.landed[...].astype(FLOAT)
            last = self.at == len(self.steps) or self.steps[self.at][2] == "back"
            target = self.result if last else self.buffer
            target[mine, :] = total.astype(self.buffer.dtype)

    def start(self):
        if self.at >= self.until:
            return
        axis, bit, kind, count = self.steps[self.at]
        self.at += 1
        side = place_bit(self.places[axis], bit)
        if kind == "halve":
            source = self.buffer.at[self.rows(self.low + count * (1 - side), count), :]
            self.low = self.low + count * side
            target = self.landed = self.landing.take(count)
        elif kind == "whole":
            source = self.buffer.at[self.rows(self.low, count), :]
            target = self.landed = self.landing.take(count)
        else:
            source = target = self.result.at[self.rows(self.low, count), :]
            self.low = self.low - count * side
        self.sent = self.copies.start(source, target, partner(self.places, axis, bit))
        self.ready = self.traffic.book(axis, bit, count * self.buffer.shape[-1] * 2)

    def advance(self):
        self.finish()
        self.start()
        if self.last and self.done():
            self.found = self.last()

    def go_on(self):
        self.until = len(self.steps)
        self.start()

    def done(self):
        return self.at >= self.until and self.sent is None


def chain_steps(rows, sizes):
    half = rows // 2
    others, left = [], half
    for bit in bits_of(sizes["tables"])[3:]:
        if left % 32 == 0:
            left //= 2
            others.append(("pair", bit, "halve", left, "inner"))
        else:
            others.append(("pair", bit, "whole", left, "inner"))
    others = others + [
        (move, bit, "back", count, who)
        for move, bit, kind, count, who in reversed(others)
        if kind == "halve"
    ]
    return [
        ("pair", 1, "halve", half, "all"),
        ("in", 2, "in", half, "row"),
        ("swap", 4, "whole", half, "inner"),
        *others,
        ("out", 2, "out", half, "row"),
        ("pair", 1, "back", half, "all"),
    ]


def chain_landing(steps):
    return sum(
        count for move, bit, kind, count, who in steps[1:] if kind in ("halve", "whole", "in")
    )


class Chain:
    def __init__(self, copies, traffic, landing, buffer, result, start, steps, places):
        self.copies, self.traffic, self.landing = copies, traffic, landing
        self.buffer, self.result, self.low = buffer, result, start
        self.steps, self.places = steps, places
        self.at, self.sent, self.landed, self.ready = 0, None, None, 0.0
        self.last, self.found = None, None
        low, high = (place_bit(places["tables"], bit) for bit in (2, 4))
        self.inner = low + high == 1
        self.outer = low + high != 1

    def rows(self, low, count):
        if isinstance(low, int):
            return pl.ds(low, count)
        return pl.ds(pl.multiple_of(low, 16), count)

    def add(self, count):
        mine = self.rows(self.low, count)
        total = self.buffer[mine, :].astype(FLOAT) + self.landed[...].astype(FLOAT)
        last = not any(step[2] in ("halve", "whole", "in") for step in self.steps[self.at :])
        target = self.result if last else self.buffer
        target[mine, :] = total.astype(self.buffer.dtype)

    def finish(self):
        if self.sent is None:
            return
        move, _, kind, count, who = self.steps[self.at - 1]
        sent, self.sent = self.sent, None
        if who == "row":
            senders, getters = (
                (self.outer, self.inner) if move == "in" else (self.inner, self.outer)
            )

            @pl.when(senders)
            def _():
                sent.wait_send()

            @pl.when(getters)
            def _():
                sent.wait_recv()
                if move == "in":
                    self.add(count)

        elif who == "inner":

            @pl.when(self.inner)
            def _():
                sent.wait()
                if kind != "back":
                    self.add(count)

        else:
            sent.wait()
            if kind != "back":
                self.add(count)

    def start(self):
        if self.at >= len(self.steps):
            return
        move, bit, kind, count, who = self.steps[self.at]
        first = self.at == 0
        self.at += 1
        place = self.places["tables"]
        side = place_bit(place, bit)
        other = flip(flip(place, 2), 4) if move == "swap" else flip(place, bit)
        if kind == "halve":
            given = self.rows(self.low + count * (1 - side), count)
            self.low = self.low + count * side
        else:
            given = self.rows(self.low, count)
        if kind in ("back", "out"):
            source = target = self.result.at[given, :]
        elif first:
            source, target = self.buffer.at[given, :], self.result.at[given, :]
            self.landed = self.result.at[self.rows(self.low, count), :]
        else:
            source = self.buffer.at[given, :]
            target = self.landed = self.landing.take(count)
        if kind == "back":
            self.low = self.low - count * side
        copy = self.copies.make(source, target, (other, self.places["heads"]))
        if who == "all":
            copy.start()
        else:
            senders = self.outer if move == "in" else self.inner

            @pl.when(senders)
            def _():
                copy.start()

        self.sent = copy
        link = move if move != "pair" else "tables" + str(min(bit, 2))
        self.ready = self.traffic.book_link(link, count * self.buffer.shape[-1] * 2)

    def advance(self):
        self.finish()
        self.start()
        if self.last and self.done():
            self.found = self.last()

    def done(self):
        return self.at >= len(self.steps) and self.sent is None


class Gather:
    def __init__(self, copies, traffic, views, size, places, bits):
        self.copies, self.traffic, self.views, self.size = copies, traffic, views, size
        self.places, self.bits = places, bits
        self.at, self.held, self.sent, self.ready = 0, [places["heads"]], [], 0.0

    def advance(self):
        self.finish()
        self.start()

    def finish(self):
        for copy in self.sent:
            copy.wait()
        if self.sent:
            self.held = self.held + [flip(slot, self.bits[self.at - 1]) for slot in self.held]
        self.sent = []

    def start(self):
        if self.at < len(self.bits):
            bit = self.bits[self.at]
            other = partner(self.places, "heads", bit)
            self.sent = [
                self.copies.start(view(slot), view(slot), other)
                for slot in self.held
                for view in self.views
            ]
            self.ready = self.traffic.book("heads", bit, self.size * len(self.held))
            self.at += 1

    def done(self):
        return self.at >= len(self.bits) and not self.sent


def places_here():
    return {"tables": lax.axis_index("tables"), "heads": lax.axis_index("heads")}


SMALL = {"head": (0, 64), "bins": (64, 64), "embed": (128, 112), "gains": (240, 16)}
SMALL_ROWS = 256
CHUNK = 256
SPAN = 2


def dot(left, right, over=(1, 0)):
    return lax.dot_general(
        left, right, (((over[0],), (over[1],)), ((), ())), preferred_element_type=FLOAT
    )


def standard(rows):
    center = rows - jnp.mean(rows, axis=-1, keepdims=True)
    scale = lax.rsqrt(jnp.mean(center * center, axis=-1, keepdims=True) + NORM_EPS)
    return center * scale, scale


def standard_back(upstream, gain_row, unit, scale):
    inner = upstream * gain_row
    lean = jnp.mean(inner, axis=-1, keepdims=True)
    tilt = jnp.mean(inner * unit, axis=-1, keepdims=True)
    return (inner - lean - unit * tilt) * scale


def as_row(column):
    return jnp.broadcast_to(column, (column.shape[0], 128)).T[:1]


def as_column(row):
    return jnp.broadcast_to(row, (8, row.shape[1])).T[:, :1]


def column_sums(rows):
    return jnp.sum(rows, axis=0, keepdims=True)


def gelu_both(hidden):
    root = 0.7978845608028654
    square = hidden * hidden
    bent = jnp.tanh(root * hidden * (1.0 + 0.044715 * square))
    half = 0.5 * (1.0 + bent)
    slope = half + 0.5 * hidden * (1.0 - bent * bent) * root * (1.0 + 0.134145 * square)
    return hidden * half, slope


def sum_squares(rows_ref, low, count):
    def piece(step, total):
        part = rows_ref[pl.ds(pl.multiple_of(low + step * 64, 64), 64), :].astype(FLOAT)
        return total + jnp.sum((part * part).reshape(8, 8, part.shape[1]), axis=0)

    return lax.fori_loop(0, count // 64, piece, jnp.zeros((8, rows_ref.shape[1]), FLOAT))


def one_value(total):
    return jnp.sum(jnp.sum(total, axis=0, keepdims=True), axis=1, keepdims=True)


class Named:
    pass


def train_kernel(shape, r):
    groups, ctx, qry, width, inner, hidden = (
        shape.groups,
        shape.ctx,
        shape.qry,
        shape.width,
        shape.inner,
        shape.hidden,
    )
    heads = inner // HD
    total_ctx, total_qry = groups * ctx, groups * qry
    block = SPAN * qry
    blocks = total_qry // block
    half = width // 2
    places = places_here()
    me = places["heads"]
    copies = Copies(r.sends, r.recvs)
    traffic = Traffic()
    over_heads, over_tables = shape.over_heads, shape.over_tables
    far_first = [bit for _, bit in reversed(over_heads)]
    tiny = Landing(r.tiny_land)
    wide = Landing(r.wide_land)
    narrow = Landing(r.narrow_land)
    def stage(number, source, target):
        copy = pltpu.make_async_copy(source, target, r.locals.at[number])
        copy.start()
        return copy

    low = 3 * inner
    loads = [
        stage(part, r.w_qkv_wide.at[part], r.back.at[pl.ds(part * inner, inner), :])
        for part in range(3)
    ]
    loads.append(stage(3, r.w_out_wide, r.small.at[pl.ds(0, inner), :]))

    def load_halves(number, source):
        rest = source.shape[0] - low
        return [
            stage(number, source.at[pl.ds(0, low), :], r.back.at[pl.ds(0, low), :]),
            stage(number + 1, source.at[pl.ds(low, rest), :], r.small.at[pl.ds(0, rest), :]),
        ]

    def take_halves(copies_in, target):
        rest = target.shape[0] - low
        for copy in copies_in:
            copy.wait()
        target[pl.ds(0, low), :] = r.back[pl.ds(0, low), :].astype(HALF)
        target[pl.ds(low, rest), :] = r.small[pl.ds(0, rest), :].astype(HALF)

    greet(places, over_heads + over_tables)

    r.feat[me, pl.ds(0, ctx), :] = r.ctx_feat[...].astype(FLOAT).T.astype(HALF)
    r.feat[me, pl.ds(ctx, qry), :] = r.qry_feat[...]
    r.ints[me] = jnp.zeros((8, ctx), jnp.int32)
    r.ints[me, 0:1, :] = r.ctx_bins[...]
    r.ints[me, 1:2, pl.ds(0, qry)] = r.qry_bins[...]
    r.ints[me, 2:3, pl.ds(0, qry)] = r.query_mask[...]
    rows_in = Gather(
        copies,
        traffic,
        [lambda slot: r.feat.at[slot], lambda slot: r.ints.at[slot]],
        (ctx + qry) * 256 + ctx * 32,
        places,
        far_first,
    )
    traffic.add(rows_in)
    mask_sum = jnp.sum(r.query_mask[...].astype(FLOAT), axis=1, keepdims=True)
    r.count_work[...] = jnp.broadcast_to(mask_sum, (16, 128))
    tiny_steps = stages_of(16, over_heads + over_tables, 16)
    counted = Sum(copies, traffic, tiny, r.count_work, r.count, 0, tiny_steps, places)
    traffic.add(counted)
    for copy in loads:
        copy.wait()
    for part in range(3):
        r.w_qkv[part] = r.back[pl.ds(part * inner, inner), :].astype(HALF)
    r.out_all[me] = r.small[pl.ds(0, inner), :].astype(HALF)
    loads = load_halves(4, r.w_up_wide)
    outs_in = Gather(
        copies, traffic, [lambda slot: r.out_all.at[slot]], inner * width * 2, places, far_first
    )

    embed_half = r.w_embed[...].astype(HALF)
    bins_half = r.w_bins[...].astype(HALF)
    gain_one, gain_two, gain_last = (r.gains[row : row + 1, :] for row in range(3))
    bin_rows = lax.broadcasted_iota(jnp.int32, (BINS, 256), 0)

    def one_hot(slot, place):
        return jnp.where(
            bin_rows == r.ints[slot, 0:1, pl.ds(pl.multiple_of(place * 256, 256), 256)], 1.0, 0.0
        ).astype(HALF)

    def embed_shard(slot):
        def context(place, _):
            at = pl.multiple_of(slot * ctx + place * 256, 256)
            feat = r.feat[slot, pl.ds(pl.multiple_of(place * 256, 256), 256), :]
            zero = dot(feat, embed_half) + dot(one_hot(slot, place), bins_half, (0, 0))
            unit, scale = standard(zero)
            normed = (unit * gain_one).astype(HALF)
            r.normed_ctx[pl.ds(at, 256), :] = normed
            r.scale_ctx[pl.ds(slot * (ctx // 256) + place, 1), :] = as_row(scale)
            keys = dot(normed, r.w_qkv[1], (1, 1))
            values = dot(normed, r.w_qkv[2], (1, 1))
            r.keys[pl.ds(at, 256), :] = keys.astype(HALF)
            r.values[pl.ds(at, 256), :] = values.astype(HALF)
            r.keys_t[:, pl.ds(at, 256)] = keys.T.astype(HALF)
            r.values_t[:, pl.ds(at, 256)] = values.T.astype(HALF)
            return 0

        lax.fori_loop(0, ctx // 256, context, 0)
        at = pl.multiple_of(slot * qry, 16)
        zero = dot(r.feat[slot, pl.ds(ctx, qry), :], embed_half)
        r.stream[pl.ds(at, qry), :] = zero
        unit, scale = standard(zero)
        normed = (unit * gain_one).astype(HALF)
        r.normed_qry[pl.ds(at, qry), :] = normed
        r.scale_qry[pl.ds(slot, 1), :] = as_row(scale)
        queries = dot(normed, r.w_qkv[0], (1, 1))
        r.queries[pl.ds(at, qry), :] = queries.astype(HALF)
        r.queries_t[slot] = queries.T.astype(HALF)

    done = 0
    while done < groups:
        for slot in rows_in.held[done:]:
            embed_shard(slot)
            done += 1
            traffic.spend(2.0)
            if done == 1:
                traffic.add(outs_in)
                take_halves(loads, r.w_up)
                loads = load_halves(6, r.w_down_wide)
            if done == 2:
                take_halves(loads, r.w_down)
        if done == len(rows_in.held) and done < groups:
            traffic.step()

    lane = lax.broadcasted_iota(jnp.int32, (1, inner), 1)
    head_rows = [
        jnp.where((lane >= h * HD) & (lane < (h + 1) * HD), 1.0, 0.0).astype(FLOAT)
        for h in range(heads)
    ]
    slots_at = lax.broadcasted_iota(jnp.int32, (1, total_ctx), 1)
    dead = jnp.where(slots_at < r.counts[0:1, 0:1], 0.0, MASKED)
    mixing = []
    for b in range(groups):
        rows = pl.ds(b * qry, qry)
        query_blk = r.queries[rows, :]
        mixed = jnp.zeros((qry, inner), FLOAT)
        for h in range(heads):
            raw = dot(query_blk * (head_rows[h] * HD**-0.5).astype(HALF), r.keys_t[...]) + dead
            raised = jnp.exp(raw - jnp.max(raw, axis=-1, keepdims=True))
            weights = (raised * (1.0 / jnp.sum(raised, axis=-1, keepdims=True))).astype(HALF)
            r.weights[h, rows, :] = weights
            mixed = mixed + dot(weights, r.values[...]) * head_rows[h]
        r.mixed[rows, :] = mixed
        r.mix_all[me, b] = mixed.astype(HALF)
        mixing.append(
            Gather(
                copies,
                traffic,
                [lambda slot, b=b: r.mix_all.at[slot, b]],
                qry * 512,
                places,
                far_first,
            )
        )
        traffic.add(mixing[-1])
        traffic.spend(2.0)

    sum_steps = stages_of(2 * block, over_heads, block)
    down_sums, back_sums = [], []
    for b in range(blocks):
        traffic.wait(outs_in, *mixing[SPAN * b : SPAN * (b + 1)])
        rows = pl.ds(b * block, block)
        attended = []
        for part in range(SPAN * b, SPAN * (b + 1)):
            total = dot(r.mix_all[0, part], r.out_all[0])
            for slot in range(1, groups):
                total = total + dot(r.mix_all[slot, part], r.out_all[slot])
            attended.append(total)
        stream = r.stream[rows, :] + jnp.concatenate(attended, axis=0)
        r.stream[rows, :] = stream
        unit, _ = standard(stream)
        normed = (unit * gain_two).astype(HALF)
        r.normed_two[rows, :] = normed
        active, slope = gelu_both(dot(normed, r.w_up[...]))
        active = active.astype(HALF)
        r.active[rows, :] = active
        r.slope[rows, :] = slope.astype(HALF)
        low = pl.ds(2 * b * block, block)
        high = pl.ds((2 * b + 1) * block, block)
        part = dot(active, r.w_down[...]).astype(HALF)
        r.down_work[low, :] = part[:, :half]
        r.down_work[high, :] = part[:, half:]
        down_sums.append(
            Sum(copies, traffic, narrow, r.down_work, r.down_sum, 2 * b * block, sum_steps, places)
        )
        traffic.add(down_sums[-1])
        traffic.spend(2.0)

    mains = []

    def send_chunk(place):
        start = CHUNK * place
        part = Chain(
            copies, traffic, wide, r.main_work, r.main, start, shape.main_steps, places
        )
        part.last = functools.partial(sum_squares, r.main, start, CHUNK)
        mains.append(part)
        traffic.add(part)
        traffic.spend(0.5)

    head_half = r.w_head[...].astype(HALF)
    traffic.wait(counted)
    divisor = jnp.maximum(r.count[0:1, 0:1], 1.0)
    tall = lax.broadcasted_iota(jnp.int32, (BINS, 256), 0)
    loss = jnp.zeros((1, 1), FLOAT)
    grad_head = jnp.zeros((BINS, width), FLOAT)
    gain_sum_last = jnp.zeros((1, width), FLOAT)
    for b in range(blocks):
        traffic.wait(counted, down_sums[b])
        rows = pl.ds(b * block, block)
        low = pl.ds(2 * b * block, block)
        high = pl.ds((2 * b + 1) * block, block)
        mlp = jnp.concatenate([r.down_sum[low, :], r.down_sum[high, :]], axis=1)
        unit, scale = standard(r.stream[rows, :] + mlp.astype(FLOAT))
        normed = (unit * gain_last).astype(HALF)
        logits = dot(normed, head_half, (1, 1))
        targets, masks = [], []
        for slot in range(SPAN * b, SPAN * (b + 1)):
            target = jnp.where(tall == r.ints[slot, 1:2, 0:256], 1.0, 0.0)
            targets.append(target.T[:qry])
            mask = jnp.broadcast_to(r.ints[slot, 2:3, 0:256].astype(FLOAT), (8, 256))
            masks.append(mask.T[:qry, :1])
        target = jnp.concatenate(targets, axis=0)
        mask = jnp.concatenate(masks, axis=0)
        top = jnp.max(logits, axis=-1, keepdims=True)
        log_bins = top + jnp.log(jnp.sum(jnp.exp(logits - top), axis=-1, keepdims=True))
        missed = log_bins - jnp.sum(target * logits, axis=-1, keepdims=True)
        loss = loss + jnp.sum(mask * missed, axis=0, keepdims=True)
        back_logits = (mask * (jnp.exp(logits - log_bins) - target) / divisor).astype(HALF)
        grad_head = grad_head + dot(back_logits, normed, (0, 0))
        back_final = dot(back_logits, head_half)
        gain_sum_last = gain_sum_last + column_sums(back_final * unit)
        back_two = standard_back(back_final, gain_last, unit, scale)
        r.back[rows, :] = back_two
        back_mlp = back_two.astype(HALF)
        r.back_mlp[rows, :] = back_mlp
        back_active = dot(back_mlp, r.w_down[...], (1, 1))
        back_up = (r.slope[rows, :].astype(FLOAT) * back_active).astype(HALF)
        r.back_up[rows, :] = back_up
        part = dot(back_up, r.w_up[...], (1, 1)).astype(HALF)
        r.down_work[low, :] = part[:, :half]
        r.down_work[high, :] = part[:, half:]
        back_sums.append(
            Sum(copies, traffic, narrow, r.down_work, r.down_sum, 2 * b * block, sum_steps, places)
        )
        traffic.add(back_sums[-1])
        traffic.spend(3.0)
    r.loss_work[...] = jnp.broadcast_to(loss / groups, (16, 128))
    losses = Sum(copies, traffic, tiny, r.loss_work, r.loss, 0, tiny_steps, places)
    traffic.add(losses)
    r.small[pl.ds(0, BINS), :] = grad_head / groups

    for place in range(hidden // CHUNK):
        at = pl.ds(place * CHUNK, CHUNK)
        r.main_work[at, :] = dot(r.active[:, at], r.back_mlp[...], (0, 0)).astype(HALF)
        send_chunk(len(mains))
    for place in range(width // CHUNK):
        at = pl.ds(place * CHUNK, CHUNK)
        to = pl.ds(hidden + place * CHUNK, CHUNK)
        r.main_work[to, :] = dot(r.normed_two[:, at], r.back_up[...], (0, 0)).astype(HALF)
        send_chunk(len(mains))

    gain_sum_two = jnp.zeros((1, width), FLOAT)
    r.keys_back[...] = jnp.zeros(r.keys_back.shape, FLOAT)
    r.values_back[...] = jnp.zeros(r.values_back.shape, FLOAT)
    for b in range(blocks):
        traffic.wait(back_sums[b])
        rows = pl.ds(b * block, block)
        low = pl.ds(2 * b * block, block)
        high = pl.ds((2 * b + 1) * block, block)
        upstream = jnp.concatenate([r.down_sum[low, :], r.down_sum[high, :]], axis=1).astype(FLOAT)
        unit, scale = standard(r.stream[rows, :])
        gain_sum_two = gain_sum_two + column_sums(upstream * unit)
        back_one = r.back[rows, :] + standard_back(upstream, gain_two, unit, scale)
        r.back[rows, :] = back_one
        back_attn = back_one.astype(HALF)
        r.slope[rows, :] = back_attn
        back_mix = dot(back_attn, r.out_all[me], (1, 1)).astype(HALF)
        r.back_mix[rows, :] = back_mix
        turned = back_mix.astype(FLOAT)
        for part in range(SPAN):
            r.back_mix_t[SPAN * b + part] = turned[part * qry : (part + 1) * qry].T.astype(HALF)
        traffic.spend(1.5)
        for h in range(heads):

            def backward(part, _, h=h):
                here = SPAN * b + part
                at = pl.ds(pl.multiple_of(here * qry, 16), qry)
                back_mix = r.back_mix[at, :]
                mine = back_mix * head_rows[h].astype(HALF)
                lean = jnp.sum(
                    mine.astype(FLOAT) * r.mixed[at, :], axis=-1, keepdims=True
                )
                weights = r.weights[h, at, :]
                back_weights = dot(mine, r.values_t[...])
                back_scores = (weights.astype(FLOAT) * (back_weights - lean)).astype(HALF)
                queries_back = dot(back_scores, r.keys[...]) * (head_rows[h] * HD**-0.5)
                if h == 0:
                    r.queries_back[at, :] = queries_back
                else:
                    r.queries_back[at, :] += queries_back
                lanes = pl.ds(h * HD, HD)
                r.values_back[lanes, :] += dot(r.back_mix_t[here, lanes, :], weights)
                r.keys_back[lanes, :] += dot(r.queries_t[here, lanes, :], back_scores)
                return 0

            lax.fori_loop(0, SPAN, backward, 0)
            traffic.spend(1.7)

    first = hidden + width
    pieces = [
        lambda: dot(r.mix_all[me].reshape(total_qry, inner), r.slope[...], (0, 0)),
        lambda: dot(r.queries_back[...].astype(HALF), r.normed_qry[...], (0, 0)),
        lambda: dot((r.keys_back[...] * HD**-0.5).astype(HALF), r.normed_ctx[...]),
        lambda: dot(r.values_back[...].astype(HALF), r.normed_ctx[...]),
    ]
    for place, piece in enumerate(pieces):
        r.main_work[pl.ds(first + place * inner, inner), :] = piece().astype(HALF)
        while (len(mains) + 1) * CHUNK <= first + (place + 1) * inner:
            send_chunk(len(mains))
        traffic.spend(0.7)

    over_gain = 1.0 / gain_one
    low_bins, low_embed, low_gains = (SMALL[name][0] for name in ("bins", "embed", "gains"))
    features = r.w_embed.shape[0]
    r.small[pl.ds(BINS, SMALL_ROWS - BINS), :] = jnp.zeros((SMALL_ROWS - BINS, width), FLOAT)
    bins_at = pl.ds(low_bins, BINS)
    embed_at = pl.ds(low_embed, features)

    def embed_back(upstream, normed, scale):
        unit = normed.astype(FLOAT) * over_gain
        return column_sums(upstream * unit), standard_back(upstream, gain_one, unit, scale)

    def context_back(place, gain_sum):
        slot, offset = lax.div(place, ctx // 256), lax.rem(place, ctx // 256)
        at = pl.ds(pl.multiple_of(place * 256, 256), 256)
        keys = (r.keys_back[:, at] * HD**-0.5).T.astype(HALF)
        values = r.values_back[:, at].T.astype(HALF)
        upstream = dot(keys, r.w_qkv[1]) + dot(values, r.w_qkv[2])
        gains, back_zero = embed_back(upstream, r.normed_ctx[at, :], as_column(r.scale_ctx[pl.ds(place, 1), :]))
        back_zero = back_zero.astype(HALF)
        feat = r.feat[slot, pl.ds(pl.multiple_of(offset * 256, 256), 256), :]
        r.small[embed_at, :] += dot(feat, back_zero, (0, 0))
        r.small[bins_at, :] += dot(one_hot(slot, offset), back_zero)
        return gain_sum + gains

    gain_sum_one = jnp.zeros((1, width), FLOAT)
    pieces = total_ctx // 256
    for part in range(2):
        gain_sum_one = lax.fori_loop(
            part * pieces // 2, (part + 1) * pieces // 2, context_back, gain_sum_one
        )
        traffic.spend(2.0)

    def query_back(slot, gain_sum):
        at = pl.ds(pl.multiple_of(slot * qry, 16), qry)
        upstream = dot(r.queries_back[at, :].astype(HALF), r.w_qkv[0])
        gains, back_zero = embed_back(upstream, r.normed_qry[at, :], as_column(r.scale_qry[pl.ds(slot, 1), :]))
        mine = jnp.where(slot == me, 1.0, 0.0)
        back_zero = (back_zero + mine * r.back[at, :]).astype(HALF)
        feat = r.feat[slot, pl.ds(ctx, qry), :]
        r.small[embed_at, :] += dot(feat, back_zero, (0, 0))
        return gain_sum + gains

    gain_sum_one = lax.fori_loop(0, groups, query_back, gain_sum_one)
    r.small[pl.ds(low_gains, 1), :] = gain_sum_one
    r.small[pl.ds(low_gains + 1, 1), :] = gain_sum_two / groups
    r.small[pl.ds(low_gains + 2, 1), :] = gain_sum_last / groups
    r.small_work[...] = r.small[...].astype(HALF)

    small_steps = stages_of(SMALL_ROWS, over_heads + over_tables, 64)
    pause = len(small_steps) - len(over_heads)
    smalls = Sum(
        copies, traffic, wide, r.small_work, r.small_out, 0, small_steps, places, until=pause
    )
    traffic.add(smalls)
    traffic.wait(smalls, losses, *mains)
    squares = one_value(sum(part.found for part in mains))
    r.square_work[...] = jnp.broadcast_to(squares, (16, 128))
    square_steps = stages_of(16, list(reversed(over_heads)), 16)
    squared = Sum(copies, traffic, tiny, r.square_work, r.square, 0, square_steps, places)
    smalls.go_on()
    traffic.add(squared)
    traffic.wait(squared, smalls)
    squares = r.square[0:8, :] + one_value(sum_squares(r.small_out, 0, SMALL_ROWS))
    row = lax.broadcasted_iota(jnp.int32, (8, 128), 0)
    r.stats[...] = jnp.where(row == 0, squares, jnp.where(row == 1, r.loss[0:8, :], r.count[0:8, :]))


def train(sizes, inputs):
    shape = Named()
    shape.groups = sizes["heads"]
    features, shape.ctx = inputs["ctx_feat"].shape
    shape.qry = inputs["qry_feat"].shape[0]
    shape.width = inputs["w_embed"].shape[1]
    shape.inner = inputs["w_out_wide"].shape[0]
    shape.hidden = inputs["w_up_wide"].shape[1]
    shape.over_tables = [("tables", bit) for bit in bits_of(sizes["tables"])]
    shape.over_heads = [("heads", bit) for bit in bits_of(sizes["heads"])]
    groups, ctx, qry, width, inner, hidden = (
        shape.groups,
        shape.ctx,
        shape.qry,
        shape.width,
        shape.inner,
        shape.hidden,
    )
    total_ctx, total_qry = groups * ctx, groups * qry
    heads = inner // HD
    main_rows = hidden + width + 4 * inner
    block = SPAN * qry
    shape.main_steps = chain_steps(CHUNK, sizes)
    small_steps = stages_of(SMALL_ROWS, shape.over_heads + shape.over_tables, 64)
    sum_steps = stages_of(2 * block, shape.over_heads, block)
    wide_rows = main_rows // CHUNK * chain_landing(shape.main_steps) + landing_rows(small_steps)
    narrow_rows = 2 * (total_qry // block) * landing_rows(sum_steps)
    every = len(shape.over_tables) + len(shape.over_heads)
    tiny_rows = 16 * (2 * every + len(shape.over_heads))
    tiny = ((16, 128), FLOAT)
    scratch = dict(
        w_qkv=((3, inner, width), HALF),
        w_up=((width, hidden), HALF),
        w_down=((hidden, width), HALF),
        feat=((groups, ctx + qry, features), HALF),
        ints=((groups, 8, ctx), jnp.int32),
        out_all=((groups, inner, width), HALF),
        count_work=tiny,
        count=tiny,
        loss_work=tiny,
        loss=tiny,
        square_work=tiny,
        square=tiny,
        normed_ctx=((total_ctx, width), HALF),
        scale_ctx=((total_ctx // 256, 256), FLOAT),
        normed_qry=((total_qry, width), HALF),
        scale_qry=((groups, qry), FLOAT),
        stream=((total_qry, width), FLOAT),
        queries=((total_qry, inner), HALF),
        queries_t=((groups, inner, qry), HALF),
        keys=((total_ctx, inner), HALF),
        values=((total_ctx, inner), HALF),
        keys_t=((inner, total_ctx), HALF),
        values_t=((inner, total_ctx), HALF),
        weights=((heads, total_qry, total_ctx), HALF),
        mixed=((total_qry, inner), FLOAT),
        mix_all=((groups, groups, qry, inner), HALF),
        normed_two=((total_qry, width), HALF),
        active=((total_qry, hidden), HALF),
        slope=((total_qry, hidden), HALF),
        down_work=((2 * total_qry, width // 2), HALF),
        down_sum=((2 * total_qry, width // 2), HALF),
        back=((total_qry, width), FLOAT),
        back_mlp=((total_qry, width), HALF),
        back_up=((total_qry, hidden), HALF),
        back_mix=((total_qry, inner), HALF),
        back_mix_t=((groups, inner, qry), HALF),
        queries_back=((total_qry, inner), FLOAT),
        keys_back=((inner, total_ctx), FLOAT),
        values_back=((inner, total_ctx), FLOAT),
        main_work=((main_rows, width), HALF),
        small=((SMALL_ROWS, width), FLOAT),
        small_work=((SMALL_ROWS, width), HALF),
        wide_land=((wide_rows, width), HALF),
        narrow_land=((narrow_rows, width // 2), HALF),
        tiny_land=((tiny_rows, 128), FLOAT),
    )
    outputs = dict(
        main=jax.ShapeDtypeStruct((main_rows, width), HALF),
        small_out=jax.ShapeDtypeStruct((SMALL_ROWS, width), HALF),
        stats=jax.ShapeDtypeStruct((8, 128), FLOAT),
    )
    names = list(inputs) + list(outputs) + list(scratch) + ["sends", "recvs", "locals"]

    def kernel(*refs):
        named = Named()
        named.__dict__.update(zip(names, refs))
        train_kernel(shape, named)

    whole = pl.BlockSpec(memory_space=pltpu.VMEM)
    semaphores = pltpu.SemaphoreType.DMA((192,))
    return pl.pallas_call(
        kernel,
        out_shape=tuple(outputs.values()),
        in_specs=[
            pl.BlockSpec(memory_space=pl.ANY) if name.endswith("_wide") else whole
            for name in inputs
        ],
        out_specs=(whole,) * 3,
        scratch_shapes=[pltpu.VMEM(size, kind) for size, kind in scratch.values()]
        + [semaphores, semaphores, pltpu.SemaphoreType.DMA((8,))],
        compiler_params=pltpu.CompilerParams(
            collective_id=1, has_side_effects=True, vmem_limit_bytes=62 * 2**20
        ),
        name="train",
    )(*inputs.values())


def adam_kernel(refs):
    (stats, main_d, main_u, main_o, main_q, main_k, main_v, small) = refs[:8]
    w = refs[8:16]
    m = refs[16:24]
    v = refs[24:32]
    w_new = refs[32:40]
    m_new = refs[40:48]
    v_new = refs[48:56]
    loss, count, norm_out = refs[56:59]
    norm = jnp.sqrt(stats[0:1, 0:1])
    factor = jnp.minimum(1.0, CLIP_NORM / (norm + 1e-06))

    def update(which, gradient, rate, decay, at=...):
        gradient = gradient.astype(FLOAT) * factor
        results = adam_update(w[which][at], m[which][at], v[which][at], gradient, rate, decay)
        for target, value in zip((w_new, m_new, v_new), results):
            target[which][at] = value

    update(6, main_d[...], RATE, DECAY)
    update(5, main_u[...], RATE, DECAY)
    update(4, main_o[...], RATE_WIDE, DECAY)
    for part, gradient in enumerate((main_q, main_k, main_v)):
        update(3, gradient[...], RATE, DECAY, at=part)

    @pl.when(pl.program_id(0) == 0)
    def _():
        loss[...] = stats[1:2, 0:1]
        count[...] = stats[2:3, 0:1]
        norm_out[...] = norm

        def rows(name, count):
            low, size = SMALL[name]
            return small[low : low + size, :].astype(FLOAT)[:count]

        update(0, rows("embed", w[0].shape[0]), RATE, DECAY)
        update(1, rows("bins", w[1].shape[0]), RATE_WIDE, DECAY)
        update(2, rows("gains", w[2].shape[0]), RATE_WIDE, 0.0)
        update(7, rows("head", w[7].shape[0]), RATE, DECAY)


def adam_all(stats, main, small, weights, firsts, seconds):
    inner, width = weights[4].shape
    hidden = weights[5].shape[1]
    steps = 6

    def fixed(array):
        return pl.BlockSpec(array.shape, lambda step: (0,) * array.ndim)

    def rows_of(rows, low=0):
        size = rows // steps
        return pl.BlockSpec((size, width), lambda step: (low // size + step, 0))

    blocks = [
        fixed(weights[0]),
        fixed(weights[1]),
        fixed(weights[2]),
        pl.BlockSpec((3, inner // steps, width), lambda step: (0, step, 0)),
        rows_of(inner),
        pl.BlockSpec((width // steps, hidden), lambda step: (step, 0)),
        rows_of(hidden),
        fixed(weights[7]),
    ]
    first = hidden + width
    shapes = [jax.ShapeDtypeStruct(weight.shape, FLOAT) for weight in weights]
    return pl.pallas_call(
        lambda *refs: adam_kernel(refs),
        grid=(steps,),
        in_specs=[fixed(stats), rows_of(hidden), rows_of(width, hidden)]
        + [rows_of(inner, first + part * inner) for part in range(4)]
        + [fixed(small)]
        + blocks * 3,
        out_specs=blocks * 3 + [pl.BlockSpec((1, 1), lambda step: (0, 0))] * 3,
        out_shape=shapes * 3 + [jax.ShapeDtypeStruct((1, 1), FLOAT)] * 3,
        compiler_params=pltpu.CompilerParams(vmem_limit_bytes=58 * 2**20),
        name="adam",
    )(stats, *[main] * 6, small, *weights, *firsts, *seconds)


def shards(
    ctx_feat,
    qry_feat,
    counts,
    ctx_bins,
    qry_bins,
    query_mask,
    w_embed,
    w_bins,
    norm_gains,
    w_qkv,
    w_out,
    w_up,
    w_down,
    w_head,
    m_embed,
    m_bins,
    m_gains,
    m_qkv,
    m_out,
    m_up,
    m_down,
    m_head,
    v_embed,
    v_bins,
    v_gains,
    v_qkv,
    v_out,
    v_up,
    v_down,
    v_head,
):
    sizes = {"tables": lax.axis_size("tables"), "heads": lax.axis_size("heads")}
    main, small, stats = train(
        sizes,
        dict(
            counts=counts.reshape(1, 1),
            ctx_feat=ctx_feat[0].T,
            qry_feat=qry_feat[0],
            ctx_bins=ctx_bins,
            qry_bins=qry_bins,
            query_mask=query_mask,
            w_embed=w_embed,
            w_bins=w_bins,
            gains=norm_gains,
            w_qkv_wide=jnp.swapaxes(w_qkv, 1, 2),
            w_out_wide=w_out,
            w_up_wide=w_up,
            w_down_wide=w_down,
            w_head=w_head.T,
        ),
    )
    results = adam_all(
        stats,
        main,
        small,
        *(
            (embed, bins, gains, jnp.swapaxes(qkv, 1, 2), out, up, down, head.T)
            for embed, bins, gains, qkv, out, up, down, head in (
                (w_embed, w_bins, norm_gains, w_qkv, w_out, w_up, w_down, w_head),
                (m_embed, m_bins, m_gains, m_qkv, m_out, m_up, m_down, m_head),
                (v_embed, v_bins, v_gains, v_qkv, v_out, v_up, v_down, v_head),
            )
        ),
    )
    *updated, loss, count, norm = results
    for low in range(0, 24, 8):
        updated[low + 3] = jnp.swapaxes(updated[low + 3], 1, 2)
        updated[low + 7] = updated[low + 7].T
    return (*updated, *(value.reshape(()) for value in (loss, count, norm)))


def solution(mesh):
    in_specs = (
        P("tables", "heads", None),
        P("tables", "heads", None),
        P("tables"),
        P("tables", "heads"),
        P("tables", "heads"),
        P("tables", "heads"),
        P(),
        P(),
        P(),
        P(None, None, "heads"),
        P("heads", None),
        P(None, "heads"),
        P("heads", None),
        P(),
        P(),
        P(),
        P(),
        P(None, None, "heads"),
        P("heads", None),
        P(None, "heads"),
        P("heads", None),
        P(),
        P(),
        P(),
        P(),
        P(None, None, "heads"),
        P("heads", None),
        P(None, "heads"),
        P("heads", None),
        P(),
    )
    out_specs = (
        P(),
        P(),
        P(),
        P(None, None, "heads"),
        P("heads", None),
        P(None, "heads"),
        P("heads", None),
        P(),
        P(),
        P(),
        P(),
        P(None, None, "heads"),
        P("heads", None),
        P(None, "heads"),
        P("heads", None),
        P(),
        P(),
        P(),
        P(),
        P(None, None, "heads"),
        P("heads", None),
        P(None, "heads"),
        P("heads", None),
        P(),
        P(),
        P(),
        P(),
    )
    return jax.shard_map(shards, mesh=mesh, in_specs=in_specs, out_specs=out_specs, check_vma=False)
```

```python
import functools

import jax
import jax.numpy as jnp
from jax import lax
from jax.experimental import pallas as pl
from jax.experimental.pallas import tpu as pltpu
from jax.sharding import PartitionSpec as P

HD = 64
BINS = 64
STEP = 10


NORM_EPS = 1e-05
ADAM_EPS = 1e-08
RATE = 0.05
RATE_WIDE = 1.0
BETA_ONE = 0.9
BETA_TWO = 0.95
DECAY = 0.1
CLIP_NORM = 0.02
MASKED = -1e30
FLOAT = jnp.float32
HALF = jnp.bfloat16
MESH = pl.DeviceIdType.MESH


def adam_update(weight, moment_one, moment_two, gradient, factor, rate, decay_rate):
    moment_one = BETA_ONE * moment_one + gradient * (factor * (1.0 - BETA_ONE))
    rooted = gradient * (factor * (1.0 - BETA_TWO) ** 0.5)
    moment_two = BETA_TWO * moment_two + rooted * rooted
    root = moment_two * lax.rsqrt(moment_two) * (1.0 - BETA_TWO**STEP) ** -0.5 + ADAM_EPS
    inverse = pl.reciprocal(root, approx=True)
    inverse = inverse * (2.0 - root * inverse)
    step = moment_one * inverse * (rate / (1.0 - BETA_ONE**STEP))
    weight = weight * (1.0 - rate * decay_rate) - step
    return (weight, moment_one, moment_two)


def place_bit(place, bit):
    return lax.rem(lax.div(place, bit), 2)


def flip(place, bit):
    return place + bit - 2 * bit * place_bit(place, bit)


def bits_of(size):
    return [1 << power for power in range(size.bit_length() - 1)]


def partner(places, axis, bit):
    other = dict(places)
    other[axis] = flip(places[axis], bit)
    return (other["tables"], other["heads"])


def greet(places, axes):
    barrier = pltpu.get_barrier_semaphore()
    across = (flip(flip(places["tables"], 2), 4), places["heads"])
    others = [partner(places, axis, bit) for axis, bit in axes] + [across]
    for other in others:
        pl.semaphore_signal(barrier, inc=1, device_id=other, device_id_type=MESH)
    pl.semaphore_wait(barrier, len(others))


class Copies:
    def __init__(self, sends, recvs):
        self.sends, self.recvs, self.used = sends, recvs, 0

    def make(self, source, target, device):
        self.used += 1
        return pltpu.make_async_remote_copy(
            src_ref=source,
            dst_ref=target,
            send_sem=self.sends.at[self.used - 1],
            recv_sem=self.recvs.at[self.used - 1],
            device_id=device,
            device_id_type=MESH,
        )

    def start(self, source, target, device):
        copy = self.make(source, target, device)
        copy.start()
        return copy


class Landing:
    def __init__(self, rows_ref):
        self.rows_ref, self.used = rows_ref, 0

    def take(self, rows):
        self.used += rows
        return self.rows_ref.at[pl.ds(self.used - rows, rows), :]


class Traffic:
    LATENCY = 4.0

    def __init__(self):
        self.now, self.free, self.flows = 0.0, {}, []

    def book(self, axis, bit, size):
        link, hops = ("core", 0.15) if (axis, bit) == ("heads", 1) else (axis + str(min(bit, 2)), 1)
        if axis == "tables" and bit > 2:
            hops = bit // 2
        self.free[link] = max(self.now, self.free.get(link, 0.0)) + hops * size * 2 / 1e5
        return self.free[link] + self.LATENCY * min(hops + 0.4, 1)

    def book_link(self, link, size):
        self.free[link] = max(self.now, self.free.get(link, 0.0)) + size * 2 / 1e5
        return self.free[link] + self.LATENCY

    def add(self, flow):
        self.flows.append(flow)
        flow.start()

    def waiting(self):
        return [flow for flow in self.flows if flow.sent]

    def step(self):
        flow = min(self.waiting(), key=lambda flow: flow.ready)
        self.now = max(self.now, flow.ready) + 0.3
        flow.advance()

    def spend(self, time):
        self.now += time
        while any(flow.ready <= self.now for flow in self.waiting()):
            self.step()

    def wait(self, *flows):
        while not all(flow.done() for flow in flows):
            self.step()


def stages_of(rows, axes, least):
    steps = []
    for axis, bit in axes:
        if rows // 2 >= least and rows % 32 == 0:
            rows //= 2
            steps.append((axis, bit, "halve", rows))
        else:
            steps.append((axis, bit, "whole", rows))
    back = [(axis, bit, "back", left) for axis, bit, kind, left in reversed(steps) if kind == "halve"]
    return steps + back


def landing_rows(steps):
    return sum(left for _, _, kind, left in steps if kind != "back")


class Sum:
    def __init__(self, copies, traffic, landing, buffer, result, start, steps, places, until=None):
        self.copies, self.traffic, self.landing = copies, traffic, landing
        self.buffer, self.result, self.low = buffer, result, start
        self.steps, self.places = steps, places
        self.until = len(steps) if until is None else until
        self.at, self.sent, self.landed, self.ready = 0, None, None, 0.0
        self.last, self.found = None, None

    def rows(self, low, count):
        if isinstance(low, int):
            return pl.ds(low, count)
        return pl.ds(pl.multiple_of(low, 16), count)

    def finish(self):
        if self.sent is None:
            return
        _, _, kind, count = self.steps[self.at - 1]
        self.sent.wait()
        self.sent = None
        if kind != "back":
            mine = self.rows(self.low, count)
            total = self.buffer[mine, :].astype(FLOAT) + self.landed[...].astype(FLOAT)
            last = self.at == len(self.steps) or self.steps[self.at][2] == "back"
            target = self.result if last else self.buffer
            target[mine, :] = total.astype(self.buffer.dtype)

    def start(self):
        if self.at >= self.until:
            return
        axis, bit, kind, count = self.steps[self.at]
        self.at += 1
        side = place_bit(self.places[axis], bit)
        if kind == "halve":
            source = self.buffer.at[self.rows(self.low + count * (1 - side), count), :]
            self.low = self.low + count * side
            target = self.landed = self.landing.take(count)
        elif kind == "whole":
            source = self.buffer.at[self.rows(self.low, count), :]
            target = self.landed = self.landing.take(count)
        else:
            source = target = self.result.at[self.rows(self.low, count), :]
            self.low = self.low - count * side
        self.sent = self.copies.start(source, target, partner(self.places, axis, bit))
        self.ready = self.traffic.book(axis, bit, count * self.buffer.shape[-1] * 2)

    def advance(self):
        self.finish()
        self.start()
        if self.last and self.done():
            self.found = self.last()

    def go_on(self):
        self.until = len(self.steps)
        self.start()

    def done(self):
        return self.at >= self.until and self.sent is None


def chain_steps(rows, sizes):
    half = rows // 2
    others, left = [], half
    for bit in bits_of(sizes["tables"])[3:]:
        if left % 32 == 0:
            left //= 2
            others.append(("pair", bit, "halve", left, "inner"))
        else:
            others.append(("pair", bit, "whole", left, "inner"))
    others = others + [
        (move, bit, "back", count, who)
        for move, bit, kind, count, who in reversed(others)
        if kind == "halve"
    ]
    return [
        ("pair", 1, "halve", half, "all"),
        ("in", 2, "in", half, "row"),
        ("swap", 4, "whole", half, "inner"),
        *others,
        ("out", 2, "out", half, "row"),
        ("pair", 1, "back", half, "all"),
    ]


def chain_landing(steps):
    return sum(
        count for move, bit, kind, count, who in steps[1:] if kind in ("halve", "whole", "in")
    )


class Chain:
    def __init__(self, copies, traffic, landing, buffer, result, start, steps, places):
        self.copies, self.traffic, self.landing = copies, traffic, landing
        self.buffer, self.result, self.low = buffer, result, start
        self.steps, self.places = steps, places
        self.at, self.sent, self.landed, self.ready = 0, None, None, 0.0
        self.last, self.found = None, None
        low, high = (place_bit(places["tables"], bit) for bit in (2, 4))
        self.inner = low + high == 1
        self.outer = low + high != 1

    def rows(self, low, count):
        if isinstance(low, int):
            return pl.ds(low, count)
        return pl.ds(pl.multiple_of(low, 16), count)

    def add(self, count):
        mine = self.rows(self.low, count)
        total = self.buffer[mine, :].astype(FLOAT) + self.landed[...].astype(FLOAT)
        last = not any(step[2] in ("halve", "whole", "in") for step in self.steps[self.at :])
        target = self.result if last else self.buffer
        target[mine, :] = total.astype(self.buffer.dtype)

    def finish(self):
        if self.sent is None:
            return
        move, _, kind, count, who = self.steps[self.at - 1]
        sent, self.sent = self.sent, None
        if who == "row":
            senders, getters = (
                (self.outer, self.inner) if move == "in" else (self.inner, self.outer)
            )

            @pl.when(senders)
            def _():
                sent.wait_send()

            @pl.when(getters)
            def _():
                sent.wait_recv()
                if move == "in":
                    self.add(count)

        elif who == "inner":

            @pl.when(self.inner)
            def _():
                sent.wait()
                if kind != "back":
                    self.add(count)

        else:
            sent.wait()
            if kind != "back":
                self.add(count)

    def start(self):
        if self.at >= len(self.steps):
            return
        move, bit, kind, count, who = self.steps[self.at]
        first = self.at == 0
        self.at += 1
        place = self.places["tables"]
        side = place_bit(place, bit)
        other = flip(flip(place, 2), 4) if move == "swap" else flip(place, bit)
        if kind == "halve":
            given = self.rows(self.low + count * (1 - side), count)
            self.low = self.low + count * side
        else:
            given = self.rows(self.low, count)
        if kind in ("back", "out"):
            source = target = self.result.at[given, :]
        elif first:
            source, target = self.buffer.at[given, :], self.result.at[given, :]
            self.landed = self.result.at[self.rows(self.low, count), :]
        else:
            source = self.buffer.at[given, :]
            target = self.landed = self.landing.take(count)
        if kind == "back":
            self.low = self.low - count * side
        copy = self.copies.make(source, target, (other, self.places["heads"]))
        if who == "all":
            copy.start()
        else:
            senders = self.outer if move == "in" else self.inner

            @pl.when(senders)
            def _():
                copy.start()

        self.sent = copy
        link = move if move != "pair" else "tables" + str(min(bit, 2))
        self.ready = self.traffic.book_link(link, count * self.buffer.shape[-1] * 2)

    def advance(self):
        self.finish()
        self.start()
        if self.last and self.done():
            self.found = self.last()

    def done(self):
        return self.at >= len(self.steps) and self.sent is None


class Gather:
    def __init__(self, copies, traffic, views, size, places, bits):
        self.copies, self.traffic, self.views, self.size = copies, traffic, views, size
        self.places, self.bits = places, bits
        self.at, self.held, self.sent, self.ready = 0, [places["heads"]], [], 0.0

    def advance(self):
        self.finish()
        self.start()

    def finish(self):
        for copy in self.sent:
            copy.wait()
        if self.sent:
            self.held = self.held + [flip(slot, self.bits[self.at - 1]) for slot in self.held]
        self.sent = []

    def start(self):
        if self.at < len(self.bits):
            bit = self.bits[self.at]
            other = partner(self.places, "heads", bit)
            self.sent = [
                self.copies.start(view(slot), view(slot), other)
                for slot in self.held
                for view in self.views
            ]
            self.ready = self.traffic.book("heads", bit, self.size * len(self.held))
            self.at += 1

    def done(self):
        return self.at >= len(self.bits) and not self.sent


def places_here():
    return {"tables": lax.axis_index("tables"), "heads": lax.axis_index("heads")}


SMALL = {"head": (0, 64), "bins": (64, 64), "embed": (128, 112), "gains": (240, 16)}
SMALL_ROWS = 256
CHUNK = 256
SPAN = 2


def dot(left, right, over=(1, 0)):
    return lax.dot_general(
        left, right, (((over[0],), (over[1],)), ((), ())), preferred_element_type=FLOAT
    )


def standard(rows):
    center = rows - jnp.mean(rows, axis=-1, keepdims=True)
    scale = lax.rsqrt(jnp.mean(center * center, axis=-1, keepdims=True) + NORM_EPS)
    return center * scale, scale


def standard_back(upstream, gain_row, unit, scale):
    inner = upstream * gain_row
    lean = jnp.mean(inner, axis=-1, keepdims=True)
    tilt = jnp.mean(inner * unit, axis=-1, keepdims=True)
    return (inner - lean - unit * tilt) * scale


def as_row(column):
    return jnp.broadcast_to(column, (column.shape[0], 128)).T[:1]


def as_column(row):
    return jnp.broadcast_to(row, (8, row.shape[1])).T[:, :1]


def column_sums(rows):
    return jnp.sum(rows, axis=0, keepdims=True)


def gelu_both(hidden):
    root = 0.7978845608028654
    square = hidden * hidden
    bent = jnp.tanh(root * hidden * (1.0 + 0.044715 * square))
    half = 0.5 * (1.0 + bent)
    slope = half + 0.5 * hidden * (1.0 - bent * bent) * root * (1.0 + 0.134145 * square)
    return hidden * half, slope


def sum_squares(rows_ref, low, count):
    def piece(step, total):
        part = rows_ref[pl.ds(pl.multiple_of(low + step * 64, 64), 64), :].astype(FLOAT)
        return total + jnp.sum((part * part).reshape(8, 8, part.shape[1]), axis=0)

    return lax.fori_loop(0, count // 64, piece, jnp.zeros((8, rows_ref.shape[1]), FLOAT))


def one_value(total):
    return jnp.sum(jnp.sum(total, axis=0, keepdims=True), axis=1, keepdims=True)


class Named:
    pass


def train_kernel(shape, r):
    groups, ctx, qry, width, inner, hidden = (
        shape.groups,
        shape.ctx,
        shape.qry,
        shape.width,
        shape.inner,
        shape.hidden,
    )
    heads = inner // HD
    total_ctx, total_qry = groups * ctx, groups * qry
    block = SPAN * qry
    blocks = total_qry // block
    half = width // 2
    places = places_here()
    me = places["heads"]
    copies = Copies(r.sends, r.recvs)
    traffic = Traffic()
    over_heads, over_tables = shape.over_heads, shape.over_tables
    far_first = [bit for _, bit in reversed(over_heads)]
    tiny = Landing(r.tiny_land)
    wide = Landing(r.wide_land)
    narrow = Landing(r.narrow_land)
    def stage(number, source, target):
        copy = pltpu.make_async_copy(source, target, r.locals.at[number])
        copy.start()
        return copy

    low = 3 * inner
    loads = [
        stage(part, r.w_qkv_wide.at[part], r.back.at[pl.ds(part * inner, inner), :])
        for part in range(3)
    ]
    loads.append(stage(3, r.w_out_wide, r.small.at[pl.ds(0, inner), :]))

    def load_halves(number, source):
        rest = source.shape[0] - low
        return [
            stage(number, source.at[pl.ds(0, low), :], r.back.at[pl.ds(0, low), :]),
            stage(number + 1, source.at[pl.ds(low, rest), :], r.small.at[pl.ds(0, rest), :]),
        ]

    def take_halves(copies_in, target):
        rest = target.shape[0] - low
        for copy in copies_in:
            copy.wait()
        target[pl.ds(0, low), :] = r.back[pl.ds(0, low), :].astype(HALF)
        target[pl.ds(low, rest), :] = r.small[pl.ds(0, rest), :].astype(HALF)

    greet(places, over_heads + over_tables)

    r.feat[me, pl.ds(0, ctx), :] = r.ctx_feat[...].astype(FLOAT).T.astype(HALF)
    r.feat[me, pl.ds(ctx, qry), :] = r.qry_feat[...]
    r.ints[me] = jnp.zeros((8, ctx), jnp.int32)
    r.ints[me, 0:1, :] = r.ctx_bins[...]
    r.ints[me, 1:2, pl.ds(0, qry)] = r.qry_bins[...]
    r.ints[me, 2:3, pl.ds(0, qry)] = r.query_mask[...]
    rows_in = Gather(
        copies,
        traffic,
        [lambda slot: r.feat.at[slot], lambda slot: r.ints.at[slot]],
        (ctx + qry) * 256 + ctx * 32,
        places,
        far_first,
    )
    traffic.add(rows_in)
    mask_sum = jnp.sum(r.query_mask[...].astype(FLOAT), axis=1, keepdims=True)
    r.count_work[...] = jnp.broadcast_to(mask_sum, (16, 128))
    tiny_steps = stages_of(16, over_heads + over_tables, 16)
    counted = Sum(copies, traffic, tiny, r.count_work, r.count, 0, tiny_steps, places)
    traffic.add(counted)
    for copy in loads:
        copy.wait()
    for part in range(3):
        r.w_qkv[part] = r.back[pl.ds(part * inner, inner), :].astype(HALF)
    r.out_all[me] = r.small[pl.ds(0, inner), :].astype(HALF)
    loads = load_halves(4, r.w_up_wide)
    outs_in = Gather(
        copies, traffic, [lambda slot: r.out_all.at[slot]], inner * width * 2, places, far_first
    )

    embed_half = r.w_embed[...].astype(HALF)
    bins_half = r.w_bins[...].astype(HALF)
    gain_one, gain_two, gain_last = (r.gains[row : row + 1, :] for row in range(3))
    bin_rows = lax.broadcasted_iota(jnp.int32, (BINS, 256), 0)

    def one_hot(slot, place):
        return jnp.where(
            bin_rows == r.ints[slot, 0:1, pl.ds(pl.multiple_of(place * 256, 256), 256)], 1.0, 0.0
        ).astype(HALF)

    def embed_shard(slot):
        def context(place, _):
            at = pl.multiple_of(slot * ctx + place * 256, 256)
            feat = r.feat[slot, pl.ds(pl.multiple_of(place * 256, 256), 256), :]
            zero = dot(feat, embed_half) + dot(one_hot(slot, place), bins_half, (0, 0))
            unit, scale = standard(zero)
            normed = (unit * gain_one).astype(HALF)
            r.normed_ctx[pl.ds(at, 256), :] = normed
            r.scale_ctx[pl.ds(slot * (ctx // 256) + place, 1), :] = as_row(scale)
            keys = dot(normed, r.w_qkv[1], (1, 1))
            values = dot(normed, r.w_qkv[2], (1, 1))
            r.keys[pl.ds(at, 256), :] = keys.astype(HALF)
            r.values[pl.ds(at, 256), :] = values.astype(HALF)
            r.keys_t[:, pl.ds(at, 256)] = keys.T.astype(HALF)
            r.values_t[:, pl.ds(at, 256)] = values.T.astype(HALF)
            return 0

        lax.fori_loop(0, ctx // 256, context, 0)
        at = pl.multiple_of(slot * qry, 16)
        zero = dot(r.feat[slot, pl.ds(ctx, qry), :], embed_half)
        r.stream[pl.ds(at, qry), :] = zero
        unit, scale = standard(zero)
        normed = (unit * gain_one).astype(HALF)
        r.normed_qry[pl.ds(at, qry), :] = normed
        r.scale_qry[pl.ds(slot, 1), :] = as_row(scale)
        queries = dot(normed, r.w_qkv[0], (1, 1))
        r.queries[pl.ds(at, qry), :] = queries.astype(HALF)
        r.queries_t[slot] = queries.T.astype(HALF)

    done = 0
    while done < groups:
        for slot in rows_in.held[done:]:
            embed_shard(slot)
            done += 1
            traffic.spend(2.0)
            if done == 1:
                traffic.add(outs_in)
                take_halves(loads, r.w_up)
                loads = load_halves(6, r.w_down_wide)
            if done == 2:
                take_halves(loads, r.w_down)
        if done == len(rows_in.held) and done < groups:
            traffic.step()

    lane = lax.broadcasted_iota(jnp.int32, (1, inner), 1)
    head_rows = [
        jnp.where((lane >= h * HD) & (lane < (h + 1) * HD), 1.0, 0.0).astype(FLOAT)
        for h in range(heads)
    ]
    slots_at = lax.broadcasted_iota(jnp.int32, (1, total_ctx), 1)
    dead = jnp.where(slots_at < r.counts[0:1, 0:1], 0.0, MASKED)
    mixing = []
    for b in range(groups):
        rows = pl.ds(b * qry, qry)
        query_blk = r.queries[rows, :]
        mixed = jnp.zeros((qry, inner), FLOAT)
        for h in range(heads):
            raw = dot(query_blk * (head_rows[h] * HD**-0.5).astype(HALF), r.keys_t[...]) + dead
            raised = jnp.exp(raw - jnp.max(raw, axis=-1, keepdims=True))
            weights = (raised * (1.0 / jnp.sum(raised, axis=-1, keepdims=True))).astype(HALF)
            r.weights[h, rows, :] = weights
            mixed = mixed + dot(weights, r.values[...]) * head_rows[h]
        r.mixed[rows, :] = mixed
        r.mix_all[me, b] = mixed.astype(HALF)
        mixing.append(
            Gather(
                copies,
                traffic,
                [lambda slot, b=b: r.mix_all.at[slot, b]],
                qry * 512,
                places,
                far_first,
            )
        )
        traffic.add(mixing[-1])
        traffic.spend(2.0)

    sum_steps = stages_of(2 * block, over_heads, block)
    down_sums, back_sums = [], []
    for b in range(blocks):
        traffic.wait(outs_in, *mixing[SPAN * b : SPAN * (b + 1)])
        rows = pl.ds(b * block, block)
        attended = []
        for part in range(SPAN * b, SPAN * (b + 1)):
            total = dot(r.mix_all[0, part], r.out_all[0])
            for slot in range(1, groups):
                total = total + dot(r.mix_all[slot, part], r.out_all[slot])
            attended.append(total)
        stream = r.stream[rows, :] + jnp.concatenate(attended, axis=0)
        r.stream[rows, :] = stream
        unit, _ = standard(stream)
        normed = (unit * gain_two).astype(HALF)
        r.normed_two[rows, :] = normed
        active, slope = gelu_both(dot(normed, r.w_up[...]))
        active = active.astype(HALF)
        r.active[rows, :] = active
        r.slope[rows, :] = slope.astype(HALF)
        low = pl.ds(2 * b * block, block)
        high = pl.ds((2 * b + 1) * block, block)
        part = dot(active, r.w_down[...]).astype(HALF)
        r.down_work[low, :] = part[:, :half]
        r.down_work[high, :] = part[:, half:]
        down_sums.append(
            Sum(copies, traffic, narrow, r.down_work, r.down_sum, 2 * b * block, sum_steps, places)
        )
        traffic.add(down_sums[-1])
        traffic.spend(2.0)

    mains = []

    def send_chunk(place):
        start = CHUNK * place
        part = Chain(
            copies, traffic, wide, r.main_work, r.main, start, shape.main_steps, places
        )
        part.last = functools.partial(sum_squares, r.main, start, CHUNK)
        mains.append(part)
        traffic.add(part)
        traffic.spend(0.5)

    head_half = r.w_head[...].astype(HALF)
    traffic.wait(counted)
    divisor = jnp.maximum(r.count[0:1, 0:1], 1.0)
    tall = lax.broadcasted_iota(jnp.int32, (BINS, 256), 0)
    loss = jnp.zeros((1, 1), FLOAT)
    grad_head = jnp.zeros((BINS, width), FLOAT)
    gain_sum_last = jnp.zeros((1, width), FLOAT)
    for b in range(blocks):
        traffic.wait(counted, down_sums[b])
        rows = pl.ds(b * block, block)
        low = pl.ds(2 * b * block, block)
        high = pl.ds((2 * b + 1) * block, block)
        mlp = jnp.concatenate([r.down_sum[low, :], r.down_sum[high, :]], axis=1)
        unit, scale = standard(r.stream[rows, :] + mlp.astype(FLOAT))
        normed = (unit * gain_last).astype(HALF)
        logits = dot(normed, head_half, (1, 1))
        targets, masks = [], []
        for slot in range(SPAN * b, SPAN * (b + 1)):
            target = jnp.where(tall == r.ints[slot, 1:2, 0:256], 1.0, 0.0)
            targets.append(target.T[:qry])
            mask = jnp.broadcast_to(r.ints[slot, 2:3, 0:256].astype(FLOAT), (8, 256))
            masks.append(mask.T[:qry, :1])
        target = jnp.concatenate(targets, axis=0)
        mask = jnp.concatenate(masks, axis=0)
        top = jnp.max(logits, axis=-1, keepdims=True)
        log_bins = top + jnp.log(jnp.sum(jnp.exp(logits - top), axis=-1, keepdims=True))
        missed = log_bins - jnp.sum(target * logits, axis=-1, keepdims=True)
        loss = loss + jnp.sum(mask * missed, axis=0, keepdims=True)
        back_logits = (mask * (jnp.exp(logits - log_bins) - target) / divisor).astype(HALF)
        grad_head = grad_head + dot(back_logits, normed, (0, 0))
        back_final = dot(back_logits, head_half)
        gain_sum_last = gain_sum_last + column_sums(back_final * unit)
        back_two = standard_back(back_final, gain_last, unit, scale)
        r.back[rows, :] = back_two
        back_mlp = back_two.astype(HALF)
        r.back_mlp[rows, :] = back_mlp
        back_active = dot(back_mlp, r.w_down[...], (1, 1))
        back_up = (r.slope[rows, :].astype(FLOAT) * back_active).astype(HALF)
        r.back_up[rows, :] = back_up
        part = dot(back_up, r.w_up[...], (1, 1)).astype(HALF)
        r.down_work[low, :] = part[:, :half]
        r.down_work[high, :] = part[:, half:]
        back_sums.append(
            Sum(copies, traffic, narrow, r.down_work, r.down_sum, 2 * b * block, sum_steps, places)
        )
        traffic.add(back_sums[-1])
        traffic.spend(3.0)
    r.loss_work[...] = jnp.broadcast_to(loss / groups, (16, 128))
    losses = Sum(copies, traffic, tiny, r.loss_work, r.loss, 0, tiny_steps, places)
    traffic.add(losses)
    r.small[pl.ds(0, BINS), :] = grad_head / groups

    for place in range(hidden // CHUNK):
        at = pl.ds(place * CHUNK, CHUNK)
        r.main_work[at, :] = dot(r.active[:, at], r.back_mlp[...], (0, 0)).astype(HALF)
        send_chunk(len(mains))
    for place in range(width // CHUNK):
        at = pl.ds(place * CHUNK, CHUNK)
        to = pl.ds(hidden + place * CHUNK, CHUNK)
        r.main_work[to, :] = dot(r.normed_two[:, at], r.back_up[...], (0, 0)).astype(HALF)
        send_chunk(len(mains))

    gain_sum_two = jnp.zeros((1, width), FLOAT)
    r.keys_back[...] = jnp.zeros(r.keys_back.shape, FLOAT)
    r.values_back[...] = jnp.zeros(r.values_back.shape, FLOAT)
    for b in range(blocks):
        traffic.wait(back_sums[b])
        rows = pl.ds(b * block, block)
        low = pl.ds(2 * b * block, block)
        high = pl.ds((2 * b + 1) * block, block)
        upstream = jnp.concatenate([r.down_sum[low, :], r.down_sum[high, :]], axis=1).astype(FLOAT)
        unit, scale = standard(r.stream[rows, :])
        gain_sum_two = gain_sum_two + column_sums(upstream * unit)
        back_one = r.back[rows, :] + standard_back(upstream, gain_two, unit, scale)
        r.back[rows, :] = back_one
        back_attn = back_one.astype(HALF)
        r.slope[rows, :] = back_attn
        back_mix = dot(back_attn, r.out_all[me], (1, 1)).astype(HALF)
        r.back_mix[rows, :] = back_mix
        turned = back_mix.astype(FLOAT)
        for part in range(SPAN):
            r.back_mix_t[SPAN * b + part] = turned[part * qry : (part + 1) * qry].T.astype(HALF)
        traffic.spend(1.5)
        for h in range(heads):

            def backward(part, _, h=h):
                here = SPAN * b + part
                at = pl.ds(pl.multiple_of(here * qry, 16), qry)
                back_mix = r.back_mix[at, :]
                mine = back_mix * head_rows[h].astype(HALF)
                lean = jnp.sum(
                    mine.astype(FLOAT) * r.mixed[at, :], axis=-1, keepdims=True
                )
                weights = r.weights[h, at, :]
                back_weights = dot(mine, r.values_t[...])
                back_scores = (weights.astype(FLOAT) * (back_weights - lean)).astype(HALF)
                queries_back = dot(back_scores, r.keys[...]) * (head_rows[h] * HD**-0.5)
                if h == 0:
                    r.queries_back[at, :] = queries_back
                else:
                    r.queries_back[at, :] += queries_back
                lanes = pl.ds(h * HD, HD)
                r.values_back[lanes, :] += dot(r.back_mix_t[here, lanes, :], weights)
                r.keys_back[lanes, :] += dot(r.queries_t[here, lanes, :], back_scores)
                return 0

            lax.fori_loop(0, SPAN, backward, 0)
            traffic.spend(1.7)

    first = hidden + width
    pieces = [
        lambda: dot(r.mix_all[me].reshape(total_qry, inner), r.slope[...], (0, 0)),
        lambda: dot(r.queries_back[...].astype(HALF), r.normed_qry[...], (0, 0)),
        lambda: dot((r.keys_back[...] * HD**-0.5).astype(HALF), r.normed_ctx[...]),
        lambda: dot(r.values_back[...].astype(HALF), r.normed_ctx[...]),
    ]
    for place, piece in enumerate(pieces):
        r.main_work[pl.ds(first + place * inner, inner), :] = piece().astype(HALF)
        while (len(mains) + 1) * CHUNK <= first + (place + 1) * inner:
            send_chunk(len(mains))
        traffic.spend(0.7)

    over_gain = 1.0 / gain_one
    low_bins, low_embed, low_gains = (SMALL[name][0] for name in ("bins", "embed", "gains"))
    features = r.w_embed.shape[0]
    r.small[pl.ds(BINS, SMALL_ROWS - BINS), :] = jnp.zeros((SMALL_ROWS - BINS, width), FLOAT)
    bins_at = pl.ds(low_bins, BINS)
    embed_at = pl.ds(low_embed, features)

    def embed_back(upstream, normed, scale):
        unit = normed.astype(FLOAT) * over_gain
        return column_sums(upstream * unit), standard_back(upstream, gain_one, unit, scale)

    def context_back(place, gain_sum):
        slot, offset = lax.div(place, ctx // 256), lax.rem(place, ctx // 256)
        at = pl.ds(pl.multiple_of(place * 256, 256), 256)
        keys = (r.keys_back[:, at] * HD**-0.5).T.astype(HALF)
        values = r.values_back[:, at].T.astype(HALF)
        upstream = dot(keys, r.w_qkv[1]) + dot(values, r.w_qkv[2])
        gains, back_zero = embed_back(upstream, r.normed_ctx[at, :], as_column(r.scale_ctx[pl.ds(place, 1), :]))
        back_zero = back_zero.astype(HALF)
        feat = r.feat[slot, pl.ds(pl.multiple_of(offset * 256, 256), 256), :]
        r.small[embed_at, :] += dot(feat, back_zero, (0, 0))
        r.small[bins_at, :] += dot(one_hot(slot, offset), back_zero)
        return gain_sum + gains

    gain_sum_one = jnp.zeros((1, width), FLOAT)
    pieces = total_ctx // 256
    for part in range(2):
        gain_sum_one = lax.fori_loop(
            part * pieces // 2, (part + 1) * pieces // 2, context_back, gain_sum_one
        )
        traffic.spend(2.0)

    def query_back(slot, gain_sum):
        at = pl.ds(pl.multiple_of(slot * qry, 16), qry)
        upstream = dot(r.queries_back[at, :].astype(HALF), r.w_qkv[0])
        gains, back_zero = embed_back(upstream, r.normed_qry[at, :], as_column(r.scale_qry[pl.ds(slot, 1), :]))
        mine = jnp.where(slot == me, 1.0, 0.0)
        back_zero = (back_zero + mine * r.back[at, :]).astype(HALF)
        feat = r.feat[slot, pl.ds(ctx, qry), :]
        r.small[embed_at, :] += dot(feat, back_zero, (0, 0))
        return gain_sum + gains

    gain_sum_one = lax.fori_loop(0, groups, query_back, gain_sum_one)
    r.small[pl.ds(low_gains, 1), :] = gain_sum_one
    r.small[pl.ds(low_gains + 1, 1), :] = gain_sum_two / groups
    r.small[pl.ds(low_gains + 2, 1), :] = gain_sum_last / groups
    r.small_work[...] = r.small[...].astype(HALF)

    small_steps = stages_of(SMALL_ROWS, over_heads + over_tables, 64)
    pause = len(small_steps) - len(over_heads)
    smalls = Sum(
        copies, traffic, wide, r.small_work, r.small_out, 0, small_steps, places, until=pause
    )
    traffic.add(smalls)
    traffic.wait(smalls, losses, *mains)
    squares = one_value(sum(part.found for part in mains))
    r.square_work[...] = jnp.broadcast_to(squares, (16, 128))
    square_steps = stages_of(16, list(reversed(over_heads)), 16)
    squared = Sum(copies, traffic, tiny, r.square_work, r.square, 0, square_steps, places)
    smalls.go_on()
    traffic.add(squared)
    traffic.wait(squared, smalls)
    squares = r.square[0:8, :] + one_value(sum_squares(r.small_out, 0, SMALL_ROWS))
    row = lax.broadcasted_iota(jnp.int32, (8, 128), 0)
    r.stats[...] = jnp.where(row == 0, squares, jnp.where(row == 1, r.loss[0:8, :], r.count[0:8, :]))


def train(sizes, inputs):
    shape = Named()
    shape.groups = sizes["heads"]
    features, shape.ctx = inputs["ctx_feat"].shape
    shape.qry = inputs["qry_feat"].shape[0]
    shape.width = inputs["w_embed"].shape[1]
    shape.inner = inputs["w_out_wide"].shape[0]
    shape.hidden = inputs["w_up_wide"].shape[1]
    shape.over_tables = [("tables", bit) for bit in bits_of(sizes["tables"])]
    shape.over_heads = [("heads", bit) for bit in bits_of(sizes["heads"])]
    groups, ctx, qry, width, inner, hidden = (
        shape.groups,
        shape.ctx,
        shape.qry,
        shape.width,
        shape.inner,
        shape.hidden,
    )
    total_ctx, total_qry = groups * ctx, groups * qry
    heads = inner // HD
    main_rows = hidden + width + 4 * inner
    block = SPAN * qry
    shape.main_steps = chain_steps(CHUNK, sizes)
    small_steps = stages_of(SMALL_ROWS, shape.over_heads + shape.over_tables, 64)
    sum_steps = stages_of(2 * block, shape.over_heads, block)
    wide_rows = main_rows // CHUNK * chain_landing(shape.main_steps) + landing_rows(small_steps)
    narrow_rows = 2 * (total_qry // block) * landing_rows(sum_steps)
    every = len(shape.over_tables) + len(shape.over_heads)
    tiny_rows = 16 * (2 * every + len(shape.over_heads))
    tiny = ((16, 128), FLOAT)
    scratch = dict(
        w_qkv=((3, inner, width), HALF),
        w_up=((width, hidden), HALF),
        w_down=((hidden, width), HALF),
        feat=((groups, ctx + qry, features), HALF),
        ints=((groups, 8, ctx), jnp.int32),
        out_all=((groups, inner, width), HALF),
        count_work=tiny,
        count=tiny,
        loss_work=tiny,
        loss=tiny,
        square_work=tiny,
        square=tiny,
        normed_ctx=((total_ctx, width), HALF),
        scale_ctx=((total_ctx // 256, 256), FLOAT),
        normed_qry=((total_qry, width), HALF),
        scale_qry=((groups, qry), FLOAT),
        stream=((total_qry, width), FLOAT),
        queries=((total_qry, inner), HALF),
        queries_t=((groups, inner, qry), HALF),
        keys=((total_ctx, inner), HALF),
        values=((total_ctx, inner), HALF),
        keys_t=((inner, total_ctx), HALF),
        values_t=((inner, total_ctx), HALF),
        weights=((heads, total_qry, total_ctx), HALF),
        mixed=((total_qry, inner), FLOAT),
        mix_all=((groups, groups, qry, inner), HALF),
        normed_two=((total_qry, width), HALF),
        active=((total_qry, hidden), HALF),
        slope=((total_qry, hidden), HALF),
        down_work=((2 * total_qry, width // 2), HALF),
        down_sum=((2 * total_qry, width // 2), HALF),
        back=((total_qry, width), FLOAT),
        back_mlp=((total_qry, width), HALF),
        back_up=((total_qry, hidden), HALF),
        back_mix=((total_qry, inner), HALF),
        back_mix_t=((groups, inner, qry), HALF),
        queries_back=((total_qry, inner), FLOAT),
        keys_back=((inner, total_ctx), FLOAT),
        values_back=((inner, total_ctx), FLOAT),
        main_work=((main_rows, width), HALF),
        small=((SMALL_ROWS, width), FLOAT),
        small_work=((SMALL_ROWS, width), HALF),
        wide_land=((wide_rows, width), HALF),
        narrow_land=((narrow_rows, width // 2), HALF),
        tiny_land=((tiny_rows, 128), FLOAT),
    )
    outputs = dict(
        main=jax.ShapeDtypeStruct((main_rows, width), HALF),
        small_out=jax.ShapeDtypeStruct((SMALL_ROWS, width), HALF),
        stats=jax.ShapeDtypeStruct((8, 128), FLOAT),
    )
    names = list(inputs) + list(outputs) + list(scratch) + ["sends", "recvs", "locals"]

    def kernel(*refs):
        named = Named()
        named.__dict__.update(zip(names, refs))
        train_kernel(shape, named)

    whole = pl.BlockSpec(memory_space=pltpu.VMEM)
    semaphores = pltpu.SemaphoreType.DMA((192,))
    return pl.pallas_call(
        kernel,
        out_shape=tuple(outputs.values()),
        in_specs=[
            pl.BlockSpec(memory_space=pl.ANY) if name.endswith("_wide") else whole
            for name in inputs
        ],
        out_specs=(whole,) * 3,
        scratch_shapes=[pltpu.VMEM(size, kind) for size, kind in scratch.values()]
        + [semaphores, semaphores, pltpu.SemaphoreType.DMA((8,))],
        compiler_params=pltpu.CompilerParams(
            collective_id=1, has_side_effects=True, vmem_limit_bytes=62 * 2**20
        ),
        name="train",
    )(*inputs.values())


def adam_kernel(refs):
    (stats, main_d, main_u, main_o, main_q, main_k, main_v, small) = refs[:8]
    w = refs[8:16]
    m = refs[16:24]
    v = refs[24:32]
    w_new = refs[32:40]
    m_new = refs[40:48]
    v_new = refs[48:56]
    loss, count, norm_out = refs[56:59]
    norm = jnp.sqrt(stats[0:1, 0:1])
    factor = jnp.minimum(1.0, CLIP_NORM / (norm + 1e-06))

    def update(which, gradient, rate, decay, at=...):
        gradient = gradient.astype(FLOAT)
        moments = (m[which][at], v[which][at], gradient, factor)
        results = adam_update(w[which][at], *moments, rate, decay)
        for target, value in zip((w_new, m_new, v_new), results):
            target[which][at] = value

    update(6, main_d[...], RATE, DECAY)
    update(5, main_u[...], RATE, DECAY)
    update(4, main_o[...], RATE_WIDE, DECAY)
    for part, gradient in enumerate((main_q, main_k, main_v)):
        update(3, gradient[...], RATE, DECAY, at=part)

    @pl.when(pl.program_id(0) == 0)
    def _():
        loss[...] = stats[1:2, 0:1]
        count[...] = stats[2:3, 0:1]
        norm_out[...] = norm

        def rows(name, count):
            low, size = SMALL[name]
            return small[low : low + size, :].astype(FLOAT)[:count]

        update(0, rows("embed", w[0].shape[0]), RATE, DECAY)
        update(1, rows("bins", w[1].shape[0]), RATE_WIDE, DECAY)
        update(2, rows("gains", w[2].shape[0]), RATE_WIDE, 0.0)
        update(7, rows("head", w[7].shape[0]), RATE, DECAY)


def adam_all(stats, main, small, weights, firsts, seconds):
    inner, width = weights[4].shape
    hidden = weights[5].shape[1]
    steps = 4

    def fixed(array):
        return pl.BlockSpec(array.shape, lambda step: (0,) * array.ndim)

    def rows_of(rows, low=0):
        size = rows // steps
        return pl.BlockSpec((size, width), lambda step: (low // size + step, 0))

    blocks = [
        fixed(weights[0]),
        fixed(weights[1]),
        fixed(weights[2]),
        pl.BlockSpec((3, inner // steps, width), lambda step: (0, step, 0)),
        rows_of(inner),
        pl.BlockSpec((width // steps, hidden), lambda step: (step, 0)),
        rows_of(hidden),
        fixed(weights[7]),
    ]
    first = hidden + width
    shapes = [jax.ShapeDtypeStruct(weight.shape, FLOAT) for weight in weights]
    return pl.pallas_call(
        lambda *refs: adam_kernel(refs),
        grid=(steps,),
        in_specs=[fixed(stats), rows_of(hidden), rows_of(width, hidden)]
        + [rows_of(inner, first + part * inner) for part in range(4)]
        + [fixed(small)]
        + blocks * 3,
        out_specs=blocks * 3 + [pl.BlockSpec((1, 1), lambda step: (0, 0))] * 3,
        out_shape=shapes * 3 + [jax.ShapeDtypeStruct((1, 1), FLOAT)] * 3,
        compiler_params=pltpu.CompilerParams(vmem_limit_bytes=58 * 2**20),
        name="adam",
    )(stats, *[main] * 6, small, *weights, *firsts, *seconds)


def shards(
    ctx_feat,
    qry_feat,
    counts,
    ctx_bins,
    qry_bins,
    query_mask,
    w_embed,
    w_bins,
    norm_gains,
    w_qkv,
    w_out,
    w_up,
    w_down,
    w_head,
    m_embed,
    m_bins,
    m_gains,
    m_qkv,
    m_out,
    m_up,
    m_down,
    m_head,
    v_embed,
    v_bins,
    v_gains,
    v_qkv,
    v_out,
    v_up,
    v_down,
    v_head,
):
    sizes = {"tables": lax.axis_size("tables"), "heads": lax.axis_size("heads")}
    main, small, stats = train(
        sizes,
        dict(
            counts=counts.reshape(1, 1),
            ctx_feat=ctx_feat[0].T,
            qry_feat=qry_feat[0],
            ctx_bins=ctx_bins,
            qry_bins=qry_bins,
            query_mask=query_mask,
            w_embed=w_embed,
            w_bins=w_bins,
            gains=norm_gains,
            w_qkv_wide=jnp.swapaxes(w_qkv, 1, 2),
            w_out_wide=w_out,
            w_up_wide=w_up,
            w_down_wide=w_down,
            w_head=w_head.T,
        ),
    )
    results = adam_all(
        stats,
        main,
        small,
        *(
            (embed, bins, gains, jnp.swapaxes(qkv, 1, 2), out, up, down, head.T)
            for embed, bins, gains, qkv, out, up, down, head in (
                (w_embed, w_bins, norm_gains, w_qkv, w_out, w_up, w_down, w_head),
                (m_embed, m_bins, m_gains, m_qkv, m_out, m_up, m_down, m_head),
                (v_embed, v_bins, v_gains, v_qkv, v_out, v_up, v_down, v_head),
            )
        ),
    )
    *updated, loss, count, norm = results
    for low in range(0, 24, 8):
        updated[low + 3] = jnp.swapaxes(updated[low + 3], 1, 2)
        updated[low + 7] = updated[low + 7].T
    return (*updated, *(value.reshape(()) for value in (loss, count, norm)))


def solution(mesh):
    in_specs = (
        P("tables", "heads", None),
        P("tables", "heads", None),
        P("tables"),
        P("tables", "heads"),
        P("tables", "heads"),
        P("tables", "heads"),
        P(),
        P(),
        P(),
        P(None, None, "heads"),
        P("heads", None),
        P(None, "heads"),
        P("heads", None),
        P(),
        P(),
        P(),
        P(),
        P(None, None, "heads"),
        P("heads", None),
        P(None, "heads"),
        P("heads", None),
        P(),
        P(),
        P(),
        P(),
        P(None, None, "heads"),
        P("heads", None),
        P(None, "heads"),
        P("heads", None),
        P(),
    )
    out_specs = (
        P(),
        P(),
        P(),
        P(None, None, "heads"),
        P("heads", None),
        P(None, "heads"),
        P("heads", None),
        P(),
        P(),
        P(),
        P(),
        P(None, None, "heads"),
        P("heads", None),
        P(None, "heads"),
        P("heads", None),
        P(),
        P(),
        P(),
        P(),
        P(None, None, "heads"),
        P("heads", None),
        P(None, "heads"),
        P("heads", None),
        P(),
        P(),
        P(),
        P(),
    )
    return jax.shard_map(shards, mesh=mesh, in_specs=in_specs, out_specs=out_specs, check_vma=False)
```

```python
import functools

import jax
import jax.numpy as jnp
from jax import lax
from jax.experimental import pallas as pl
from jax.experimental.pallas import tpu as pltpu
from jax.sharding import PartitionSpec as P

HD = 64
BINS = 64
STEP = 10


NORM_EPS = 1e-05
ADAM_EPS = 1e-08
RATE = 0.05
RATE_WIDE = 1.0
BETA_ONE = 0.9
BETA_TWO = 0.95
DECAY = 0.1
CLIP_NORM = 0.02
MASKED = -1e30
FLOAT = jnp.float32
HALF = jnp.bfloat16
MESH = pl.DeviceIdType.MESH


def adam_update(weight, moment_one, moment_two, gradient, factor, rate, decay_rate):
    moment_one = BETA_ONE * moment_one + gradient * (factor * (1.0 - BETA_ONE))
    rooted = gradient * (factor * (1.0 - BETA_TWO) ** 0.5)
    moment_two = BETA_TWO * moment_two + rooted * rooted
    root = moment_two * lax.rsqrt(moment_two) * (1.0 - BETA_TWO**STEP) ** -0.5 + ADAM_EPS
    inverse = pl.reciprocal(root, approx=True)
    inverse = inverse * (2.0 - root * inverse)
    step = moment_one * inverse * (rate / (1.0 - BETA_ONE**STEP))
    weight = weight * (1.0 - rate * decay_rate) - step
    return (weight, moment_one, moment_two)


def place_bit(place, bit):
    return lax.rem(lax.div(place, bit), 2)


def flip(place, bit):
    return place + bit - 2 * bit * place_bit(place, bit)


def bits_of(size):
    return [1 << power for power in range(size.bit_length() - 1)]


def partner(places, axis, bit):
    other = dict(places)
    other[axis] = flip(places[axis], bit)
    return (other["tables"], other["heads"])


def greet(places, axes):
    barrier = pltpu.get_barrier_semaphore()
    across = (flip(flip(places["tables"], 2), 4), places["heads"])
    others = [partner(places, axis, bit) for axis, bit in axes] + [across]
    for other in others:
        pl.semaphore_signal(barrier, inc=1, device_id=other, device_id_type=MESH)
    pl.semaphore_wait(barrier, len(others))


class Copies:
    def __init__(self, sends, recvs):
        self.sends, self.recvs, self.used = sends, recvs, 0

    def make(self, source, target, device):
        self.used += 1
        return pltpu.make_async_remote_copy(
            src_ref=source,
            dst_ref=target,
            send_sem=self.sends.at[self.used - 1],
            recv_sem=self.recvs.at[self.used - 1],
            device_id=device,
            device_id_type=MESH,
        )

    def start(self, source, target, device):
        copy = self.make(source, target, device)
        copy.start()
        return copy


class Landing:
    def __init__(self, rows_ref):
        self.rows_ref, self.used = rows_ref, 0

    def take(self, rows):
        self.used += rows
        return self.rows_ref.at[pl.ds(self.used - rows, rows), :]


class Traffic:
    LATENCY = 4.0

    def __init__(self):
        self.now, self.free, self.flows = 0.0, {}, []

    def book(self, axis, bit, size):
        link, hops = ("core", 0.15) if (axis, bit) == ("heads", 1) else (axis + str(min(bit, 2)), 1)
        if axis == "tables" and bit > 2:
            hops = bit // 2
        self.free[link] = max(self.now, self.free.get(link, 0.0)) + hops * size * 2 / 1e5
        return self.free[link] + self.LATENCY * min(hops + 0.4, 1)

    def book_link(self, link, size):
        self.free[link] = max(self.now, self.free.get(link, 0.0)) + size * 2 / 1e5
        return self.free[link] + self.LATENCY

    def add(self, flow):
        self.flows.append(flow)
        flow.start()

    def waiting(self):
        return [flow for flow in self.flows if flow.sent]

    def step(self):
        flow = min(self.waiting(), key=lambda flow: flow.ready)
        self.now = max(self.now, flow.ready) + 0.3
        flow.advance()

    def spend(self, time):
        self.now += time
        while any(flow.ready <= self.now for flow in self.waiting()):
            self.step()

    def wait(self, *flows):
        while not all(flow.done() for flow in flows):
            self.step()


def stages_of(rows, axes, least):
    steps = []
    for axis, bit in axes:
        if rows // 2 >= least and rows % 32 == 0:
            rows //= 2
            steps.append((axis, bit, "halve", rows))
        else:
            steps.append((axis, bit, "whole", rows))
    back = [(axis, bit, "back", left) for axis, bit, kind, left in reversed(steps) if kind == "halve"]
    return steps + back


def landing_rows(steps):
    return sum(left for _, _, kind, left in steps if kind != "back")


class Sum:
    def __init__(self, copies, traffic, landing, buffer, result, start, steps, places, until=None):
        self.copies, self.traffic, self.landing = copies, traffic, landing
        self.buffer, self.result, self.low = buffer, result, start
        self.steps, self.places = steps, places
        self.until = len(steps) if until is None else until
        self.at, self.sent, self.landed, self.ready = 0, None, None, 0.0
        self.last, self.found = None, None

    def rows(self, low, count):
        if isinstance(low, int):
            return pl.ds(low, count)
        return pl.ds(pl.multiple_of(low, 16), count)

    def finish(self):
        if self.sent is None:
            return
        _, _, kind, count = self.steps[self.at - 1]
        self.sent.wait()
        self.sent = None
        if kind != "back":
            mine = self.rows(self.low, count)
            total = self.buffer[mine, :].astype(FLOAT) + self.landed[...].astype(FLOAT)
            last = self.at == len(self.steps) or self.steps[self.at][2] == "back"
            target = self.result if last else self.buffer
            target[mine, :] = total.astype(self.buffer.dtype)

    def start(self):
        if self.at >= self.until:
            return
        axis, bit, kind, count = self.steps[self.at]
        self.at += 1
        side = place_bit(self.places[axis], bit)
        if kind == "halve":
            source = self.buffer.at[self.rows(self.low + count * (1 - side), count), :]
            self.low = self.low + count * side
            target = self.landed = self.landing.take(count)
        elif kind == "whole":
            source = self.buffer.at[self.rows(self.low, count), :]
            target = self.landed = self.landing.take(count)
        else:
            source = target = self.result.at[self.rows(self.low, count), :]
            self.low = self.low - count * side
        self.sent = self.copies.start(source, target, partner(self.places, axis, bit))
        self.ready = self.traffic.book(axis, bit, count * self.buffer.shape[-1] * 2)

    def advance(self):
        self.finish()
        self.start()
        if self.last and self.done():
            self.found = self.last()

    def go_on(self):
        self.until = len(self.steps)
        self.start()

    def done(self):
        return self.at >= self.until and self.sent is None


def chain_steps(rows, sizes):
    half = rows // 2
    others, left = [], half
    for bit in bits_of(sizes["tables"])[3:]:
        if left % 32 == 0:
            left //= 2
            others.append(("pair", bit, "halve", left, "inner"))
        else:
            others.append(("pair", bit, "whole", left, "inner"))
    others = others + [
        (move, bit, "back", count, who)
        for move, bit, kind, count, who in reversed(others)
        if kind == "halve"
    ]
    return [
        ("pair", 1, "halve", half, "all"),
        ("in", 2, "in", half, "row"),
        ("swap", 4, "whole", half, "inner"),
        *others,
        ("out", 2, "out", half, "row"),
        ("pair", 1, "back", half, "all"),
    ]


def chain_landing(steps):
    return sum(
        count for move, bit, kind, count, who in steps[1:] if kind in ("halve", "whole", "in")
    )


class Chain:
    def __init__(self, copies, traffic, landing, buffer, result, start, steps, places):
        self.copies, self.traffic, self.landing = copies, traffic, landing
        self.buffer, self.result, self.low = buffer, result, start
        self.steps, self.places = steps, places
        self.at, self.sent, self.landed, self.ready = 0, None, None, 0.0
        self.last, self.found = None, None
        low, high = (place_bit(places["tables"], bit) for bit in (2, 4))
        self.inner = low + high == 1
        self.outer = low + high != 1

    def rows(self, low, count):
        if isinstance(low, int):
            return pl.ds(low, count)
        return pl.ds(pl.multiple_of(low, 16), count)

    def add(self, count):
        mine = self.rows(self.low, count)
        total = self.buffer[mine, :].astype(FLOAT) + self.landed[...].astype(FLOAT)
        last = not any(step[2] in ("halve", "whole", "in") for step in self.steps[self.at :])
        target = self.result if last else self.buffer
        target[mine, :] = total.astype(self.buffer.dtype)

    def finish(self):
        if self.sent is None:
            return
        move, _, kind, count, who = self.steps[self.at - 1]
        sent, self.sent = self.sent, None
        if who == "row":
            senders, getters = (
                (self.outer, self.inner) if move == "in" else (self.inner, self.outer)
            )

            @pl.when(senders)
            def _():
                sent.wait_send()

            @pl.when(getters)
            def _():
                sent.wait_recv()
                if move == "in":
                    self.add(count)

        elif who == "inner":

            @pl.when(self.inner)
            def _():
                sent.wait()
                if kind != "back":
                    self.add(count)

        else:
            sent.wait()
            if kind != "back":
                self.add(count)

    def start(self):
        if self.at >= len(self.steps):
            return
        move, bit, kind, count, who = self.steps[self.at]
        first = self.at == 0
        self.at += 1
        place = self.places["tables"]
        side = place_bit(place, bit)
        other = flip(flip(place, 2), 4) if move == "swap" else flip(place, bit)
        if kind == "halve":
            given = self.rows(self.low + count * (1 - side), count)
            self.low = self.low + count * side
        else:
            given = self.rows(self.low, count)
        if kind in ("back", "out"):
            source = target = self.result.at[given, :]
        elif first:
            source, target = self.buffer.at[given, :], self.result.at[given, :]
            self.landed = self.result.at[self.rows(self.low, count), :]
        else:
            source = self.buffer.at[given, :]
            target = self.landed = self.landing.take(count)
        if kind == "back":
            self.low = self.low - count * side
        copy = self.copies.make(source, target, (other, self.places["heads"]))
        if who == "all":
            copy.start()
        else:
            senders = self.outer if move == "in" else self.inner

            @pl.when(senders)
            def _():
                copy.start()

        self.sent = copy
        link = move if move != "pair" else "tables" + str(min(bit, 2))
        self.ready = self.traffic.book_link(link, count * self.buffer.shape[-1] * 2)

    def advance(self):
        self.finish()
        self.start()
        if self.last and self.done():
            self.found = self.last()

    def done(self):
        return self.at >= len(self.steps) and self.sent is None


class Gather:
    def __init__(self, copies, traffic, views, size, places, bits):
        self.copies, self.traffic, self.views, self.size = copies, traffic, views, size
        self.places, self.bits = places, bits
        self.at, self.held, self.sent, self.ready = 0, [places["heads"]], [], 0.0

    def advance(self):
        self.finish()
        self.start()

    def finish(self):
        for copy in self.sent:
            copy.wait()
        if self.sent:
            self.held = self.held + [flip(slot, self.bits[self.at - 1]) for slot in self.held]
        self.sent = []

    def start(self):
        if self.at < len(self.bits):
            bit = self.bits[self.at]
            other = partner(self.places, "heads", bit)
            self.sent = [
                self.copies.start(view(slot), view(slot), other)
                for slot in self.held
                for view in self.views
            ]
            self.ready = self.traffic.book("heads", bit, self.size * len(self.held))
            self.at += 1

    def done(self):
        return self.at >= len(self.bits) and not self.sent


def places_here():
    return {"tables": lax.axis_index("tables"), "heads": lax.axis_index("heads")}


SMALL = {"head": (0, 64), "bins": (64, 64), "embed": (128, 112), "gains": (240, 16)}
SMALL_ROWS = 256
CHUNK = 256
SPAN = 2


def dot(left, right, over=(1, 0)):
    return lax.dot_general(
        left, right, (((over[0],), (over[1],)), ((), ())), preferred_element_type=FLOAT
    )


def standard(rows):
    center = rows - jnp.mean(rows, axis=-1, keepdims=True)
    scale = lax.rsqrt(jnp.mean(center * center, axis=-1, keepdims=True) + NORM_EPS)
    return center * scale, scale


def standard_back(upstream, gain_row, unit, scale):
    inner = upstream * gain_row
    lean = jnp.mean(inner, axis=-1, keepdims=True)
    tilt = jnp.mean(inner * unit, axis=-1, keepdims=True)
    return (inner - lean - unit * tilt) * scale


def as_row(column):
    return jnp.broadcast_to(column, (column.shape[0], 128)).T[:1]


def as_column(row):
    return jnp.broadcast_to(row, (8, row.shape[1])).T[:, :1]


def column_sums(rows):
    return jnp.sum(rows, axis=0, keepdims=True)


def gelu_both(hidden):
    root = 0.7978845608028654
    square = hidden * hidden
    bent = jnp.tanh(root * hidden * (1.0 + 0.044715 * square))
    half = 0.5 * (1.0 + bent)
    slope = half + 0.5 * hidden * (1.0 - bent * bent) * root * (1.0 + 0.134145 * square)
    return hidden * half, slope


def sum_squares(rows_ref, low, count):
    def piece(step, total):
        part = rows_ref[pl.ds(pl.multiple_of(low + step * 64, 64), 64), :].astype(FLOAT)
        return total + jnp.sum((part * part).reshape(8, 8, part.shape[1]), axis=0)

    return lax.fori_loop(0, count // 64, piece, jnp.zeros((8, rows_ref.shape[1]), FLOAT))


def one_value(total):
    return jnp.sum(jnp.sum(total, axis=0, keepdims=True), axis=1, keepdims=True)


class Named:
    pass


def train_kernel(shape, r):
    groups, ctx, qry, width, inner, hidden = (
        shape.groups,
        shape.ctx,
        shape.qry,
        shape.width,
        shape.inner,
        shape.hidden,
    )
    heads = inner // HD
    total_ctx, total_qry = groups * ctx, groups * qry
    block = SPAN * qry
    blocks = total_qry // block
    half = width // 2
    places = places_here()
    me = places["heads"]
    copies = Copies(r.sends, r.recvs)
    traffic = Traffic()
    over_heads, over_tables = shape.over_heads, shape.over_tables
    far_first = [bit for _, bit in reversed(over_heads)]
    tiny = Landing(r.tiny_land)
    wide = Landing(r.wide_land)
    narrow = Landing(r.narrow_land)
    def stage(number, source, target):
        copy = pltpu.make_async_copy(source, target, r.locals.at[number])
        copy.start()
        return copy

    low = 3 * inner
    loads = [
        stage(part, r.w_qkv_wide.at[part], r.back.at[pl.ds(part * inner, inner), :])
        for part in range(3)
    ]
    loads.append(stage(3, r.w_out_wide, r.small.at[pl.ds(0, inner), :]))

    def load_halves(number, source):
        rest = source.shape[0] - low
        return [
            stage(number, source.at[pl.ds(0, low), :], r.back.at[pl.ds(0, low), :]),
            stage(number + 1, source.at[pl.ds(low, rest), :], r.small.at[pl.ds(0, rest), :]),
        ]

    def take_halves(copies_in, target):
        rest = target.shape[0] - low
        for copy in copies_in:
            copy.wait()
        target[pl.ds(0, low), :] = r.back[pl.ds(0, low), :].astype(HALF)
        target[pl.ds(low, rest), :] = r.small[pl.ds(0, rest), :].astype(HALF)

    greet(places, over_heads + over_tables)

    r.feat[me, pl.ds(0, ctx), :] = r.ctx_feat[...].astype(FLOAT).T.astype(HALF)
    r.feat[me, pl.ds(ctx, qry), :] = r.qry_feat[...]
    r.ints[me] = jnp.zeros((8, ctx), jnp.int32)
    r.ints[me, 0:1, :] = r.ctx_bins[...]
    r.ints[me, 1:2, pl.ds(0, qry)] = r.qry_bins[...]
    r.ints[me, 2:3, pl.ds(0, qry)] = r.query_mask[...]
    rows_in = Gather(
        copies,
        traffic,
        [lambda slot: r.feat.at[slot], lambda slot: r.ints.at[slot]],
        (ctx + qry) * 256 + ctx * 32,
        places,
        far_first,
    )
    traffic.add(rows_in)
    mask_sum = jnp.sum(r.query_mask[...].astype(FLOAT), axis=1, keepdims=True)
    r.count_work[...] = jnp.broadcast_to(mask_sum, (16, 128))
    tiny_steps = stages_of(16, over_heads + over_tables, 16)
    counted = Sum(copies, traffic, tiny, r.count_work, r.count, 0, tiny_steps, places)
    traffic.add(counted)
    for copy in loads:
        copy.wait()
    for part in range(3):
        r.w_qkv[part] = r.back[pl.ds(part * inner, inner), :].astype(HALF)
    r.out_all[me] = r.small[pl.ds(0, inner), :].astype(HALF)
    loads = load_halves(4, r.w_up_wide)
    outs_in = Gather(
        copies, traffic, [lambda slot: r.out_all.at[slot]], inner * width * 2, places, far_first
    )

    embed_half = r.w_embed[...].astype(HALF)
    bins_half = r.w_bins[...].astype(HALF)
    gain_one, gain_two, gain_last = (r.gains[row : row + 1, :] for row in range(3))
    bin_rows = lax.broadcasted_iota(jnp.int32, (BINS, 256), 0)

    def one_hot(slot, place):
        return jnp.where(
            bin_rows == r.ints[slot, 0:1, pl.ds(pl.multiple_of(place * 256, 256), 256)], 1.0, 0.0
        ).astype(HALF)

    def embed_shard(slot):
        def context(place, _):
            at = pl.multiple_of(slot * ctx + place * 256, 256)
            feat = r.feat[slot, pl.ds(pl.multiple_of(place * 256, 256), 256), :]
            zero = dot(feat, embed_half) + dot(one_hot(slot, place), bins_half, (0, 0))
            unit, scale = standard(zero)
            normed = (unit * gain_one).astype(HALF)
            r.normed_ctx[pl.ds(at, 256), :] = normed
            r.scale_ctx[pl.ds(slot * (ctx // 256) + place, 1), :] = as_row(scale)
            keys = dot(normed, r.w_qkv[1], (1, 1))
            values = dot(normed, r.w_qkv[2], (1, 1))
            r.keys[pl.ds(at, 256), :] = keys.astype(HALF)
            r.values[pl.ds(at, 256), :] = values.astype(HALF)
            r.keys_t[:, pl.ds(at, 256)] = keys.T.astype(HALF)
            r.values_t[:, pl.ds(at, 256)] = values.T.astype(HALF)
            return 0

        lax.fori_loop(0, ctx // 256, context, 0)
        at = pl.multiple_of(slot * qry, 16)
        zero = dot(r.feat[slot, pl.ds(ctx, qry), :], embed_half)
        r.stream[pl.ds(at, qry), :] = zero
        unit, scale = standard(zero)
        normed = (unit * gain_one).astype(HALF)
        r.normed_qry[pl.ds(at, qry), :] = normed
        r.scale_qry[pl.ds(slot, 1), :] = as_row(scale)
        queries = dot(normed, r.w_qkv[0], (1, 1))
        r.queries[pl.ds(at, qry), :] = queries.astype(HALF)
        r.queries_t[slot] = queries.T.astype(HALF)

    done = 0
    while done < groups:
        for slot in rows_in.held[done:]:
            embed_shard(slot)
            done += 1
            traffic.spend(2.0)
            if done == 1:
                traffic.add(outs_in)
                take_halves(loads, r.w_up)
                loads = load_halves(6, r.w_down_wide)
            if done == 2:
                take_halves(loads, r.w_down)
        if done == len(rows_in.held) and done < groups:
            traffic.step()

    lane = lax.broadcasted_iota(jnp.int32, (1, inner), 1)
    head_rows = [
        jnp.where((lane >= h * HD) & (lane < (h + 1) * HD), 1.0, 0.0).astype(FLOAT)
        for h in range(heads)
    ]
    slots_at = lax.broadcasted_iota(jnp.int32, (1, total_ctx), 1)
    dead = jnp.where(slots_at < r.counts[0:1, 0:1], 0.0, MASKED)
    mixing = []
    for b in range(groups):
        rows = pl.ds(b * qry, qry)
        query_blk = r.queries[rows, :]
        mixed = jnp.zeros((qry, inner), FLOAT)
        for h in range(heads):
            raw = dot(query_blk * (head_rows[h] * HD**-0.5).astype(HALF), r.keys_t[...]) + dead
            raised = jnp.exp(raw - jnp.max(raw, axis=-1, keepdims=True))
            weights = (raised * (1.0 / jnp.sum(raised, axis=-1, keepdims=True))).astype(HALF)
            r.weights[h, rows, :] = weights
            mixed = mixed + dot(weights, r.values[...]) * head_rows[h]
        r.mixed[rows, :] = mixed
        r.mix_all[me, b] = mixed.astype(HALF)
        mixing.append(
            Gather(
                copies,
                traffic,
                [lambda slot, b=b: r.mix_all.at[slot, b]],
                qry * 512,
                places,
                far_first,
            )
        )
        traffic.add(mixing[-1])
        traffic.spend(2.0)

    sum_steps = stages_of(2 * block, over_heads, block)
    down_sums, back_sums = [], []
    for b in range(blocks):
        traffic.wait(outs_in, *mixing[SPAN * b : SPAN * (b + 1)])
        rows = pl.ds(b * block, block)
        attended = []
        for part in range(SPAN * b, SPAN * (b + 1)):
            total = dot(r.mix_all[0, part], r.out_all[0])
            for slot in range(1, groups):
                total = total + dot(r.mix_all[slot, part], r.out_all[slot])
            attended.append(total)
        stream = r.stream[rows, :] + jnp.concatenate(attended, axis=0)
        r.stream[rows, :] = stream
        unit, _ = standard(stream)
        normed = (unit * gain_two).astype(HALF)
        r.normed_two[rows, :] = normed
        active, slope = gelu_both(dot(normed, r.w_up[...]))
        active = active.astype(HALF)
        r.active[rows, :] = active
        r.slope[rows, :] = slope.astype(HALF)
        low = pl.ds(2 * b * block, block)
        high = pl.ds((2 * b + 1) * block, block)
        part = dot(active, r.w_down[...]).astype(HALF)
        r.down_work[low, :] = part[:, :half]
        r.down_work[high, :] = part[:, half:]
        down_sums.append(
            Sum(copies, traffic, narrow, r.down_work, r.down_sum, 2 * b * block, sum_steps, places)
        )
        traffic.add(down_sums[-1])
        traffic.spend(2.0)

    mains = []

    def send_chunk(place):
        start = CHUNK * place
        part = Chain(
            copies, traffic, wide, r.main_work, r.main, start, shape.main_steps, places
        )
        part.last = functools.partial(sum_squares, r.main, start, CHUNK)
        mains.append(part)
        traffic.add(part)
        traffic.spend(0.5)

    head_half = r.w_head[...].astype(HALF)
    traffic.wait(counted)
    divisor = jnp.maximum(r.count[0:1, 0:1], 1.0)
    tall = lax.broadcasted_iota(jnp.int32, (BINS, 256), 0)
    loss = jnp.zeros((1, 1), FLOAT)
    grad_head = jnp.zeros((BINS, width), FLOAT)
    gain_sum_last = jnp.zeros((1, width), FLOAT)
    for b in range(blocks):
        traffic.wait(counted, down_sums[b])
        rows = pl.ds(b * block, block)
        low = pl.ds(2 * b * block, block)
        high = pl.ds((2 * b + 1) * block, block)
        mlp = jnp.concatenate([r.down_sum[low, :], r.down_sum[high, :]], axis=1)
        unit, scale = standard(r.stream[rows, :] + mlp.astype(FLOAT))
        normed = (unit * gain_last).astype(HALF)
        logits = dot(normed, head_half, (1, 1))
        targets, masks = [], []
        for slot in range(SPAN * b, SPAN * (b + 1)):
            target = jnp.where(tall == r.ints[slot, 1:2, 0:256], 1.0, 0.0)
            targets.append(target.T[:qry])
            mask = jnp.broadcast_to(r.ints[slot, 2:3, 0:256].astype(FLOAT), (8, 256))
            masks.append(mask.T[:qry, :1])
        target = jnp.concatenate(targets, axis=0)
        mask = jnp.concatenate(masks, axis=0)
        top = jnp.max(logits, axis=-1, keepdims=True)
        log_bins = top + jnp.log(jnp.sum(jnp.exp(logits - top), axis=-1, keepdims=True))
        missed = log_bins - jnp.sum(target * logits, axis=-1, keepdims=True)
        loss = loss + jnp.sum(mask * missed, axis=0, keepdims=True)
        back_logits = (mask * (jnp.exp(logits - log_bins) - target) / divisor).astype(HALF)
        grad_head = grad_head + dot(back_logits, normed, (0, 0))
        back_final = dot(back_logits, head_half)
        gain_sum_last = gain_sum_last + column_sums(back_final * unit)
        back_two = standard_back(back_final, gain_last, unit, scale)
        r.back[rows, :] = back_two
        back_mlp = back_two.astype(HALF)
        r.back_mlp[rows, :] = back_mlp
        back_active = dot(back_mlp, r.w_down[...], (1, 1))
        back_up = (r.slope[rows, :].astype(FLOAT) * back_active).astype(HALF)
        r.back_up[rows, :] = back_up
        part = dot(back_up, r.w_up[...], (1, 1)).astype(HALF)
        r.down_work[low, :] = part[:, :half]
        r.down_work[high, :] = part[:, half:]
        back_sums.append(
            Sum(copies, traffic, narrow, r.down_work, r.down_sum, 2 * b * block, sum_steps, places)
        )
        traffic.add(back_sums[-1])
        traffic.spend(3.0)
    r.loss_work[...] = jnp.broadcast_to(loss / groups, (16, 128))
    losses = Sum(copies, traffic, tiny, r.loss_work, r.loss, 0, tiny_steps, places)
    r.small[pl.ds(0, BINS), :] = grad_head / groups

    for place in range(hidden // CHUNK):
        at = pl.ds(place * CHUNK, CHUNK)
        r.main_work[at, :] = dot(r.active[:, at], r.back_mlp[...], (0, 0)).astype(HALF)
        send_chunk(len(mains))
    for place in range(width // CHUNK):
        at = pl.ds(place * CHUNK, CHUNK)
        to = pl.ds(hidden + place * CHUNK, CHUNK)
        r.main_work[to, :] = dot(r.normed_two[:, at], r.back_up[...], (0, 0)).astype(HALF)
        send_chunk(len(mains))

    gain_sum_two = jnp.zeros((1, width), FLOAT)
    r.keys_back[...] = jnp.zeros(r.keys_back.shape, FLOAT)
    r.values_back[...] = jnp.zeros(r.values_back.shape, FLOAT)
    for b in range(blocks):
        traffic.wait(back_sums[b])
        rows = pl.ds(b * block, block)
        low = pl.ds(2 * b * block, block)
        high = pl.ds((2 * b + 1) * block, block)
        upstream = jnp.concatenate([r.down_sum[low, :], r.down_sum[high, :]], axis=1).astype(FLOAT)
        unit, scale = standard(r.stream[rows, :])
        gain_sum_two = gain_sum_two + column_sums(upstream * unit)
        back_one = r.back[rows, :] + standard_back(upstream, gain_two, unit, scale)
        r.back[rows, :] = back_one
        back_attn = back_one.astype(HALF)
        r.slope[rows, :] = back_attn
        back_mix = dot(back_attn, r.out_all[me], (1, 1)).astype(HALF)
        r.back_mix[rows, :] = back_mix
        turned = back_mix.astype(FLOAT)
        for part in range(SPAN):
            r.back_mix_t[SPAN * b + part] = turned[part * qry : (part + 1) * qry].T.astype(HALF)
        traffic.spend(1.5)
        for h in range(heads):

            def backward(part, _, h=h):
                here = SPAN * b + part
                at = pl.ds(pl.multiple_of(here * qry, 16), qry)
                back_mix = r.back_mix[at, :]
                mine = back_mix * head_rows[h].astype(HALF)
                lean = jnp.sum(
                    mine.astype(FLOAT) * r.mixed[at, :], axis=-1, keepdims=True
                )
                weights = r.weights[h, at, :]
                back_weights = dot(mine, r.values_t[...])
                back_scores = (weights.astype(FLOAT) * (back_weights - lean)).astype(HALF)
                queries_back = dot(back_scores, r.keys[...]) * (head_rows[h] * HD**-0.5)
                if h == 0:
                    r.queries_back[at, :] = queries_back
                else:
                    r.queries_back[at, :] += queries_back
                lanes = pl.ds(h * HD, HD)
                r.values_back[lanes, :] += dot(r.back_mix_t[here, lanes, :], weights)
                r.keys_back[lanes, :] += dot(r.queries_t[here, lanes, :], back_scores)
                return 0

            lax.fori_loop(0, SPAN, backward, 0)
            traffic.spend(1.7)

    first = hidden + width
    pieces = [
        lambda: dot(r.mix_all[me].reshape(total_qry, inner), r.slope[...], (0, 0)),
        lambda: dot(r.queries_back[...].astype(HALF), r.normed_qry[...], (0, 0)),
        lambda: dot((r.keys_back[...] * HD**-0.5).astype(HALF), r.normed_ctx[...]),
        lambda: dot(r.values_back[...].astype(HALF), r.normed_ctx[...]),
    ]
    for place, piece in enumerate(pieces):
        r.main_work[pl.ds(first + place * inner, inner), :] = piece().astype(HALF)
        while (len(mains) + 1) * CHUNK <= first + (place + 1) * inner:
            send_chunk(len(mains))
        traffic.spend(0.7)

    over_gain = 1.0 / gain_one
    low_bins, low_embed, low_gains = (SMALL[name][0] for name in ("bins", "embed", "gains"))
    features = r.w_embed.shape[0]
    r.small[pl.ds(BINS, SMALL_ROWS - BINS), :] = jnp.zeros((SMALL_ROWS - BINS, width), FLOAT)
    bins_at = pl.ds(low_bins, BINS)
    embed_at = pl.ds(low_embed, features)

    def embed_back(upstream, normed, scale):
        unit = normed.astype(FLOAT) * over_gain
        return column_sums(upstream * unit), standard_back(upstream, gain_one, unit, scale)

    def context_back(place, gain_sum):
        slot, offset = lax.div(place, ctx // 256), lax.rem(place, ctx // 256)
        at = pl.ds(pl.multiple_of(place * 256, 256), 256)
        keys = (r.keys_back[:, at] * HD**-0.5).T.astype(HALF)
        values = r.values_back[:, at].T.astype(HALF)
        upstream = dot(keys, r.w_qkv[1]) + dot(values, r.w_qkv[2])
        gains, back_zero = embed_back(upstream, r.normed_ctx[at, :], as_column(r.scale_ctx[pl.ds(place, 1), :]))
        back_zero = back_zero.astype(HALF)
        feat = r.feat[slot, pl.ds(pl.multiple_of(offset * 256, 256), 256), :]
        r.small[embed_at, :] += dot(feat, back_zero, (0, 0))
        r.small[bins_at, :] += dot(one_hot(slot, offset), back_zero)
        return gain_sum + gains

    gain_sum_one = jnp.zeros((1, width), FLOAT)
    pieces = total_ctx // 256
    for part in range(2):
        gain_sum_one = lax.fori_loop(
            part * pieces // 2, (part + 1) * pieces // 2, context_back, gain_sum_one
        )
        traffic.spend(2.0)

    def query_back(slot, gain_sum):
        at = pl.ds(pl.multiple_of(slot * qry, 16), qry)
        upstream = dot(r.queries_back[at, :].astype(HALF), r.w_qkv[0])
        gains, back_zero = embed_back(upstream, r.normed_qry[at, :], as_column(r.scale_qry[pl.ds(slot, 1), :]))
        mine = jnp.where(slot == me, 1.0, 0.0)
        back_zero = (back_zero + mine * r.back[at, :]).astype(HALF)
        feat = r.feat[slot, pl.ds(ctx, qry), :]
        r.small[embed_at, :] += dot(feat, back_zero, (0, 0))
        return gain_sum + gains

    gain_sum_one = lax.fori_loop(0, groups, query_back, gain_sum_one)
    r.small[pl.ds(low_gains, 1), :] = gain_sum_one
    r.small[pl.ds(low_gains + 1, 1), :] = gain_sum_two / groups
    r.small[pl.ds(low_gains + 2, 1), :] = gain_sum_last / groups
    r.small_work[...] = r.small[...].astype(HALF)

    small_steps = stages_of(SMALL_ROWS, over_heads + over_tables, 64)
    pause = len(small_steps) - len(over_heads)
    smalls = Sum(
        copies, traffic, wide, r.small_work, r.small_out, 0, small_steps, places, until=pause
    )
    traffic.add(smalls)
    traffic.add(losses)
    traffic.wait(smalls, losses, *mains)
    squares = one_value(sum(part.found for part in mains))
    r.square_work[...] = jnp.broadcast_to(squares, (16, 128))
    square_steps = stages_of(16, list(reversed(over_heads)), 16)
    squared = Sum(copies, traffic, tiny, r.square_work, r.square, 0, square_steps, places)
    smalls.go_on()
    traffic.add(squared)
    traffic.wait(squared, smalls)
    squares = r.square[0:8, :] + one_value(sum_squares(r.small_out, 0, SMALL_ROWS))
    row = lax.broadcasted_iota(jnp.int32, (8, 128), 0)
    r.stats[...] = jnp.where(row == 0, squares, jnp.where(row == 1, r.loss[0:8, :], r.count[0:8, :]))


def train(sizes, inputs):
    shape = Named()
    shape.groups = sizes["heads"]
    features, shape.ctx = inputs["ctx_feat"].shape
    shape.qry = inputs["qry_feat"].shape[0]
    shape.width = inputs["w_embed"].shape[1]
    shape.inner = inputs["w_out_wide"].shape[0]
    shape.hidden = inputs["w_up_wide"].shape[1]
    shape.over_tables = [("tables", bit) for bit in bits_of(sizes["tables"])]
    shape.over_heads = [("heads", bit) for bit in bits_of(sizes["heads"])]
    groups, ctx, qry, width, inner, hidden = (
        shape.groups,
        shape.ctx,
        shape.qry,
        shape.width,
        shape.inner,
        shape.hidden,
    )
    total_ctx, total_qry = groups * ctx, groups * qry
    heads = inner // HD
    main_rows = hidden + width + 4 * inner
    block = SPAN * qry
    shape.main_steps = chain_steps(CHUNK, sizes)
    small_steps = stages_of(SMALL_ROWS, shape.over_heads + shape.over_tables, 64)
    sum_steps = stages_of(2 * block, shape.over_heads, block)
    wide_rows = main_rows // CHUNK * chain_landing(shape.main_steps) + landing_rows(small_steps)
    narrow_rows = 2 * (total_qry // block) * landing_rows(sum_steps)
    every = len(shape.over_tables) + len(shape.over_heads)
    tiny_rows = 16 * (2 * every + len(shape.over_heads))
    tiny = ((16, 128), FLOAT)
    scratch = dict(
        w_qkv=((3, inner, width), HALF),
        w_up=((width, hidden), HALF),
        w_down=((hidden, width), HALF),
        feat=((groups, ctx + qry, features), HALF),
        ints=((groups, 8, ctx), jnp.int32),
        out_all=((groups, inner, width), HALF),
        count_work=tiny,
        count=tiny,
        loss_work=tiny,
        loss=tiny,
        square_work=tiny,
        square=tiny,
        normed_ctx=((total_ctx, width), HALF),
        scale_ctx=((total_ctx // 256, 256), FLOAT),
        normed_qry=((total_qry, width), HALF),
        scale_qry=((groups, qry), FLOAT),
        stream=((total_qry, width), FLOAT),
        queries=((total_qry, inner), HALF),
        queries_t=((groups, inner, qry), HALF),
        keys=((total_ctx, inner), HALF),
        values=((total_ctx, inner), HALF),
        keys_t=((inner, total_ctx), HALF),
        values_t=((inner, total_ctx), HALF),
        weights=((heads, total_qry, total_ctx), HALF),
        mixed=((total_qry, inner), FLOAT),
        mix_all=((groups, groups, qry, inner), HALF),
        normed_two=((total_qry, width), HALF),
        active=((total_qry, hidden), HALF),
        slope=((total_qry, hidden), HALF),
        down_work=((2 * total_qry, width // 2), HALF),
        down_sum=((2 * total_qry, width // 2), HALF),
        back=((total_qry, width), FLOAT),
        back_mlp=((total_qry, width), HALF),
        back_up=((total_qry, hidden), HALF),
        back_mix=((total_qry, inner), HALF),
        back_mix_t=((groups, inner, qry), HALF),
        queries_back=((total_qry, inner), FLOAT),
        keys_back=((inner, total_ctx), FLOAT),
        values_back=((inner, total_ctx), FLOAT),
        main_work=((main_rows, width), HALF),
        small=((SMALL_ROWS, width), FLOAT),
        small_work=((SMALL_ROWS, width), HALF),
        wide_land=((wide_rows, width), HALF),
        narrow_land=((narrow_rows, width // 2), HALF),
        tiny_land=((tiny_rows, 128), FLOAT),
    )
    outputs = dict(
        main=jax.ShapeDtypeStruct((main_rows, width), HALF),
        small_out=jax.ShapeDtypeStruct((SMALL_ROWS, width), HALF),
        stats=jax.ShapeDtypeStruct((8, 128), FLOAT),
    )
    names = list(inputs) + list(outputs) + list(scratch) + ["sends", "recvs", "locals"]

    def kernel(*refs):
        named = Named()
        named.__dict__.update(zip(names, refs))
        train_kernel(shape, named)

    whole = pl.BlockSpec(memory_space=pltpu.VMEM)
    semaphores = pltpu.SemaphoreType.DMA((192,))
    return pl.pallas_call(
        kernel,
        out_shape=tuple(outputs.values()),
        in_specs=[
            pl.BlockSpec(memory_space=pl.ANY) if name.endswith("_wide") else whole
            for name in inputs
        ],
        out_specs=(whole,) * 3,
        scratch_shapes=[pltpu.VMEM(size, kind) for size, kind in scratch.values()]
        + [semaphores, semaphores, pltpu.SemaphoreType.DMA((8,))],
        compiler_params=pltpu.CompilerParams(
            collective_id=1, has_side_effects=True, vmem_limit_bytes=62 * 2**20
        ),
        name="train",
    )(*inputs.values())


def adam_kernel(refs):
    (stats, main_d, main_u, main_o, main_q, main_k, main_v, small) = refs[:8]
    w = refs[8:16]
    m = refs[16:24]
    v = refs[24:32]
    w_new = refs[32:40]
    m_new = refs[40:48]
    v_new = refs[48:56]
    loss, count, norm_out = refs[56:59]
    norm = jnp.sqrt(stats[0:1, 0:1])
    factor = jnp.minimum(1.0, CLIP_NORM / (norm + 1e-06))

    def update(which, gradient, rate, decay, at=...):
        gradient = gradient.astype(FLOAT)
        moments = (m[which][at], v[which][at], gradient, factor)
        results = adam_update(w[which][at], *moments, rate, decay)
        for target, value in zip((w_new, m_new, v_new), results):
            target[which][at] = value

    update(6, main_d[...], RATE, DECAY)
    update(5, main_u[...], RATE, DECAY)
    update(4, main_o[...], RATE_WIDE, DECAY)
    for part, gradient in enumerate((main_q, main_k, main_v)):
        update(3, gradient[...], RATE, DECAY, at=part)

    @pl.when(pl.program_id(0) == 0)
    def _():
        loss[...] = stats[1:2, 0:1]
        count[...] = stats[2:3, 0:1]
        norm_out[...] = norm

        def rows(name, count):
            low, size = SMALL[name]
            return small[low : low + size, :].astype(FLOAT)[:count]

        update(0, rows("embed", w[0].shape[0]), RATE, DECAY)
        update(1, rows("bins", w[1].shape[0]), RATE_WIDE, DECAY)
        update(2, rows("gains", w[2].shape[0]), RATE_WIDE, 0.0)
        update(7, rows("head", w[7].shape[0]), RATE, DECAY)


def adam_all(stats, main, small, weights, firsts, seconds):
    inner, width = weights[4].shape
    hidden = weights[5].shape[1]
    steps = 4

    def fixed(array):
        return pl.BlockSpec(array.shape, lambda step: (0,) * array.ndim)

    def rows_of(rows, low=0):
        size = rows // steps
        return pl.BlockSpec((size, width), lambda step: (low // size + step, 0))

    blocks = [
        fixed(weights[0]),
        fixed(weights[1]),
        fixed(weights[2]),
        pl.BlockSpec((3, inner // steps, width), lambda step: (0, step, 0)),
        rows_of(inner),
        pl.BlockSpec((width // steps, hidden), lambda step: (step, 0)),
        rows_of(hidden),
        fixed(weights[7]),
    ]
    first = hidden + width
    shapes = [jax.ShapeDtypeStruct(weight.shape, FLOAT) for weight in weights]
    return pl.pallas_call(
        lambda *refs: adam_kernel(refs),
        grid=(steps,),
        in_specs=[fixed(stats), rows_of(hidden), rows_of(width, hidden)]
        + [rows_of(inner, first + part * inner) for part in range(4)]
        + [fixed(small)]
        + blocks * 3,
        out_specs=blocks * 3 + [pl.BlockSpec((1, 1), lambda step: (0, 0))] * 3,
        out_shape=shapes * 3 + [jax.ShapeDtypeStruct((1, 1), FLOAT)] * 3,
        compiler_params=pltpu.CompilerParams(vmem_limit_bytes=58 * 2**20),
        name="adam",
    )(stats, *[main] * 6, small, *weights, *firsts, *seconds)


def shards(
    ctx_feat,
    qry_feat,
    counts,
    ctx_bins,
    qry_bins,
    query_mask,
    w_embed,
    w_bins,
    norm_gains,
    w_qkv,
    w_out,
    w_up,
    w_down,
    w_head,
    m_embed,
    m_bins,
    m_gains,
    m_qkv,
    m_out,
    m_up,
    m_down,
    m_head,
    v_embed,
    v_bins,
    v_gains,
    v_qkv,
    v_out,
    v_up,
    v_down,
    v_head,
):
    sizes = {"tables": lax.axis_size("tables"), "heads": lax.axis_size("heads")}
    main, small, stats = train(
        sizes,
        dict(
            counts=counts.reshape(1, 1),
            ctx_feat=ctx_feat[0].T,
            qry_feat=qry_feat[0],
            ctx_bins=ctx_bins,
            qry_bins=qry_bins,
            query_mask=query_mask,
            w_embed=w_embed,
            w_bins=w_bins,
            gains=norm_gains,
            w_qkv_wide=jnp.swapaxes(w_qkv, 1, 2),
            w_out_wide=w_out,
            w_up_wide=w_up,
            w_down_wide=w_down,
            w_head=w_head.T,
        ),
    )
    results = adam_all(
        stats,
        main,
        small,
        *(
            (embed, bins, gains, jnp.swapaxes(qkv, 1, 2), out, up, down, head.T)
            for embed, bins, gains, qkv, out, up, down, head in (
                (w_embed, w_bins, norm_gains, w_qkv, w_out, w_up, w_down, w_head),
                (m_embed, m_bins, m_gains, m_qkv, m_out, m_up, m_down, m_head),
                (v_embed, v_bins, v_gains, v_qkv, v_out, v_up, v_down, v_head),
            )
        ),
    )
    *updated, loss, count, norm = results
    for low in range(0, 24, 8):
        updated[low + 3] = jnp.swapaxes(updated[low + 3], 1, 2)
        updated[low + 7] = updated[low + 7].T
    return (*updated, *(value.reshape(()) for value in (loss, count, norm)))


def solution(mesh):
    in_specs = (
        P("tables", "heads", None),
        P("tables", "heads", None),
        P("tables"),
        P("tables", "heads"),
        P("tables", "heads"),
        P("tables", "heads"),
        P(),
        P(),
        P(),
        P(None, None, "heads"),
        P("heads", None),
        P(None, "heads"),
        P("heads", None),
        P(),
        P(),
        P(),
        P(),
        P(None, None, "heads"),
        P("heads", None),
        P(None, "heads"),
        P("heads", None),
        P(),
        P(),
        P(),
        P(),
        P(None, None, "heads"),
        P("heads", None),
        P(None, "heads"),
        P("heads", None),
        P(),
    )
    out_specs = (
        P(),
        P(),
        P(),
        P(None, None, "heads"),
        P("heads", None),
        P(None, "heads"),
        P("heads", None),
        P(),
        P(),
        P(),
        P(),
        P(None, None, "heads"),
        P("heads", None),
        P(None, "heads"),
        P("heads", None),
        P(),
        P(),
        P(),
        P(),
        P(None, None, "heads"),
        P("heads", None),
        P(None, "heads"),
        P("heads", None),
        P(),
        P(),
        P(),
        P(),
    )
    return jax.shard_map(shards, mesh=mesh, in_specs=in_specs, out_specs=out_specs, check_vma=False)
```
